32 devices in a mesh: comm: 8 (over z, x), sub: 4 (over y, core).
Axes of the slice: x: 2, y: 2, z: 4, core: 2. Of those that a mesh axis runs over, the one named last changes fastest.
Arguments:
- features: float32 [73728, 1024], P(('comm', 'sub')), may hold values from -6 to 6
- q_weight: float32 [1024, 1024], P(('comm', 'sub')), may hold values from -0.1875 to 0.1875
- q_bias: float32 [1024], P(('comm', 'sub')), may hold values from -3 to 3
- w_weight: float32 [2048, 1024], P(('comm', 'sub')), may hold values from -0.125 to 0.125
- w_bias: float32 [1024], P(('comm', 'sub')), may hold values from -3 to 3
- nbr_index: int32 [73728, 50], P(('comm', 'sub')), may hold values from 0 to 2431
- nbr_count: int32 [73728], P(('comm', 'sub')), may hold values from 5 to 50
- importance: float32 [73728, 50], P(('comm', 'sub')), may hold values from 0.1 to 10
- send_rows: int32 [32, 32, 4], P(('comm', 'sub')), may hold values from 0 to 2303
- cotangent: float32 [73728, 1024], P(('comm', 'sub')), may hold values from -6 to 6
Outputs:
- embedding: float32 [73728, 1024], P(('comm', 'sub'))
- grad_features: float32 [73728, 1024], P(('comm', 'sub'))
- grad_q_weight: float32 [1024, 1024], P(('comm', 'sub'))
- grad_q_bias: float32 [1024], P(('comm', 'sub'))
- grad_w_weight: float32 [2048, 1024], P(('comm', 'sub'))
- grad_w_bias: float32 [1024], P(('comm', 'sub'))
The draws below stay inside these ranges and needn't reach their ends.
All inputs are finite; a program needn't handle non-finite values.
Results may differ from the reference program's by a relative error of at most 0.0085.
Values may be sent and summed in bfloat16 or wider, within the bound.
A program may use at most 256 MiB of HBM per device.

```python
import math
import jax
import jax.numpy as jnp
from jax import lax

D = 1024
FANOUT = 50
NODE_DEV = 2304
HALO_PEER = 4
NODES = 73728
N_COMM = 8
N_SUB = 4
DEVICES = 32


def plant(result, key, least, top_value):
    extent = result.shape
    spot = [jax.random.randint(jax.random.fold_in(key, axis), (), 0, extent[axis]) for axis in range(len(extent))]
    result = result.at[tuple(spot)].set(least)
    longest = extent.index(max(extent))
    spot[longest] = (spot[longest] + 1) % extent[longest]
    return result.at[tuple(spot)].set(top_value)


def levels(rng, extent, shards, smallest, largest):
    gain, own = 1.0, jax.random.fold_in(rng, 6)
    for axis_at, shards_of in shards:
        draws = jnp.exp(jax.random.uniform(jax.random.fold_in(own, axis_at), (shards_of,), jnp.float32, smallest / len(shards), largest / len(shards)))
        gain = gain * jnp.repeat(draws, extent[axis_at] // shards_of).reshape([-1 if axis == axis_at else 1 for axis in range(len(extent))])
    return gain


def normal_values(stream_key, shape, spread, reach, split=(), kind=jnp.bfloat16):
    values = spread * jax.random.normal(stream_key, shape, jnp.float32)
    if split:
        values = values * levels(stream_key, shape, split, -0.22, 0.18)
    return jnp.clip(values, -reach, reach).astype(kind)


def setup_inputs(seed: int = 0) -> dict:
    streams_of = jax.random.split(jax.random.key(seed), 11)
    features = normal_values(streams_of[0], (NODES, D), 1.0, 6.0, ((0, 32),), jnp.float32)
    q_weight = normal_values(streams_of[1], (D, D), D ** -0.5, 0.1875, ((0, 32),), jnp.float32)
    q_bias = normal_values(streams_of[2], (D,), 0.5, 3.0, ((0, 32),), jnp.float32)
    w_weight = normal_values(streams_of[3], (2 * D, D), (2 * D) ** -0.5, 0.125, ((0, 32),), jnp.float32)
    w_bias = normal_values(streams_of[4], (D,), 0.5, 3.0, ((0, 32),), jnp.float32)
    nbr_index = plant(jax.random.randint(streams_of[5], (NODES, FANOUT), 0, NODE_DEV + DEVICES * HALO_PEER), jax.random.fold_in(streams_of[5], 1), 0, (NODE_DEV + DEVICES * HALO_PEER) - 1).astype(jnp.int32)
    nbr_count = plant(jax.random.randint(streams_of[6], (NODES,), FANOUT // 10, FANOUT + 1), jax.random.fold_in(streams_of[6], 1), FANOUT // 10, FANOUT).astype(jnp.int32)
    importance = jnp.clip(jnp.exp(math.log(10.0) - 4.6051702 * jax.random.uniform(streams_of[7], (NODES, FANOUT), jnp.float32) ** levels(streams_of[7], (NODES, FANOUT), ((0, 32),), -0.2, 0.2)), 0.1, 10.0)
    send_rows = plant(jax.random.randint(streams_of[8], (DEVICES, DEVICES, HALO_PEER), 0, NODE_DEV), jax.random.fold_in(streams_of[8], 1), 0, NODE_DEV - 1).astype(jnp.int32)
    cotangent = normal_values(streams_of[9], (NODES, D), 1.0, 6.0, ((0, 32),), jnp.float32)
    return {"features": features, "q_weight": q_weight, "q_bias": q_bias, "w_weight": w_weight, "w_bias": w_bias, "nbr_index": nbr_index, "nbr_count": nbr_count, "importance": importance, "send_rows": send_rows, "cotangent": cotangent}


@jax.custom_vjp
def low(v):
    return lax.optimization_barrier(v.astype(jnp.bfloat16)).astype(jnp.float32)

@jax.custom_vjp
def low_back(v):
    return v

def low_keep(v):
    return (low(v), None)

def low_pass(kept, grad):
    return (grad,)

def back_keep(v):
    return (v, None)

def back_low(kept, grad):
    return (low(grad),)
low.defvjp(low_keep, low_pass)
low_back.defvjp(back_keep, back_low)

def pool_block(neigh, index_block, alpha_block):
    return jnp.einsum('nk,nkd->nd', alpha_block, neigh[index_block], precision=lax.Precision.HIGHEST)

def reference(features, q_weight, q_bias, w_weight, w_bias, nbr_index, nbr_count, importance, send_rows, cotangent):
    devices = N_COMM * N_SUB
    nodes = features.shape[0]
    owned = nodes // devices
    per_peer = send_rows.shape[2]
    fanout = nbr_index.shape[1]
    local = nbr_index.reshape(devices, owned, fanout)
    owner = jnp.arange(devices, dtype=jnp.int32)[:, None, None]
    halo = jnp.maximum(local - owned, 0)
    peer = (halo // per_peer).astype(jnp.int32)
    slot = (halo % per_peer).astype(jnp.int32)
    remote = peer * owned + send_rows[peer, owner, slot]
    neighbour = jnp.where(local < owned, owner * owned + local, remote).reshape(nodes, fanout).astype(jnp.int32)
    present = jnp.arange(fanout, dtype=jnp.int32)[None, :] < nbr_count[:, None]
    weights = jnp.where(present, importance, jnp.zeros_like(importance))
    alpha = low(weights / lax.optimization_barrier(jnp.sum(weights, axis=1, keepdims=True)))
    block = math.gcd(owned, 256)
    index_blocks = neighbour.reshape(nodes // block, block, fanout)
    alpha_blocks = alpha.reshape(nodes // block, block, fanout)

    def forward(feats, qmat, qvec, wmat, wvec):
        feat_low = low(feats)
        pre_hidden = low_back(jnp.dot(feat_low, low(qmat), precision=lax.Precision.HIGHEST) + low(qvec))
        neigh = low(jax.nn.gelu(pre_hidden))
        pooled = lax.map(jax.checkpoint(lambda pair: pool_block(neigh, pair[0], pair[1])), (index_blocks, alpha_blocks))
        joined = jnp.concatenate([feat_low, low(pooled.reshape(nodes, -1))], axis=1)
        pre_out = low_back(jnp.dot(joined, low(wmat), precision=lax.Precision.HIGHEST) + low(wvec))
        act = jax.nn.gelu(pre_out)
        return act * lax.rsqrt(lax.optimization_barrier(jnp.mean(act * act, axis=1, keepdims=True)) + 1e-06)
    embedding, backward = jax.vjp(forward, features, q_weight, q_bias, w_weight, w_bias)
    grad_features, grad_q_weight, grad_q_bias, grad_w_weight, grad_w_bias = backward(cotangent)
    return (embedding, grad_features, grad_q_weight, grad_q_bias, grad_w_weight, grad_w_bias)
```

```python
import functools

import jax
import jax.numpy as jnp
from jax import lax
from jax.experimental import pallas as pl
from jax.experimental.pallas import tpu as pltpu
from jax.sharding import PartitionSpec as P

BF = jnp.bfloat16
F32 = jnp.float32


def finish(pre_out):
    act = jax.nn.gelu(pre_out)
    return act * lax.rsqrt(jnp.mean(act * act, axis=1, keepdims=True) + 1e-06)


def build_kernel(index_ref, count_ref, importance_ref, own_ref, halo_ref, *, rows, halo, block):
    his = (rows + halo + 255) // 256
    pairs = (his + 1) // 2
    fanout = index_ref.shape[1]
    lane = lax.broadcasted_iota(jnp.int32, (16, 128), 1)
    sublane = lax.broadcasted_iota(jnp.int32, (16, 128), 0)
    parity = (sublane >= 8).astype(jnp.int32)
    half = (lane >= 64).astype(jnp.int32)
    los = lax.broadcasted_iota(jnp.int32, (256, 128), 0).astype(BF)
    left = lax.broadcasted_iota(jnp.int32, (1, 128), 1) < 64
    hi_pattern = [(2 * t + parity).astype(BF) for t in range(pairs)]
    row_mask = [(sublane & 7) == 2 * c + half for c in range(4)]
    zero = jnp.zeros((), BF)
    one = jnp.ones((), BF)

    def twice(x):
        x = jnp.concatenate([x, jnp.zeros((16, 64 - fanout), F32)], axis=1)
        return jnp.concatenate([x, x], axis=1)

    def step(g, carry):
        at = pl.ds(pl.multiple_of(g * 16, 16), 16)
        index = index_ref[at, :]
        slot = lax.broadcasted_iota(jnp.int32, index.shape, 1)
        weight = jnp.where(slot < count_ref[at, :], importance_ref[at, :], 0.0)
        alpha = twice(weight / jnp.sum(weight, axis=1, keepdims=True))
        hi = twice((index >> 8).astype(F32))
        lo = twice((index & 255).astype(F32))
        tiles = []
        for s in range(2):
            left_parts, right_parts = [], []
            for c in range(4):
                r = s * 8 + 2 * c

                def pick(x):
                    return jnp.where(left, x[r : r + 1, :], x[r + 1 : r + 2, :]).astype(BF)

                lo_row = jnp.broadcast_to(pick(lo), (256, 128))
                right_parts.append(jnp.where(lo_row == los, one, zero))
                kept = jnp.where(row_mask[c], jnp.broadcast_to(pick(alpha), (16, 128)), zero)
                hi_row = jnp.broadcast_to(pick(hi), (16, 128))
                left_parts.append(
                    jnp.concatenate(
                        [jnp.where(hi_row == hi_pattern[t], kept, zero) for t in range(pairs)], axis=0
                    )
                )
            tiles.append(
                lax.dot_general(
                    jnp.concatenate(left_parts, axis=1),
                    jnp.concatenate(right_parts, axis=1),
                    (((1,), (1,)), ((), ())),
                    preferred_element_type=F32,
                )
            )
        for h in range(his):
            tile = jnp.concatenate([t[h * 8 : (h + 1) * 8, :] for t in tiles], axis=0).astype(BF)
            if h * 256 < rows:
                own_ref[at, h * 256 : (h + 1) * 256] = tile
            else:
                start = h * 256 - rows
                stop = min(start + 256, halo)
                halo_ref[at, start:stop] = tile[:, : stop - start]
        return carry

    lax.fori_loop(0, block // 16, step, 0, unroll=16)


def build_mixing(nbr_index, nbr_count, importance, halo):
    rows, fanout = nbr_index.shape
    block = 256
    return pl.pallas_call(
        functools.partial(build_kernel, rows=rows, halo=halo, block=block),
        grid=(rows // block,),
        in_specs=[
            pl.BlockSpec((block, fanout), lambda i: (i, 0)),
            pl.BlockSpec((block, 1), lambda i: (i, 0)),
            pl.BlockSpec((block, fanout), lambda i: (i, 0)),
        ],
        out_specs=[
            pl.BlockSpec((block, rows), lambda i: (i, 0)),
            pl.BlockSpec((block, halo), lambda i: (i, 0)),
        ],
        out_shape=[
            jax.ShapeDtypeStruct((rows, rows), BF),
            jax.ShapeDtypeStruct((rows, halo), BF),
        ],
        compiler_params=pltpu.CompilerParams(vmem_limit_bytes=40 * 2**20),
        cost_estimate=pl.CostEstimate(
            flops=2 * rows * 10 * 8 * 64 * 256, bytes_accessed=4 * rows * rows, transcendentals=0
        ),
        name="build_mixing",
    )(nbr_index, nbr_count.reshape(rows, 1), importance)


def shards(
    features,
    q_weight,
    q_bias,
    w_weight,
    w_bias,
    nbr_index,
    nbr_count,
    importance,
    send_rows,
    cotangent,
):
    devices = lax.axis_size(("comm", "sub"))
    rows, width = features.shape
    fanout = nbr_index.shape[1]
    per_peer = send_rows.shape[2]
    halo = devices * per_peer
    own_mix, halo_mix = build_mixing(nbr_index, nbr_count, importance, halo)
    q_full, w_full, qbias_full, wbias_full = (
        lax.all_gather(q_weight.astype(jnp.bfloat16), ("comm", "sub"), axis=0, tiled=True),
        lax.all_gather(w_weight.astype(jnp.bfloat16), ("comm", "sub"), axis=0, tiled=True),
        lax.all_gather(q_bias.astype(jnp.bfloat16), ("comm", "sub"), axis=0, tiled=True),
        lax.all_gather(w_bias.astype(jnp.bfloat16), ("comm", "sub"), axis=0, tiled=True),
    )
    feat_low = features.astype(jnp.bfloat16)
    pre_hidden = jnp.dot(feat_low, q_full, preferred_element_type=jnp.float32) + qbias_full.astype(
        jnp.float32
    )
    neigh_low = jax.nn.gelu(pre_hidden).astype(jnp.bfloat16)
    targets = send_rows[0]
    outgoing = neigh_low[targets]
    incoming = lax.all_to_all(outgoing, ("comm", "sub"), split_axis=0, concat_axis=0, tiled=True)
    pooled = jnp.dot(own_mix, neigh_low, preferred_element_type=F32) + jnp.dot(
        halo_mix, incoming.reshape(halo, width), preferred_element_type=F32
    )
    joined = jnp.concatenate([feat_low, pooled.astype(jnp.bfloat16)], axis=1)
    pre_out = jnp.dot(joined, w_full, preferred_element_type=jnp.float32) + wbias_full.astype(
        jnp.float32
    )
    embedding, finish_back = jax.vjp(finish, pre_out)
    grad_pre_out = finish_back(cotangent)[0].astype(jnp.bfloat16)
    grad_w = lax.dot_general(
        joined, grad_pre_out, (((0,), (0,)), ((), ())), preferred_element_type=jnp.float32
    )
    grad_wbias = jnp.sum(grad_pre_out.astype(jnp.float32), axis=0)
    grad_joined = lax.dot_general(
        grad_pre_out, w_full, (((1,), (1,)), ((), ())), preferred_element_type=jnp.float32
    )
    grad_pooled = grad_joined[:, width:]
    contract = (((0,), (0,)), ((), ()))

    grad_pooled = grad_pooled.astype(BF)
    outgoing_grad = lax.dot_general(halo_mix, grad_pooled, contract, preferred_element_type=F32)
    returned = lax.all_to_all(
        outgoing_grad.reshape(devices, per_peer, width),
        ("comm", "sub"),
        split_axis=0,
        concat_axis=0,
        tiled=True,
    )
    grad_neigh = lax.dot_general(own_mix, grad_pooled, contract, preferred_element_type=F32)
    grad_neigh = grad_neigh.at[targets.reshape(-1)].add(returned.reshape(halo, width))
    gelu_value, gelu_back = jax.vjp(jax.nn.gelu, pre_hidden)
    grad_pre_hidden = gelu_back(grad_neigh)[0].astype(jnp.bfloat16)
    grad_q = lax.dot_general(
        feat_low, grad_pre_hidden, (((0,), (0,)), ((), ())), preferred_element_type=jnp.float32
    )
    grad_qbias = jnp.sum(grad_pre_hidden.astype(jnp.float32), axis=0)
    grad_features = grad_joined[:, :width] + lax.dot_general(
        grad_pre_hidden, q_full, (((1,), (1,)), ((), ())), preferred_element_type=jnp.float32
    )
    grad_q_shard, grad_w_shard, grad_qbias_shard, grad_wbias_shard = (
        lax.psum_scatter(grad_q, ("comm", "sub"), scatter_dimension=0, tiled=True),
        lax.psum_scatter(grad_w, ("comm", "sub"), scatter_dimension=0, tiled=True),
        lax.psum_scatter(grad_qbias, ("comm", "sub"), scatter_dimension=0, tiled=True),
        lax.psum_scatter(grad_wbias, ("comm", "sub"), scatter_dimension=0, tiled=True),
    )
    return (
        embedding,
        grad_features,
        grad_q_shard,
        grad_qbias_shard,
        grad_w_shard,
        grad_wbias_shard,
    )


def solution(mesh):
    in_specs = (
        P(("comm", "sub"), None),
        P(("comm", "sub"), None),
        P(("comm", "sub")),
        P(("comm", "sub"), None),
        P(("comm", "sub")),
        P(("comm", "sub"), None),
        P(("comm", "sub")),
        P(("comm", "sub"), None),
        P(("comm", "sub"), None, None),
        P(("comm", "sub"), None),
    )
    out_specs = (
        P(("comm", "sub"), None),
        P(("comm", "sub"), None),
        P(("comm", "sub"), None),
        P(("comm", "sub")),
        P(("comm", "sub"), None),
        P(("comm", "sub")),
    )
    return jax.shard_map(shards, mesh=mesh, in_specs=in_specs, out_specs=out_specs, check_vma=False)
```

```python
import functools

import jax
import jax.numpy as jnp
from jax import lax
from jax.experimental import pallas as pl
from jax.experimental.pallas import tpu as pltpu
from jax.sharding import PartitionSpec as P

BF = jnp.bfloat16
F32 = jnp.float32


def finish(pre_out):
    act = jax.nn.gelu(pre_out)
    return act * lax.rsqrt(jnp.mean(act * act, axis=1, keepdims=True) + 1e-06)


def build_kernel(index_ref, count_ref, importance_ref, own_ref, halo_ref, *, rows, halo, block):
    his = (rows + halo + 255) // 256
    pairs = (his + 1) // 2
    fanout = index_ref.shape[1]
    lane = lax.broadcasted_iota(jnp.int32, (16, 128), 1)
    sublane = lax.broadcasted_iota(jnp.int32, (16, 128), 0)
    parity = (sublane >= 8).astype(jnp.int32)
    half = (lane >= 64).astype(jnp.int32)
    los = lax.broadcasted_iota(jnp.int32, (256, 128), 0).astype(BF)
    left = lax.broadcasted_iota(jnp.int32, (1, 128), 1) < 64
    hi_pattern = [(2 * t + parity).astype(BF) for t in range(pairs)]
    row_mask = [(sublane & 7) == 2 * c + half for c in range(4)]
    zero = jnp.zeros((), BF)
    one = jnp.ones((), BF)

    def twice(x):
        x = jnp.concatenate([x, jnp.zeros((16, 64 - fanout), F32)], axis=1)
        return jnp.concatenate([x, x], axis=1)

    def step(g, carry):
        at = pl.ds(pl.multiple_of(g * 16, 16), 16)
        index = index_ref[at, :]
        slot = lax.broadcasted_iota(jnp.int32, index.shape, 1)
        weight = jnp.where(slot < count_ref[at, :], importance_ref[at, :], 0.0)
        alpha = twice(weight / jnp.sum(weight, axis=1, keepdims=True))
        hi = twice((index >> 8).astype(F32))
        lo = twice((index & 255).astype(F32))
        tiles = []
        for s in range(2):
            left_parts, right_parts = [], []
            for c in range(4):
                r = s * 8 + 2 * c

                def pick(x):
                    return jnp.where(left, x[r : r + 1, :], x[r + 1 : r + 2, :]).astype(BF)

                lo_row = jnp.broadcast_to(pick(lo), (256, 128))
                right_parts.append(jnp.where(lo_row == los, one, zero))
                kept = jnp.where(row_mask[c], jnp.broadcast_to(pick(alpha), (16, 128)), zero)
                hi_row = jnp.broadcast_to(pick(hi), (16, 128))
                left_parts.append(
                    jnp.concatenate(
                        [jnp.where(hi_row == hi_pattern[t], kept, zero) for t in range(pairs)], axis=0
                    )
                )
            tiles.append(
                lax.dot_general(
                    jnp.concatenate(left_parts, axis=1),
                    jnp.concatenate(right_parts, axis=1),
                    (((1,), (1,)), ((), ())),
                    preferred_element_type=F32,
                )
            )
        for h in range(his):
            tile = jnp.concatenate([t[h * 8 : (h + 1) * 8, :] for t in tiles], axis=0).astype(BF)
            if h * 256 < rows:
                own_ref[at, h * 256 : (h + 1) * 256] = tile
            else:
                start = h * 256 - rows
                stop = min(start + 256, halo)
                halo_ref[at, start:stop] = tile[:, : stop - start]
        return carry

    lax.fori_loop(0, block // 16, step, 0, unroll=16)


def build_mixing(nbr_index, nbr_count, importance, halo):
    rows, fanout = nbr_index.shape
    block = 256
    return pl.pallas_call(
        functools.partial(build_kernel, rows=rows, halo=halo, block=block),
        grid=(rows // block,),
        in_specs=[
            pl.BlockSpec((block, fanout), lambda i: (i, 0)),
            pl.BlockSpec((block, 1), lambda i: (i, 0)),
            pl.BlockSpec((block, fanout), lambda i: (i, 0)),
        ],
        out_specs=[
            pl.BlockSpec((block, rows), lambda i: (i, 0)),
            pl.BlockSpec((block, halo), lambda i: (i, 0)),
        ],
        out_shape=[
            jax.ShapeDtypeStruct((rows, rows), BF),
            jax.ShapeDtypeStruct((rows, halo), BF),
        ],
        compiler_params=pltpu.CompilerParams(vmem_limit_bytes=40 * 2**20),
        cost_estimate=pl.CostEstimate(
            flops=2 * rows * 10 * 8 * 64 * 256, bytes_accessed=4 * rows * rows, transcendentals=0
        ),
        name="build_mixing",
    )(nbr_index, nbr_count.reshape(rows, 1), importance)


AXES = ("comm", "sub")


def swap(x, bit, devices):
    return lax.ppermute(x, AXES, [(i, i ^ (1 << bit)) for i in range(devices)])


def doubled(x, devices):
    me = lax.axis_index(AXES)
    x = x[None]
    for bit in range(devices.bit_length() - 1):
        other = swap(x, bit, devices)
        first = ((me >> bit) & 1) == 0
        x = jnp.where(first, jnp.concatenate([x, other]), jnp.concatenate([other, x]))
    return x


def summed(x, devices):
    for bit in range(devices.bit_length() - 1):
        x = x + swap(x, bit, devices)
    return x


def halve(part, left, bit, devices):
    mine = (lax.axis_index(AXES) >> bit) & 1
    axis = left.index(bit)
    keep = lax.dynamic_index_in_dim(part, mine, axis, keepdims=False)
    sent = lax.dynamic_index_in_dim(part, 1 - mine, axis, keepdims=False)
    total = keep.astype(F32) + swap(sent, bit, devices).astype(F32)
    return total, [b for b in left if b != bit]


def scatter_sum(partial, devices):
    bits = list(range(devices.bit_length() - 1))[::-1]
    width = partial.shape[1]
    part = partial.reshape([2] * len(bits) + [-1, width])
    part, left = halve(part, bits, 0, devices)
    part = part.astype(BF)
    rows = part.shape[-2] // 2
    orders = ([1, 2] + list(range(3, len(bits))), [2, 1] + list(range(3, len(bits))))
    halves = [(part[..., :rows, :], left), (part[..., rows:, :], left)]
    for step in range(len(bits) - 1):
        for s in range(2):
            total, rest = halve(halves[s][0], halves[s][1], orders[s][step], devices)
            halves[s] = (total if len(rest) == 0 else total.astype(BF), rest)
    return jnp.concatenate([h[0] for h in halves], axis=0)


def shards(
    features,
    q_weight,
    q_bias,
    w_weight,
    w_bias,
    nbr_index,
    nbr_count,
    importance,
    send_rows,
    cotangent,
):
    devices = lax.axis_size(("comm", "sub"))
    rows, width = features.shape
    fanout = nbr_index.shape[1]
    per_peer = send_rows.shape[2]
    halo = devices * per_peer
    own_mix, halo_mix = build_mixing(nbr_index, nbr_count, importance, halo)
    q_full, w_full = (
        lax.all_gather(q_weight.astype(BF), AXES, axis=0, tiled=True),
        lax.all_gather(w_weight.astype(BF), AXES, axis=0, tiled=True),
    )
    biases = doubled(jnp.stack([q_bias, w_bias]), devices)
    qbias_full = biases[:, 0].reshape(width).astype(BF)
    wbias_full = biases[:, 1].reshape(width).astype(BF)
    feat_low = features.astype(jnp.bfloat16)
    pre_hidden = jnp.dot(feat_low, q_full, preferred_element_type=jnp.float32) + qbias_full.astype(
        jnp.float32
    )
    neigh_low = jax.nn.gelu(pre_hidden).astype(jnp.bfloat16)
    targets = send_rows[0]
    outgoing = neigh_low[targets]
    incoming = lax.all_to_all(outgoing, ("comm", "sub"), split_axis=0, concat_axis=0, tiled=True)
    pooled = jnp.dot(own_mix, neigh_low, preferred_element_type=F32) + jnp.dot(
        halo_mix, incoming.reshape(halo, width), preferred_element_type=F32
    )
    joined = jnp.concatenate([feat_low, pooled.astype(jnp.bfloat16)], axis=1)
    pre_out = jnp.dot(joined, w_full, preferred_element_type=jnp.float32) + wbias_full.astype(
        jnp.float32
    )
    embedding, finish_back = jax.vjp(finish, pre_out)
    grad_pre_out = finish_back(cotangent)[0].astype(jnp.bfloat16)
    grad_w = lax.dot_general(
        joined, grad_pre_out, (((0,), (0,)), ((), ())), preferred_element_type=jnp.float32
    )
    grad_wbias = jnp.sum(grad_pre_out.astype(jnp.float32), axis=0)
    grad_joined = lax.dot_general(
        grad_pre_out, w_full, (((1,), (1,)), ((), ())), preferred_element_type=jnp.float32
    )
    grad_pooled = grad_joined[:, width:]
    contract = (((0,), (0,)), ((), ()))

    grad_pooled = grad_pooled.astype(BF)
    outgoing_grad = lax.dot_general(halo_mix, grad_pooled, contract, preferred_element_type=F32)
    returned = lax.all_to_all(
        outgoing_grad.reshape(devices, per_peer, width),
        ("comm", "sub"),
        split_axis=0,
        concat_axis=0,
        tiled=True,
    )
    grad_neigh = lax.dot_general(own_mix, grad_pooled, contract, preferred_element_type=F32)
    grad_neigh = grad_neigh.at[targets.reshape(-1)].add(returned.reshape(halo, width))
    gelu_value, gelu_back = jax.vjp(jax.nn.gelu, pre_hidden)
    grad_pre_hidden = gelu_back(grad_neigh)[0].astype(jnp.bfloat16)
    grad_q = lax.dot_general(
        feat_low, grad_pre_hidden, (((0,), (0,)), ((), ())), preferred_element_type=jnp.float32
    )
    grad_qbias = jnp.sum(grad_pre_hidden.astype(jnp.float32), axis=0)
    grad_features = grad_joined[:, :width] + lax.dot_general(
        grad_pre_hidden, q_full, (((1,), (1,)), ((), ())), preferred_element_type=jnp.float32
    )
    me = lax.axis_index(AXES)
    bias_sums = summed(jnp.stack([grad_qbias, grad_wbias]), devices)
    bias_shards = lax.dynamic_slice_in_dim(bias_sums, me * (width // devices), width // devices, 1)
    grad_q_shard = scatter_sum(grad_q.astype(BF), devices)
    grad_w_shard = scatter_sum(grad_w.astype(BF), devices)
    grad_qbias_shard, grad_wbias_shard = bias_shards[0], bias_shards[1]
    return (
        embedding,
        grad_features,
        grad_q_shard,
        grad_qbias_shard,
        grad_w_shard,
        grad_wbias_shard,
    )


def solution(mesh):
    in_specs = (
        P(("comm", "sub"), None),
        P(("comm", "sub"), None),
        P(("comm", "sub")),
        P(("comm", "sub"), None),
        P(("comm", "sub")),
        P(("comm", "sub"), None),
        P(("comm", "sub")),
        P(("comm", "sub"), None),
        P(("comm", "sub"), None, None),
        P(("comm", "sub"), None),
    )
    out_specs = (
        P(("comm", "sub"), None),
        P(("comm", "sub"), None),
        P(("comm", "sub"), None),
        P(("comm", "sub")),
        P(("comm", "sub"), None),
        P(("comm", "sub")),
    )
    return jax.shard_map(shards, mesh=mesh, in_specs=in_specs, out_specs=out_specs, check_vma=False)
```

```python
import functools
import math

import jax
import jax.numpy as jnp
from jax import lax
from jax.experimental import pallas as pl
from jax.experimental.pallas import tpu as pltpu
from jax.sharding import PartitionSpec as P

BF = jnp.bfloat16
F32 = jnp.float32
AXES = ("comm", "sub")


def build_rows(index_ref, count_ref, importance_ref, own_ref, halo_ref, first, *, rows, halo):
    his = (rows + halo + 255) // 256
    pairs = (his + 1) // 2
    fanout = index_ref.shape[0]
    at = slice(first, first + 128)
    lane = lax.broadcasted_iota(jnp.int32, (16, 128), 1)
    sublane = lax.broadcasted_iota(jnp.int32, (16, 128), 0)
    parity = (sublane >= 8).astype(jnp.int32)
    half = (lane >= 64).astype(jnp.int32)
    los = lax.broadcasted_iota(jnp.int32, (64, 256), 1).astype(BF)
    left = lax.broadcasted_iota(jnp.int32, (1, 128), 1) < 64
    hi_pattern = [(2 * t + parity).astype(BF) for t in range(pairs)]
    row_mask = [(sublane & 7) == 2 * c + half for c in range(4)]
    zero = jnp.zeros((), BF)
    one = jnp.ones((), BF)

    def slots(x):
        return jnp.concatenate([x, jnp.zeros((64 - fanout, 128), F32)], axis=0)

    def by_row(x):
        x = slots(x).T
        return jnp.concatenate([x, x], axis=1)

    index = index_ref[:, at]
    slot = lax.broadcasted_iota(jnp.int32, index.shape, 0)
    weight = jnp.where(slot < count_ref[:, at], importance_ref[:, at], 0.0)
    alpha = by_row(weight / jnp.sum(weight, axis=0, keepdims=True))
    hi = by_row((index >> 8).astype(F32))
    lo = slots((index & 255).astype(F32)).astype(BF)
    for g in range(0, 128, 16):
        tiles = []
        for s in range(2):
            left_parts, right_parts = [], []
            for c in range(4):
                r = g + s * 8 + 2 * c

                def pick(x):
                    return jnp.where(left, x[r : r + 1, :], x[r + 1 : r + 2, :]).astype(BF)

                kept = jnp.where(row_mask[c], jnp.broadcast_to(pick(alpha), (16, 128)), zero)
                hi_row = jnp.broadcast_to(pick(hi), (16, 128))
                left_parts.append(
                    jnp.concatenate(
                        [jnp.where(hi_row == hi_pattern[t], kept, zero) for t in range(pairs)], axis=0
                    )
                )
                for q in (r, r + 1):
                    right_parts.append(jnp.where(jnp.broadcast_to(lo[:, q : q + 1], (64, 256)) == los, one, zero))
            tiles.append(
                jnp.dot(
                    jnp.concatenate(left_parts, axis=1),
                    jnp.concatenate(right_parts, axis=0),
                    preferred_element_type=F32,
                )
            )
        for h in range(his):
            tile = jnp.concatenate([t[h * 8 : (h + 1) * 8, :] for t in tiles], axis=0).astype(BF)
            to = slice(first + g, first + g + 16)
            if h * 256 < rows:
                own_ref[to, h * 256 : (h + 1) * 256] = tile
            else:
                start = h * 256 - rows
                stop = min(start + 256, halo)
                halo_ref[to, start:stop] = tile[:, : stop - start]


def build_kernel(index_ref, count_ref, importance_ref, own_ref, halo_ref, *, rows, halo):
    for first in range(0, own_ref.shape[0], 128):
        build_rows(index_ref, count_ref, importance_ref, own_ref, halo_ref, first, rows=rows, halo=halo)


def build_mixing(nbr_index, nbr_count, importance, halo):
    rows, fanout = nbr_index.shape
    block = 256
    return pl.pallas_call(
        functools.partial(build_kernel, rows=rows, halo=halo),
        grid=(rows // block,),
        in_specs=[
            pl.BlockSpec((fanout, block), lambda i: (0, i)),
            pl.BlockSpec((1, block), lambda i: (0, i)),
            pl.BlockSpec((fanout, block), lambda i: (0, i)),
        ],
        out_specs=[
            pl.BlockSpec((block, rows), lambda i: (i, 0)),
            pl.BlockSpec((block, halo), lambda i: (i, 0)),
        ],
        out_shape=[
            jax.ShapeDtypeStruct((rows, rows), BF),
            jax.ShapeDtypeStruct((rows, halo), BF),
        ],
        compiler_params=pltpu.CompilerParams(vmem_limit_bytes=40 * 2**20),
        name="build_mixing",
    )(nbr_index.T, nbr_count.reshape(1, rows), importance.T)


def gelu_pair(x):
    c = math.sqrt(2.0 / math.pi)
    square = x * x
    t = jnp.tanh(x * (c + (c * 0.044715) * square))
    half = 0.5 + 0.5 * t
    slope = x * (0.5 - 0.5 * t * t) * (c + (3.0 * c * 0.044715) * square)
    return x * half, half + slope


def hidden_rows(features_ref, q, bias, sent_rows, low_ref, neigh_ref, slope_ref, sent_ref, start):
    block, width = features_ref.shape
    low_ref[...] = features_ref[...].astype(BF)
    for c in range(0, width, 256):
        pre = jnp.dot(low_ref[...], q[:, c : c + 256], preferred_element_type=F32) + bias[:, c : c + 256]
        value, slope = gelu_pair(pre)
        neigh_ref[:, c : c + 256] = value.astype(BF)
        slope_ref[:, c : c + 256] = slope.astype(BF)
    local = lax.broadcasted_iota(jnp.int32, (sent_rows.shape[0], block), 1) + start
    chosen = jnp.where(local == sent_rows, 1.0, 0.0).astype(BF)
    picked = jnp.dot(chosen, neigh_ref[...], preferred_element_type=F32)
    sent_ref[...] += picked


def gather_kernel(
    index_ref,
    count_ref,
    importance_ref,
    features_ref,
    q_ref,
    w_ref,
    bias_ref,
    send_ref,
    own_ref,
    halo_ref,
    low_ref,
    neigh_ref,
    slope_ref,
    sent_ref,
    q_full,
    w_full,
    bias_out,
    q_buf,
    w_own,
    bias_buf,
    sent_acc,
    local_sem,
    send_sem,
    recv_sem,
    *,
    subs,
    bits,
):
    i = pl.program_id(0)
    rows = own_ref.shape[1]
    halo = halo_ref.shape[1]
    builds = rows // own_ref.shape[0]
    block, width = features_ref.shape
    steps = builds + rows // block
    me = lax.axis_index("comm") * subs + lax.axis_index("sub")
    mine = [(me // (1 << b)) % 2 for b in range(bits)]
    order = list(range(bits))[::-1]

    def partner(b):
        other = me + (1 << b) * (1 - 2 * mine[b])
        return (other // subs, other % subs)

    def spot(done, part=slice(None), columns=slice(None)):
        lead = tuple(slice(None) if b in done else mine[b] for b in order)
        return lead + (part, columns)

    def copy(n, source, target, b):
        return pltpu.make_async_remote_copy(
            src_ref=source,
            dst_ref=target,
            send_sem=send_sem.at[n],
            recv_sem=recv_sem.at[n],
            device_id=partner(b),
            device_id_type=pl.DeviceIdType.MESH,
        )

    high = list(range(3, bits))[::-1]
    left, right = pl.ds(0, width // 2), pl.ds(width // 2, width // 2)
    count = [0]

    def exchange(buf, b, done, part=slice(None), columns=slice(None), source=None):
        at = buf.at[spot(done, part, columns)]
        n = count[0]
        count[0] += 1
        return copy(n, at if source is None else source, at, b)

    def chain(buf, own, split, part=slice(None)):
        groups = []
        done = []
        for b in high:
            groups.append([exchange(buf, b, done, part, source=own if not done else None)])
            done = done + [b]
        if split:
            groups.append([exchange(buf, 1, done, part, left), exchange(buf, 2, done, part, right)])
            groups.append(
                [exchange(buf, 2, done + [1], part, left), exchange(buf, 1, done + [2], part, right)]
            )
        else:
            groups.append([exchange(buf, 1, done)])
            groups.append([exchange(buf, 2, done + [1])])
        groups.append([exchange(buf, 0, done + [1, 2], part)])
        return groups

    w_rows = w_own.shape[0]
    top, bottom = pl.ds(0, w_rows // 2), pl.ds(w_rows // 2, w_rows // 2)
    chains = {
        "q": chain(q_buf, None, True),
        "bias": chain(bias_buf, None, False),
        "w0": chain(w_full, w_own.at[top], True, top),
        "w1": chain(w_full, w_own.at[bottom], True, bottom),
    }
    w_local = pltpu.make_async_copy(w_own, w_full.at[spot([])], local_sem.at[0])
    q_local = pltpu.make_async_copy(q_buf, q_full, local_sem.at[1])
    last = len(chains["q"]) - 1

    def begin(name, n):
        for c in chains[name][n]:
            c.start()

    def finish(name, n):
        for c in chains[name][n]:
            c.wait()

    def advance(name, n):
        finish(name, n)
        begin(name, n + 1)

    @pl.when(i == 0)
    def _():
        q_buf[spot([])] = q_ref[...].astype(BF)
        w_own[...] = w_ref[...].astype(BF)
        bias_buf[spot([])] = bias_ref[...]
        sent_acc[...] = jnp.zeros_like(sent_acc)
        w_local.start()
        barrier = pltpu.get_barrier_semaphore()
        for b in range(bits):
            pl.semaphore_signal(barrier, inc=1, device_id=partner(b), device_id_type=pl.DeviceIdType.MESH)
        pl.semaphore_wait(barrier, bits)
        begin("q", 0)
        begin("bias", 0)
        w_local.wait()

    events = {
        (0, 1): [("w0", -1)],
        (2, 0): [("q", 0), ("bias", 0)],
        (3, 0): [("w0", 0), ("w1", -1)],
        (3, 1): [("q", 1), ("bias", 1)],
        (4, 1): [("w0", 1)],
        (5, 0): [("q", 2), ("bias", 2)],
        (5, 1): [("w1", 0)],
        (7, 0): [("w0", 2), ("w1", 1)],
        (8, 0): [("q", 3), ("bias", 3)],
        (builds + 1, 0): [("w0", 3)],
        (builds + 2, 0): [("w1", 2)],
    }

    def happen(part):
        for (step, at), names in events.items():
            if at == part:

                @pl.when(i == step)
                def _(names=names):
                    for name, n in names:
                        if n < 0:
                            begin(name, 0)
                        else:
                            advance(name, n)

    happen(0)
    for part in range(2):
        if part == 1:
            happen(1)

        @pl.when(i < builds)
        def _(part=part):
            build_rows(
                index_ref, count_ref, importance_ref, own_ref, halo_ref, part * 128, rows=rows, halo=halo
            )

    @pl.when(i == builds)
    def _():
        finish("q", last)
        finish("bias", last)
        q_local.start()
        share = width >> bits
        for k in range(2):
            pieces = []
            for e in range(1 << bits):
                piece = bias_buf[tuple((e >> b) & 1 for b in order)]
                pieces.append(piece[0:1, k * share : (k + 1) * share])
            bias_out[k : k + 1, :] = jnp.concatenate(pieces, axis=1).astype(BF).astype(F32)
        bias_out[2:, :] = jnp.zeros((6, width), F32)

    @pl.when(i >= builds)
    def _():
        q = q_buf[...].reshape(width, width)
        hidden_rows(
            features_ref,
            q,
            bias_out[0:1, :],
            send_ref[...],
            low_ref,
            neigh_ref,
            slope_ref,
            sent_acc,
            (i - builds) * block,
        )

    @pl.when(i == steps - 1)
    def _():
        sent_ref[...] = sent_acc[...].astype(BF)
        finish("w0", last)
        advance("w1", last - 1)
        q_local.wait()
        finish("w1", last)


def gather_and_transform(features, q_weight, q_bias, w_weight, w_bias, nbr_index, nbr_count, importance, send_rows):
    comms, subs = lax.axis_size("comm"), lax.axis_size("sub")
    devices = comms * subs
    bits = devices.bit_length() - 1
    rows, width = features.shape
    fanout = nbr_index.shape[1]
    halo = send_rows.shape[1] * send_rows.shape[2]
    block = 256
    builds = rows // block
    q_rows, w_rows = q_weight.shape[0], w_weight.shape[0]
    share = q_bias.shape[0]
    bias_tile = jnp.pad(jnp.concatenate([q_bias, w_bias])[None], ((0, 7), (0, 128 - 2 * share)))
    lead = (2,) * bits

    def built(i):
        return (jnp.minimum(i, builds - 1), 0)

    def built_columns(i):
        return (0, jnp.minimum(i, builds - 1))

    def later(i):
        return (jnp.maximum(i - builds, 0), 0)

    def whole(*shape):
        return pl.BlockSpec(shape, lambda i: (0,) * len(shape))

    copies = 4 * bits + 3 * 2
    out = pl.pallas_call(
        functools.partial(gather_kernel, subs=subs, bits=bits),
        grid=(builds + rows // block,),
        in_specs=[
            pl.BlockSpec((fanout, block), built_columns),
            pl.BlockSpec((1, block), built_columns),
            pl.BlockSpec((fanout, block), built_columns),
            pl.BlockSpec((block, width), later),
            whole(q_rows, width),
            whole(w_rows, width),
            whole(8, 128),
            whole(halo, 1),
        ],
        out_specs=[
            pl.BlockSpec((block, rows), built),
            pl.BlockSpec((block, halo), built),
            pl.BlockSpec((block, width), later),
            pl.BlockSpec((block, width), later),
            pl.BlockSpec((block, width), later),
            whole(halo, width),
            pl.BlockSpec(memory_space=pl.ANY),
            pl.BlockSpec(memory_space=pl.ANY),
            whole(8, width),
        ],
        out_shape=[
            jax.ShapeDtypeStruct((rows, rows), BF),
            jax.ShapeDtypeStruct((rows, halo), BF),
            jax.ShapeDtypeStruct((rows, width), BF),
            jax.ShapeDtypeStruct((rows, width), BF),
            jax.ShapeDtypeStruct((rows, width), BF),
            jax.ShapeDtypeStruct((halo, width), BF),
            jax.ShapeDtypeStruct(lead + (q_rows, width), BF),
            jax.ShapeDtypeStruct(lead + (w_rows, width), BF),
            jax.ShapeDtypeStruct((8, width), F32),
        ],
        scratch_shapes=[
            pltpu.VMEM(lead + (q_rows, width), BF),
            pltpu.VMEM((w_rows, width), BF),
            pltpu.VMEM(lead + (8, 128), F32),
            pltpu.VMEM((halo, width), F32),
            pltpu.SemaphoreType.DMA((2,)),
            pltpu.SemaphoreType.DMA((copies,)),
            pltpu.SemaphoreType.DMA((copies,)),
        ],
        compiler_params=pltpu.CompilerParams(
            collective_id=0, has_side_effects=True, vmem_limit_bytes=48 * 2**20
        ),
        name="gather_and_transform",
    )(
        nbr_index.T,
        nbr_count.reshape(1, rows),
        importance.T,
        features,
        q_weight,
        w_weight,
        bias_tile,
        send_rows.reshape(halo, 1),
    )
    own_mix, halo_mix, low, neigh, slope, sent, q_full, w_full, biases = out
    return (
        own_mix,
        halo_mix,
        low,
        neigh,
        slope,
        sent,
        q_full.reshape(devices * q_rows, width),
        w_full.reshape(devices * w_rows, width),
        biases[0],
        biases[1],
    )


def gather_plain(features, q_weight, q_bias, w_weight, w_bias, nbr_index, nbr_count, importance, send_rows):
    rows, width = features.shape
    devices, per_peer = send_rows.shape[1:]
    halo = devices * per_peer
    own_mix, halo_mix = build_mixing(nbr_index, nbr_count, importance, halo)
    q_full = lax.all_gather(q_weight.astype(BF), AXES, axis=0, tiled=True)
    w_full = lax.all_gather(w_weight.astype(BF), AXES, axis=0, tiled=True)
    biases = doubled(jnp.stack([q_bias, w_bias]), devices)
    qbias_full = biases[:, 0].reshape(width).astype(BF).astype(F32)
    wbias_full = biases[:, 1].reshape(width).astype(BF).astype(F32)
    low = features.astype(BF)
    neigh, slope = gelu_pair(jnp.dot(low, q_full, preferred_element_type=F32) + qbias_full)
    neigh = neigh.astype(BF)
    sent = neigh[send_rows.reshape(-1)]
    return own_mix, halo_mix, low, neigh, slope.astype(BF), sent, q_full, w_full, qbias_full, wbias_full


def resident(*shape):
    return pl.BlockSpec(shape, lambda i: (0,) * len(shape), pipeline_mode=pl.Buffered(1))


def by_rows(*shape):
    return pl.BlockSpec(shape, lambda i: (i,) + (0,) * (len(shape) - 1))


def product_kernel(mix_ref, table_ref, out_ref):
    out_ref[...] = jnp.dot(mix_ref[...], table_ref[...], preferred_element_type=F32)


def pool_own(own_mix, neigh):
    rows, width = neigh.shape
    block = 384
    return pl.pallas_call(
        product_kernel,
        grid=(rows // block,),
        in_specs=[by_rows(block, rows), resident(rows, width)],
        out_specs=by_rows(block, width),
        out_shape=jax.ShapeDtypeStruct((rows, width), F32),
        compiler_params=pltpu.CompilerParams(vmem_limit_bytes=40 * 2**20),
        cost_estimate=pl.CostEstimate(
            flops=2 * rows * rows * width, bytes_accessed=2 * rows * rows + 6 * rows * width, transcendentals=0
        ),
        name="pool_own",
    )(own_mix, neigh)


def combine_kernel(
    own_ref,
    halo_ref,
    incoming_ref,
    low_ref,
    w_ref,
    bias_ref,
    cotangent_ref,
    embedding_ref,
    pooled_ref,
    grad_ref,
    grad_pooled_ref,
    sent_ref,
    bias_grad_ref,
    act_buf,
    slope_buf,
):
    i = pl.program_id(0)
    block, width = low_ref.shape
    chunk = 256

    @pl.when(i == 0)
    def _():
        sent_ref[...] = jnp.zeros_like(sent_ref)
        bias_grad_ref[...] = jnp.zeros_like(bias_grad_ref)

    pooled = own_ref[...] + jnp.dot(halo_ref[...], incoming_ref[...], preferred_element_type=F32)
    pooled_ref[...] = pooled.astype(BF)
    squares = jnp.zeros((block, 128), F32)
    dots = jnp.zeros((block, 128), F32)
    for c in range(0, width, chunk):
        at = slice(c, c + chunk)
        pre = jnp.dot(low_ref[...], w_ref[:width, at], preferred_element_type=F32)
        pre += jnp.dot(pooled_ref[...], w_ref[width:, at], preferred_element_type=F32)
        act, slope = gelu_pair(pre + bias_ref[:, at])
        act_buf[:, at] = act
        slope_buf[:, at] = slope
        square = act * act
        dot = act * cotangent_ref[:, at]
        for k in range(0, chunk, 128):
            squares += square[:, k : k + 128]
            dots += dot[:, k : k + 128]
    scale = lax.rsqrt(jnp.sum(squares, axis=1, keepdims=True) * (1.0 / width) + 1e-06)
    pull = jnp.sum(dots, axis=1, keepdims=True) * (1.0 / width) * scale * scale * scale
    for c in range(0, width, chunk):
        at = slice(c, c + chunk)
        act = act_buf[:, at]
        embedding_ref[:, at] = act * scale
        grad = slope_buf[:, at] * (cotangent_ref[:, at] * scale - act * pull)
        grad_ref[:, at] = grad.astype(BF)
        bias_grad_ref[0:1, at] += jnp.sum(grad_ref[:, at].astype(F32), axis=0, keepdims=True)
    for c in range(0, width, chunk):
        at = slice(c, c + chunk)
        back = lax.dot_general(
            grad_ref[...],
            w_ref[width + c : width + c + chunk, :],
            (((1,), (1,)), ((), ())),
            preferred_element_type=F32,
        )
        grad_pooled_ref[:, at] = back.astype(BF)
    sent_ref[...] += lax.dot_general(
        halo_ref[...], grad_pooled_ref[...], (((0,), (0,)), ((), ())), preferred_element_type=F32
    )


def combine(pooled_own, halo_mix, incoming, low, w_full, w_bias, cotangent):
    rows, width = low.shape
    halo = incoming.shape[0]
    block = 256
    return pl.pallas_call(
        combine_kernel,
        grid=(rows // block,),
        in_specs=[
            by_rows(block, width),
            by_rows(block, halo),
            resident(halo, width),
            by_rows(block, width),
            resident(2 * width, width),
            resident(1, width),
            by_rows(block, width),
        ],
        out_specs=[
            by_rows(block, width),
            by_rows(block, width),
            by_rows(block, width),
            by_rows(block, width),
            pl.BlockSpec((halo, width), lambda i: (0, 0)),
            pl.BlockSpec((8, width), lambda i: (0, 0)),
        ],
        out_shape=[
            jax.ShapeDtypeStruct((rows, width), F32),
            jax.ShapeDtypeStruct((rows, width), BF),
            jax.ShapeDtypeStruct((rows, width), BF),
            jax.ShapeDtypeStruct((rows, width), BF),
            jax.ShapeDtypeStruct((halo, width), F32),
            jax.ShapeDtypeStruct((8, width), F32),
        ],
        scratch_shapes=[pltpu.VMEM((block, width), F32), pltpu.VMEM((block, width), F32)],
        compiler_params=pltpu.CompilerParams(vmem_limit_bytes=48 * 2**20),
        cost_estimate=pl.CostEstimate(
            flops=6 * rows * width * width, bytes_accessed=22 * rows * width, transcendentals=rows * width
        ),
        name="combine",
    )(pooled_own, halo_mix, incoming, low, w_full, w_bias.reshape(1, width), cotangent)


def swap(x, bit, devices):
    return lax.ppermute(x, AXES, [(i, i ^ (1 << bit)) for i in range(devices)])


def doubled(x, devices):
    me = lax.axis_index(AXES)
    x = x[None]
    for bit in range(devices.bit_length() - 1):
        other = swap(x, bit, devices)
        first = ((me >> bit) & 1) == 0
        x = jnp.where(first, jnp.concatenate([x, other]), jnp.concatenate([other, x]))
    return x


def summed(x, devices):
    for bit in range(devices.bit_length() - 1):
        x = x + swap(x, bit, devices)
    return x


def halve(part, left, bit, devices):
    mine = (lax.axis_index(AXES) >> bit) & 1
    axis = left.index(bit)
    keep = lax.dynamic_index_in_dim(part, mine, axis, keepdims=False)
    sent = lax.dynamic_index_in_dim(part, 1 - mine, axis, keepdims=False)
    total = keep.astype(F32) + swap(sent, bit, devices).astype(F32)
    return total, [b for b in left if b != bit]


def scatter_sum(partial, devices):
    bits = list(range(devices.bit_length() - 1))[::-1]
    width = partial.shape[1]
    part = partial.reshape([2] * len(bits) + [-1, width])
    part, left = halve(part, bits, 0, devices)
    part = part.astype(BF)
    rows = part.shape[-2] // 2
    orders = ([1, 2] + list(range(3, len(bits))), [2, 1] + list(range(3, len(bits))))
    halves = [(part[..., :rows, :], left), (part[..., rows:, :], left)]
    for step in range(len(bits) - 1):
        for s in range(2):
            total, rest = halve(halves[s][0], halves[s][1], orders[s][step], devices)
            halves[s] = (total if len(rest) == 0 else total.astype(BF), rest)
    return jnp.concatenate([h[0] for h in halves], axis=0)


def shards(
    features,
    q_weight,
    q_bias,
    w_weight,
    w_bias,
    nbr_index,
    nbr_count,
    importance,
    send_rows,
    cotangent,
):
    devices = lax.axis_size(("comm", "sub"))
    rows, width = features.shape
    fanout = nbr_index.shape[1]
    per_peer = send_rows.shape[2]
    halo = devices * per_peer
    kernel_fits = devices == 32 and q_weight.shape[0] % 16 == 0
    gather = gather_and_transform if kernel_fits else gather_plain
    own_mix, halo_mix, feat_low, neigh_low, slope, outgoing, q_full, w_full, qbias_full, wbias_full = gather(
        features, q_weight, q_bias, w_weight, w_bias, nbr_index, nbr_count, importance, send_rows
    )
    targets = send_rows[0]
    incoming = lax.all_to_all(
        outgoing.reshape(devices, per_peer, width), AXES, split_axis=0, concat_axis=0, tiled=True
    )
    pooled_own = pool_own(own_mix, neigh_low)
    embedding, pooled, grad_pre_out, grad_pooled, outgoing_grad, grad_wbias = combine(
        pooled_own, halo_mix, incoming.reshape(halo, width), feat_low, w_full, wbias_full, cotangent
    )
    grad_wbias = grad_wbias[0]
    joined = jnp.concatenate([feat_low, pooled], axis=1)
    contract = (((0,), (0,)), ((), ()))
    grad_w = lax.dot_general(joined, grad_pre_out, contract, preferred_element_type=F32)
    grad_low = lax.dot_general(
        grad_pre_out, w_full[:width], (((1,), (1,)), ((), ())), preferred_element_type=F32
    )
    returned = lax.all_to_all(
        outgoing_grad.reshape(devices, per_peer, width),
        ("comm", "sub"),
        split_axis=0,
        concat_axis=0,
        tiled=True,
    )
    grad_neigh = lax.dot_general(own_mix, grad_pooled, contract, preferred_element_type=F32)
    grad_neigh = grad_neigh.at[targets.reshape(-1)].add(returned.reshape(halo, width))
    grad_pre_hidden = (slope.astype(F32) * grad_neigh).astype(BF)
    grad_q = lax.dot_general(
        feat_low, grad_pre_hidden, (((0,), (0,)), ((), ())), preferred_element_type=jnp.float32
    )
    grad_qbias = jnp.sum(grad_pre_hidden.astype(jnp.float32), axis=0)
    grad_features = grad_low + lax.dot_general(
        grad_pre_hidden, q_full, (((1,), (1,)), ((), ())), preferred_element_type=jnp.float32
    )
    me = lax.axis_index(AXES)
    bias_sums = summed(jnp.stack([grad_qbias, grad_wbias]), devices)
    bias_shards = lax.dynamic_slice_in_dim(bias_sums, me * (width // devices), width // devices, 1)
    grad_q_shard = scatter_sum(grad_q.astype(BF), devices)
    grad_w_shard = scatter_sum(grad_w.astype(BF), devices)
    grad_qbias_shard, grad_wbias_shard = bias_shards[0], bias_shards[1]
    return (
        embedding,
        grad_features,
        grad_q_shard,
        grad_qbias_shard,
        grad_w_shard,
        grad_wbias_shard,
    )


def solution(mesh):
    in_specs = (
        P(("comm", "sub"), None),
        P(("comm", "sub"), None),
        P(("comm", "sub")),
        P(("comm", "sub"), None),
        P(("comm", "sub")),
        P(("comm", "sub"), None),
        P(("comm", "sub")),
        P(("comm", "sub"), None),
        P(("comm", "sub"), None, None),
        P(("comm", "sub"), None),
    )
    out_specs = (
        P(("comm", "sub"), None),
        P(("comm", "sub"), None),
        P(("comm", "sub"), None),
        P(("comm", "sub")),
        P(("comm", "sub"), None),
        P(("comm", "sub")),
    )
    return jax.shard_map(shards, mesh=mesh, in_specs=in_specs, out_specs=out_specs, check_vma=False)
```

```python
import functools
import math

import jax
import jax.numpy as jnp
from jax import lax
from jax.experimental import pallas as pl
from jax.experimental.pallas import tpu as pltpu
from jax.sharding import PartitionSpec as P

BF = jnp.bfloat16
F32 = jnp.float32
AXES = ("comm", "sub")


def build_rows(index_ref, count_ref, importance_ref, own_ref, halo_ref, first, target, *, rows, halo):
    his = (rows + halo + 255) // 256
    pairs = (his + 1) // 2
    fanout = index_ref.shape[0]
    at = slice(first, first + 128)
    lane = lax.broadcasted_iota(jnp.int32, (16, 128), 1)
    sublane = lax.broadcasted_iota(jnp.int32, (16, 128), 0)
    parity = (sublane >= 8).astype(jnp.int32)
    half = (lane >= 64).astype(jnp.int32)
    los = lax.broadcasted_iota(jnp.int32, (64, 256), 1).astype(BF)
    left = lax.broadcasted_iota(jnp.int32, (1, 128), 1) < 64
    hi_pattern = [(2 * t + parity).astype(BF) for t in range(pairs)]
    row_mask = [(sublane & 7) == 2 * c + half for c in range(4)]
    zero = jnp.zeros((), BF)
    one = jnp.ones((), BF)

    def slots(x):
        return jnp.concatenate([x, jnp.zeros((64 - fanout, 128), F32)], axis=0)

    def by_row(x):
        x = slots(x).T
        return jnp.concatenate([x, x], axis=1)

    index = index_ref[:, at]
    slot = lax.broadcasted_iota(jnp.int32, index.shape, 0)
    weight = jnp.where(slot < count_ref[:, at], importance_ref[:, at], 0.0)
    alpha = by_row(weight / jnp.sum(weight, axis=0, keepdims=True))
    hi = by_row((index >> 8).astype(F32))
    lo = slots((index & 255).astype(F32)).astype(BF)
    for g in range(0, 128, 16):
        tiles = []
        for s in range(2):
            left_parts, right_parts = [], []
            for c in range(4):
                r = g + s * 8 + 2 * c

                def pick(x):
                    return jnp.where(left, x[r : r + 1, :], x[r + 1 : r + 2, :]).astype(BF)

                kept = jnp.where(row_mask[c], jnp.broadcast_to(pick(alpha), (16, 128)), zero)
                hi_row = jnp.broadcast_to(pick(hi), (16, 128))
                left_parts.append(
                    jnp.concatenate(
                        [jnp.where(hi_row == hi_pattern[t], kept, zero) for t in range(pairs)], axis=0
                    )
                )
                for q in (r, r + 1):
                    right_parts.append(jnp.where(jnp.broadcast_to(lo[:, q : q + 1], (64, 256)) == los, one, zero))
            tiles.append(
                jnp.dot(
                    jnp.concatenate(left_parts, axis=1),
                    jnp.concatenate(right_parts, axis=0),
                    preferred_element_type=F32,
                )
            )
        for h in range(his):
            tile = jnp.concatenate([t[h * 8 : (h + 1) * 8, :] for t in tiles], axis=0).astype(BF)
            to = slice(first + g, first + g + 16)
            if h * 256 < rows:
                own_ref[pl.ds(pl.multiple_of(target + g, 16), 16), h * 256 : (h + 1) * 256] = tile
            else:
                start = h * 256 - rows
                stop = min(start + 256, halo)
                halo_ref[to, start:stop] = tile[:, : stop - start]


def build_kernel(index_ref, count_ref, importance_ref, own_ref, halo_ref, *, rows, halo):
    for first in range(0, own_ref.shape[0], 128):
        build_rows(index_ref, count_ref, importance_ref, own_ref, halo_ref, first, first, rows=rows, halo=halo)


def build_mixing(nbr_index, nbr_count, importance, halo):
    rows, fanout = nbr_index.shape
    block = 256
    return pl.pallas_call(
        functools.partial(build_kernel, rows=rows, halo=halo),
        grid=(rows // block,),
        in_specs=[
            pl.BlockSpec((fanout, block), lambda i: (0, i)),
            pl.BlockSpec((1, block), lambda i: (0, i)),
            pl.BlockSpec((fanout, block), lambda i: (0, i)),
        ],
        out_specs=[
            pl.BlockSpec((block, rows), lambda i: (i, 0)),
            pl.BlockSpec((block, halo), lambda i: (i, 0)),
        ],
        out_shape=[
            jax.ShapeDtypeStruct((rows, rows), BF),
            jax.ShapeDtypeStruct((rows, halo), BF),
        ],
        compiler_params=pltpu.CompilerParams(vmem_limit_bytes=40 * 2**20),
        name="build_mixing",
    )(nbr_index.T, nbr_count.reshape(1, rows), importance.T)


def gelu_pair(x):
    c = math.sqrt(2.0 / math.pi)
    square = x * x
    t = jnp.tanh(x * (c + (c * 0.044715) * square))
    half = 0.5 + 0.5 * t
    slope = x * (0.5 - 0.5 * t * t) * (c + (3.0 * c * 0.044715) * square)
    return x * half, half + slope


def hidden_rows(features_ref, q, bias, sent_rows, low_ref, neigh_ref, slope_ref, sent_ref, start):
    block, width = features_ref.shape
    at_rows = pl.ds(pl.multiple_of(start, block), block)
    low_ref[...] = features_ref[...].astype(BF)
    for c in range(0, width, 256):
        at = slice(c, c + 256)
        pre = jnp.dot(low_ref[...], q[:, at], preferred_element_type=F32) + bias[:, at]
        value, slope = gelu_pair(pre)
        neigh_ref[at_rows, at] = value.astype(BF)
        slope_ref[:, at] = slope.astype(BF)
    local = lax.broadcasted_iota(jnp.int32, (sent_rows.shape[0], block), 1) + start
    chosen = jnp.where(local == sent_rows, 1.0, 0.0).astype(BF)
    sent_ref[...] += jnp.dot(chosen, neigh_ref[at_rows, :], preferred_element_type=F32)


def ring_copies(groups, index, blocks_ref, landed_ref, send_sem, recv_sem, device_of):
    copies = []
    for k in range(1, groups):
        other = (index + k) % groups
        copies.append(
            pltpu.make_async_remote_copy(
                src_ref=blocks_ref.at[other],
                dst_ref=landed_ref.at[index],
                send_sem=send_sem.at[k - 1],
                recv_sem=recv_sem.at[k - 1],
                device_id=device_of(other),
                device_id_type=pl.DeviceIdType.MESH,
            )
        )
    return copies


def regroup(x, outer, inner, per):
    count = x.shape[0]
    to = lax.broadcasted_iota(jnp.int32, (count, count), 0)
    place = lax.broadcasted_iota(jnp.int32, (count, count), 1)
    source = ((to // per) % outer) * (inner * per) + (to // (per * outer)) * per + to % per
    chosen = jnp.where(place == source, 1.0, 0.0).astype(BF)
    return jnp.dot(chosen, x, preferred_element_type=F32).astype(BF)


def greet(comm, sub, comms, subs):
    barrier = pltpu.get_barrier_semaphore()
    for k in range(1, comms):
        pl.semaphore_signal(
            barrier, inc=1, device_id=((comm + k) % comms, sub), device_id_type=pl.DeviceIdType.MESH
        )
    for k in range(1, subs):
        pl.semaphore_signal(
            barrier, inc=1, device_id=(comm, (sub + k) % subs), device_id_type=pl.DeviceIdType.MESH
        )
    pl.semaphore_wait(barrier, comms + subs - 2)


def gather_kernel(
    index_ref,
    count_ref,
    importance_ref,
    features_ref,
    q_ref,
    w_ref,
    bias_ref,
    send_ref,
    own_out,
    halo_ref,
    low_ref,
    slope_ref,
    pooled_ref,
    incoming_ref,
    q_full,
    w_full,
    bias_out,
    own_mix,
    neigh,
    q_buf,
    w_own,
    bias_buf,
    sent_acc,
    sub_blocks,
    sub_landed,
    comm_blocks,
    comm_landed,
    local_sem,
    mix_sem,
    send_sem,
    recv_sem,
    sub_send,
    sub_recv,
    comm_send,
    comm_recv,
    *,
    comms,
    subs,
    bits,
    block,
    pool_block,
):
    i = pl.program_id(0)
    rows = own_mix.shape[0]
    halo = halo_ref.shape[1]
    width = neigh.shape[1]
    builds = rows // block
    hidden_end = 2 * builds
    steps = hidden_end + rows // pool_block
    comm, sub = lax.axis_index("comm"), lax.axis_index("sub")
    me = comm * subs + sub
    mine = [(me // (1 << b)) % 2 for b in range(bits)]
    order = list(range(bits))[::-1]

    def partner(b):
        other = me + (1 << b) * (1 - 2 * mine[b])
        return (other // subs, other % subs)

    def spot(done, part=slice(None), columns=slice(None)):
        lead = tuple(slice(None) if b in done else mine[b] for b in order)
        return lead + (part, columns)

    high = list(range(3, bits))[::-1]
    left, right = pl.ds(0, width // 2), pl.ds(width // 2, width // 2)
    count = [0]

    def exchange(buf, b, done, part=slice(None), columns=slice(None), source=None):
        at = buf.at[spot(done, part, columns)]
        n = count[0]
        count[0] += 1
        return pltpu.make_async_remote_copy(
            src_ref=at if source is None else source,
            dst_ref=at,
            send_sem=send_sem.at[n],
            recv_sem=recv_sem.at[n],
            device_id=partner(b),
            device_id_type=pl.DeviceIdType.MESH,
        )

    def chain(buf, own, split, part=slice(None)):
        groups = []
        done = []
        for b in high:
            groups.append([exchange(buf, b, done, part, source=own if not done else None)])
            done = done + [b]
        if split:
            groups.append([exchange(buf, 1, done, part, left), exchange(buf, 2, done, part, right)])
            groups.append(
                [exchange(buf, 2, done + [1], part, left), exchange(buf, 1, done + [2], part, right)]
            )
        else:
            groups.append([exchange(buf, 1, done)])
            groups.append([exchange(buf, 2, done + [1])])
        groups.append([exchange(buf, 0, done + [1, 2], part)])
        return groups

    w_rows = w_own.shape[0]
    top, bottom = pl.ds(0, w_rows // 2), pl.ds(w_rows // 2, w_rows // 2)
    chains = {
        "q": chain(q_buf, None, True),
        "bias": chain(bias_buf, None, False),
        "w0": chain(w_full, w_own.at[top], True, top),
        "w1": chain(w_full, w_own.at[bottom], True, bottom),
        "sub": [ring_copies(subs, sub, sub_blocks, sub_landed, sub_send, sub_recv, lambda j: (comm, j))],
        "comm": [ring_copies(comms, comm, comm_blocks, comm_landed, comm_send, comm_recv, lambda j: (j, sub))],
    }
    w_local = pltpu.make_async_copy(w_own, w_full.at[spot([])], local_sem.at[0])
    q_local = pltpu.make_async_copy(q_buf, q_full, local_sem.at[1])
    last = len(chains["q"]) - 1

    def mix_copy(step):
        at = pl.ds(pl.multiple_of(step * block, block), block)
        return pltpu.make_async_copy(own_mix.at[at, :], own_out.at[at, :], mix_sem)

    def begin(name, n):
        for c in chains[name][n]:
            c.start()

    def finish(name, n):
        for c in chains[name][n]:
            c.wait()

    def happen(part):
        for (step, at), names in events.items():
            if at == part:

                @pl.when(i == step)
                def _(names=names):
                    for name, n in names:
                        if n >= 0:
                            finish(name, n)
                        if n < last:
                            begin(name, n + 1)

    @pl.when(i == 0)
    def _():
        q_buf[spot([])] = q_ref[...].astype(BF)
        w_own[...] = w_ref[...].astype(BF)
        bias_buf[spot([])] = bias_ref[...]
        sent_acc[...] = jnp.zeros_like(sent_acc)
        w_local.start()
        greet(comm, sub, comms, subs)
        begin("q", 0)
        begin("bias", 0)
        w_local.wait()

    events = {
        (0, 1): [("w0", -1)],
        (2, 0): [("q", 0), ("bias", 0)],
        (3, 0): [("w0", 0), ("w1", -1)],
        (3, 1): [("q", 1), ("bias", 1)],
        (4, 1): [("w0", 1)],
        (5, 0): [("q", 2), ("bias", 2)],
        (5, 1): [("w1", 0)],
        (7, 0): [("w0", 2), ("w1", 1)],
        (8, 0): [("q", 3), ("bias", 3)],
        (builds + 2, 0): [("w0", 3)],
        (builds + 4, 0): [("w1", 2)],
        (hidden_end, 0): [("w0", 4)],
        (hidden_end + 1, 0): [("w1", 3)],
    }

    happen(0)
    for part in range(block // 128):
        if part == 1:
            happen(1)

        @pl.when(i < builds)
        def _(part=part):
            build_rows(
                index_ref,
                count_ref,
                importance_ref,
                own_mix,
                halo_ref,
                part * 128,
                i * block + part * 128,
                rows=rows,
                halo=halo,
            )

    @pl.when(i < builds)
    def _():
        mix_copy(i).start()

    @pl.when(i == builds)
    def _():
        finish("q", last)
        finish("bias", last)
        q_local.start()
        share = width >> bits
        for k in range(2):
            pieces = []
            for e in range(1 << bits):
                piece = bias_buf[tuple((e >> b) & 1 for b in order)]
                pieces.append(piece[0:1, k * share : (k + 1) * share])
            bias_out[k : k + 1, :] = jnp.concatenate(pieces, axis=1).astype(BF).astype(F32)
        bias_out[2:, :] = jnp.zeros((6, width), F32)

    @pl.when(jnp.logical_and(i >= builds, i < hidden_end))
    def _():
        mix_copy(i - builds).wait()
        q = q_buf[...].reshape(width, width)
        hidden_rows(
            features_ref,
            q,
            bias_out[0:1, :],
            send_ref[...],
            low_ref,
            neigh,
            slope_ref,
            sent_acc,
            (i - builds) * block,
        )

    @pl.when(i == hidden_end - 1)
    def _():
        sub_blocks[...] = sent_acc[...].astype(BF).reshape(sub_blocks.shape)
        begin("sub", 0)
        sub_landed[sub] = sub_blocks[sub]

    @pl.when(i == hidden_end + 2)
    def _():
        finish("sub", 0)
        moved = regroup(sub_landed[...].reshape(halo, width), subs, comms, halo // (subs * comms))
        comm_blocks[...] = moved.reshape(comm_blocks.shape)
        begin("comm", 0)
        comm_landed[comm] = comm_blocks[comm]

    @pl.when(i >= hidden_end)
    def _():
        at = pl.ds(pl.multiple_of((i - hidden_end) * pool_block, pool_block), pool_block)
        pooled_ref[...] = jnp.dot(own_mix[at, :], neigh[...], preferred_element_type=F32)

    @pl.when(i == steps - 1)
    def _():
        finish("w1", last)
        q_local.wait()
        finish("comm", 0)
        incoming_ref[...] = comm_landed[...].reshape(halo, width)


def gather_and_transform(features, q_weight, q_bias, w_weight, w_bias, nbr_index, nbr_count, importance, send_rows):
    comms, subs = lax.axis_size("comm"), lax.axis_size("sub")
    devices = comms * subs
    bits = devices.bit_length() - 1
    rows, width = features.shape
    fanout = nbr_index.shape[1]
    per = send_rows.shape[2]
    halo = devices * per
    block, pool_block = 256, 384
    builds = rows // block
    q_rows, w_rows = q_weight.shape[0], w_weight.shape[0]
    share = q_bias.shape[0]
    bias_tile = jnp.pad(jnp.concatenate([q_bias, w_bias])[None], ((0, 7), (0, 128 - 2 * share)))
    by_sub = send_rows.reshape(comms, subs, per).transpose(1, 0, 2).reshape(halo, 1)
    lead = (2,) * bits

    def built(i):
        return (jnp.minimum(i, builds - 1), 0)

    def built_columns(i):
        return (0, jnp.minimum(i, builds - 1))

    def later(i):
        return (jnp.clip(i - builds, 0, builds - 1), 0)

    def pooled_at(i):
        return (jnp.maximum(i - 2 * builds, 0), 0)

    def whole(*shape):
        return pl.BlockSpec(shape, lambda i: (0,) * len(shape))

    copies = 4 * bits + 3 * 2
    out = pl.pallas_call(
        functools.partial(
            gather_kernel, comms=comms, subs=subs, bits=bits, block=block, pool_block=pool_block
        ),
        grid=(2 * builds + rows // pool_block,),
        in_specs=[
            pl.BlockSpec((fanout, block), built_columns),
            pl.BlockSpec((1, block), built_columns),
            pl.BlockSpec((fanout, block), built_columns),
            pl.BlockSpec((block, width), later),
            whole(q_rows, width),
            whole(w_rows, width),
            whole(8, 128),
            whole(halo, 1),
        ],
        out_specs=[
            pl.BlockSpec(memory_space=pl.ANY),
            pl.BlockSpec((block, halo), built),
            pl.BlockSpec((block, width), later),
            pl.BlockSpec((block, width), later),
            pl.BlockSpec((pool_block, width), pooled_at),
            whole(halo, width),
            pl.BlockSpec(memory_space=pl.ANY),
            pl.BlockSpec(memory_space=pl.ANY),
            whole(8, width),
        ],
        out_shape=[
            jax.ShapeDtypeStruct((rows, rows), BF),
            jax.ShapeDtypeStruct((rows, halo), BF),
            jax.ShapeDtypeStruct((rows, width), BF),
            jax.ShapeDtypeStruct((rows, width), BF),
            jax.ShapeDtypeStruct((rows, width), F32),
            jax.ShapeDtypeStruct((halo, width), BF),
            jax.ShapeDtypeStruct(lead + (q_rows, width), BF),
            jax.ShapeDtypeStruct(lead + (w_rows, width), BF),
            jax.ShapeDtypeStruct((8, width), F32),
        ],
        scratch_shapes=[
            pltpu.VMEM((rows, rows), BF),
            pltpu.VMEM((rows, width), BF),
            pltpu.VMEM(lead + (q_rows, width), BF),
            pltpu.VMEM((w_rows, width), BF),
            pltpu.VMEM(lead + (8, 128), F32),
            pltpu.VMEM((halo, width), F32),
            pltpu.VMEM((subs, halo // subs, width), BF),
            pltpu.VMEM((subs, halo // subs, width), BF),
            pltpu.VMEM((comms, halo // comms, width), BF),
            pltpu.VMEM((comms, halo // comms, width), BF),
            pltpu.SemaphoreType.DMA((2,)),
            pltpu.SemaphoreType.DMA,
            pltpu.SemaphoreType.DMA((copies,)),
            pltpu.SemaphoreType.DMA((copies,)),
            pltpu.SemaphoreType.DMA((subs - 1,)),
            pltpu.SemaphoreType.DMA((subs - 1,)),
            pltpu.SemaphoreType.DMA((comms - 1,)),
            pltpu.SemaphoreType.DMA((comms - 1,)),
        ],
        compiler_params=pltpu.CompilerParams(
            collective_id=0, has_side_effects=True, vmem_limit_bytes=56 * 2**20
        ),
        name="gather_and_transform",
    )(
        nbr_index.T,
        nbr_count.reshape(1, rows),
        importance.T,
        features,
        q_weight,
        w_weight,
        bias_tile,
        by_sub,
    )
    own_mix, halo_mix, low, slope, pooled_own, incoming, q_full, w_full, biases = out
    return (
        own_mix,
        halo_mix,
        low,
        slope,
        pooled_own,
        incoming,
        q_full.reshape(devices * q_rows, width),
        w_full.reshape(devices * w_rows, width),
        biases[0],
        biases[1],
    )


def gather_plain(features, q_weight, q_bias, w_weight, w_bias, nbr_index, nbr_count, importance, send_rows):
    rows, width = features.shape
    devices, per_peer = send_rows.shape[1:]
    halo = devices * per_peer
    own_mix, halo_mix = build_mixing(nbr_index, nbr_count, importance, halo)
    q_full = lax.all_gather(q_weight.astype(BF), AXES, axis=0, tiled=True)
    w_full = lax.all_gather(w_weight.astype(BF), AXES, axis=0, tiled=True)
    biases = doubled(jnp.stack([q_bias, w_bias]), devices)
    qbias_full = biases[:, 0].reshape(width).astype(BF).astype(F32)
    wbias_full = biases[:, 1].reshape(width).astype(BF).astype(F32)
    low = features.astype(BF)
    neigh, slope = gelu_pair(jnp.dot(low, q_full, preferred_element_type=F32) + qbias_full)
    neigh = neigh.astype(BF)
    sent = neigh[send_rows[0]]
    incoming = lax.all_to_all(sent, AXES, split_axis=0, concat_axis=0, tiled=True).reshape(halo, width)
    pooled_own = pool_own(own_mix, neigh)
    return own_mix, halo_mix, low, slope.astype(BF), pooled_own, incoming, q_full, w_full, qbias_full, wbias_full


def resident(*shape):
    return pl.BlockSpec(shape, lambda i: (0,) * len(shape), pipeline_mode=pl.Buffered(1))


def by_rows(*shape):
    return pl.BlockSpec(shape, lambda i: (i,) + (0,) * (len(shape) - 1))


def product_kernel(mix_ref, table_ref, out_ref):
    out_ref[...] = jnp.dot(mix_ref[...], table_ref[...], preferred_element_type=F32)


def pool_own(own_mix, neigh):
    rows, width = neigh.shape
    block = 384
    return pl.pallas_call(
        product_kernel,
        grid=(rows // block,),
        in_specs=[by_rows(block, rows), resident(rows, width)],
        out_specs=by_rows(block, width),
        out_shape=jax.ShapeDtypeStruct((rows, width), F32),
        compiler_params=pltpu.CompilerParams(vmem_limit_bytes=40 * 2**20),
        cost_estimate=pl.CostEstimate(
            flops=2 * rows * rows * width, bytes_accessed=2 * rows * rows + 6 * rows * width, transcendentals=0
        ),
        name="pool_own",
    )(own_mix, neigh)


def combine_kernel(
    own_ref,
    halo_ref,
    incoming_ref,
    low_ref,
    w_ref,
    bias_ref,
    cotangent_ref,
    embedding_ref,
    pooled_ref,
    grad_ref,
    grad_pooled_ref,
    sent_ref,
    bias_grad_ref,
    act_buf,
    slope_buf,
):
    i = pl.program_id(0)
    block, width = low_ref.shape
    chunk = 256

    @pl.when(i == 0)
    def _():
        sent_ref[...] = jnp.zeros_like(sent_ref)
        bias_grad_ref[...] = jnp.zeros_like(bias_grad_ref)

    pooled = own_ref[...] + jnp.dot(halo_ref[...], incoming_ref[...], preferred_element_type=F32)
    pooled_ref[...] = pooled.astype(BF)
    squares = jnp.zeros((block, 128), F32)
    dots = jnp.zeros((block, 128), F32)
    for c in range(0, width, chunk):
        at = slice(c, c + chunk)
        pre = jnp.dot(low_ref[...], w_ref[:width, at], preferred_element_type=F32)
        pre += jnp.dot(pooled_ref[...], w_ref[width:, at], preferred_element_type=F32)
        act, slope = gelu_pair(pre + bias_ref[:, at])
        act_buf[:, at] = act
        slope_buf[:, at] = slope
        square = act * act
        dot = act * cotangent_ref[:, at]
        for k in range(0, chunk, 128):
            squares += square[:, k : k + 128]
            dots += dot[:, k : k + 128]
    scale = lax.rsqrt(jnp.sum(squares, axis=1, keepdims=True) * (1.0 / width) + 1e-06)
    pull = jnp.sum(dots, axis=1, keepdims=True) * (1.0 / width) * scale * scale * scale
    for c in range(0, width, chunk):
        at = slice(c, c + chunk)
        act = act_buf[:, at]
        embedding_ref[:, at] = act * scale
        grad = slope_buf[:, at] * (cotangent_ref[:, at] * scale - act * pull)
        grad_ref[:, at] = grad.astype(BF)
        bias_grad_ref[0:1, at] += jnp.sum(grad_ref[:, at].astype(F32), axis=0, keepdims=True)
    for c in range(0, width, chunk):
        at = slice(c, c + chunk)
        back = lax.dot_general(
            grad_ref[...],
            w_ref[width + c : width + c + chunk, :],
            (((1,), (1,)), ((), ())),
            preferred_element_type=F32,
        )
        grad_pooled_ref[:, at] = back.astype(BF)
    sent_ref[...] += lax.dot_general(
        halo_ref[...], grad_pooled_ref[...], (((0,), (0,)), ((), ())), preferred_element_type=F32
    )


def combine(pooled_own, halo_mix, incoming, low, w_full, w_bias, cotangent):
    rows, width = low.shape
    halo = incoming.shape[0]
    block = 256
    return pl.pallas_call(
        combine_kernel,
        grid=(rows // block,),
        in_specs=[
            by_rows(block, width),
            by_rows(block, halo),
            resident(halo, width),
            by_rows(block, width),
            resident(2 * width, width),
            resident(1, width),
            by_rows(block, width),
        ],
        out_specs=[
            by_rows(block, width),
            by_rows(block, width),
            by_rows(block, width),
            by_rows(block, width),
            pl.BlockSpec((halo, width), lambda i: (0, 0)),
            pl.BlockSpec((8, width), lambda i: (0, 0)),
        ],
        out_shape=[
            jax.ShapeDtypeStruct((rows, width), F32),
            jax.ShapeDtypeStruct((rows, width), BF),
            jax.ShapeDtypeStruct((rows, width), BF),
            jax.ShapeDtypeStruct((rows, width), BF),
            jax.ShapeDtypeStruct((halo, width), F32),
            jax.ShapeDtypeStruct((8, width), F32),
        ],
        scratch_shapes=[pltpu.VMEM((block, width), F32), pltpu.VMEM((block, width), F32)],
        compiler_params=pltpu.CompilerParams(vmem_limit_bytes=48 * 2**20),
        cost_estimate=pl.CostEstimate(
            flops=6 * rows * width * width, bytes_accessed=22 * rows * width, transcendentals=rows * width
        ),
        name="combine",
    )(pooled_own, halo_mix, incoming, low, w_full, w_bias.reshape(1, width), cotangent)


def swap(x, bit, devices):
    return lax.ppermute(x, AXES, [(i, i ^ (1 << bit)) for i in range(devices)])


def doubled(x, devices):
    me = lax.axis_index(AXES)
    x = x[None]
    for bit in range(devices.bit_length() - 1):
        other = swap(x, bit, devices)
        first = ((me >> bit) & 1) == 0
        x = jnp.where(first, jnp.concatenate([x, other]), jnp.concatenate([other, x]))
    return x


def summed(x, devices):
    for bit in range(devices.bit_length() - 1):
        x = x + swap(x, bit, devices)
    return x


def halve(part, left, bit, devices):
    mine = (lax.axis_index(AXES) >> bit) & 1
    axis = left.index(bit)
    keep = lax.dynamic_index_in_dim(part, mine, axis, keepdims=False)
    sent = lax.dynamic_index_in_dim(part, 1 - mine, axis, keepdims=False)
    total = keep.astype(F32) + swap(sent, bit, devices).astype(F32)
    return total, [b for b in left if b != bit]


def scatter_sum(partial, devices):
    bits = list(range(devices.bit_length() - 1))[::-1]
    width = partial.shape[1]
    part = partial.reshape([2] * len(bits) + [-1, width])
    part, left = halve(part, bits, 0, devices)
    part = part.astype(BF)
    rows = part.shape[-2] // 2
    orders = ([1, 2] + list(range(3, len(bits))), [2, 1] + list(range(3, len(bits))))
    halves = [(part[..., :rows, :], left), (part[..., rows:, :], left)]
    for step in range(len(bits) - 1):
        for s in range(2):
            total, rest = halve(halves[s][0], halves[s][1], orders[s][step], devices)
            halves[s] = (total if len(rest) == 0 else total.astype(BF), rest)
    return jnp.concatenate([h[0] for h in halves], axis=0)


def back_plain(
    own_mix, low, slope, pooled, grad_out, grad_pooled, sent_grad, grad_wbias, q_full, w_full, send_rows
):
    rows, width = low.shape
    devices, per = send_rows.shape[1:]
    contract = (((0,), (0,)), ((), ()))
    returned = lax.all_to_all(
        sent_grad.reshape(devices, per, width), AXES, split_axis=0, concat_axis=0, tiled=True
    )
    joined = jnp.concatenate([low, pooled], axis=1)
    grad_w = lax.dot_general(joined, grad_out, contract, preferred_element_type=F32)
    grad_low = lax.dot_general(grad_out, w_full[:width], (((1,), (1,)), ((), ())), preferred_element_type=F32)
    grad_neigh = lax.dot_general(own_mix, grad_pooled, contract, preferred_element_type=F32)
    grad_neigh = grad_neigh.at[send_rows.reshape(-1)].add(returned.reshape(devices * per, width))
    grad_hidden = (slope.astype(F32) * grad_neigh).astype(BF)
    grad_q = lax.dot_general(low, grad_hidden, contract, preferred_element_type=F32)
    grad_qbias = jnp.sum(grad_hidden.astype(F32), axis=0)
    grad_features = grad_low + lax.dot_general(
        grad_hidden, q_full, (((1,), (1,)), ((), ())), preferred_element_type=F32
    )
    me = lax.axis_index(AXES)
    share = width // devices
    sums = summed(jnp.stack([grad_qbias, grad_wbias[0]]), devices)
    sums = lax.dynamic_slice_in_dim(sums, me * share, share, 1)
    return (
        grad_features,
        scatter_sum(grad_q.astype(BF), devices),
        sums[0],
        scatter_sum(grad_w.astype(BF), devices),
        sums[1],
    )


class ScatterSum:
    def __init__(self, refs, orders, mine, partner):
        self.held, self.sent, self.got, self.next_sent, self.next_got, self.send_sem, self.recv_sem = refs
        self.orders, self.mine, self.partner = orders, mine, partner
        self.bits = len(mine)
        self.lead = list(range(1, self.bits))[::-1]
        self.half = self.held.shape[-1] // 2

    def copy(self, n, source, target, b):
        return pltpu.make_async_remote_copy(
            src_ref=source,
            dst_ref=target,
            send_sem=self.send_sem.at[n],
            recv_sem=self.recv_sem.at[n],
            device_id=self.partner(b),
            device_id_type=pl.DeviceIdType.MESH,
        )

    def first(self, top):
        return self.copy(top, self.sent.at[self.top_index(top)], self.got.at[self.top_index(top)], 0)

    def top_index(self, top):
        return ((top // 2) % 2, top % 2)

    def later(self, k):
        out = []
        for h in range(2):
            n = 4 + 2 * (k - 1) + h
            at = (h,) + (slice(self.offset(k), self.offset(k) + (1 << (self.bits - 1 - k))),)
            out.append(self.copy(n, self.next_sent.at[at], self.next_got.at[at], self.orders[h][k - 1]))
        return out

    def offset(self, k):
        return (1 << (self.bits - 1)) - (1 << (self.bits - k))

    def spot(self, chosen):
        return tuple(chosen[b] for b in self.lead)

    def absorb(self, k):
        for h in range(2):
            order = self.orders[h]
            fixed = order[:k]
            free = [b for b in self.lead if b not in fixed]
            columns = slice(h * self.half, (h + 1) * self.half)

            def total(chosen, h=h, free=free, columns=columns):
                at = self.spot(chosen)
                if k == 0:
                    came = self.got[at + (slice(None), columns)]
                else:
                    place = self.offset(k)
                    for p, b in enumerate(free[::-1]):
                        place = place + chosen[b] * (1 << p)
                    came = self.next_got[h, place]
                return at, self.held[at + (slice(None), columns)] + came.astype(F32)

            if not free:
                at, value = total({b: self.mine[b] for b in fixed})
                self.held[at + (slice(None), columns)] = value
                continue
            split = order[k]
            others = [b for b in free if b != split]

            def body(n, carry, total=total, split=split, others=others, fixed=fixed, columns=columns, h=h):
                chosen = {b: self.mine[b] for b in fixed}
                for p, b in enumerate(others[::-1]):
                    chosen[b] = (n // (1 << p)) % 2
                chosen[split] = self.mine[split]
                at, value = total(chosen)
                self.held[at + (slice(None), columns)] = value
                chosen[split] = 1 - self.mine[split]
                _, value = total(chosen)
                self.next_sent[h, self.offset(k + 1) + n] = value.astype(BF)
                return carry

            lax.fori_loop(0, 1 << len(others), body, 0)

    def start(self, k):
        for c in self.later(k):
            c.start()

    def wait(self, k):
        for c in [self.first(t) for t in range(4)] if k == 0 else self.later(k):
            c.wait()

    def result(self):
        return self.held[self.spot({b: self.mine[b] for b in self.lead})]


def back_body(
    mix_ref,
    slope_ref,
    sent_grad_ref,
    w_bias_ref,
    target_ref,
    low_hbm,
    pooled_hbm,
    out_hbm,
    grad_pooled_hbm,
    w_hbm,
    q_hbm,
    features_ref,
    q_out,
    w_out,
    bias_out,
    joined,
    grad_out,
    grad_pooled,
    w_top,
    q_full,
    q_bias_acc,
    bias_sent,
    bias_got,
    comm_blocks,
    comm_landed,
    sub_blocks,
    sub_landed,
    *rest,
    comms,
    subs,
    bits,
    mix_block,
    row_block,
):
    sets = [rest[7 * k : 7 * k + 7] for k in range(3)]
    load_sem, bias_send, bias_recv, comm_send, comm_recv, sub_send, sub_recv = rest[21:]
    i = pl.program_id(0)
    rows, width = grad_out.shape
    halo = sent_grad_ref.shape[0]
    half = width // 2
    comm, sub = lax.axis_index("comm"), lax.axis_index("sub")
    me = comm * subs + sub
    mine = [(me // (1 << b)) % 2 for b in range(bits)]
    tn = (((0,), (0,)), ((), ()))
    nt = (((1,), (1,)), ((), ()))

    def partner(b):
        other = me + (1 << b) * (1 - 2 * mine[b])
        return (other // subs, other % subs)

    high = list(range(3, bits))
    orders = ([1, 2] + high, [2, 1] + high)
    w_sets = [ScatterSum(sets[k], orders, mine, partner) for k in range(2)]
    q_set = ScatterSum(sets[2], orders, mine, partner)

    left, right = pl.ds(0, half), pl.ds(half, half)
    loads = [
        (out_hbm.at[:, left], grad_out.at[:, left]),
        (low_hbm.at[:, left], joined.at[:, pl.ds(0, half)]),
        (low_hbm.at[:, right], joined.at[:, pl.ds(half, half)]),
        (pooled_hbm.at[:, left], joined.at[:, pl.ds(2 * half, half)]),
        (pooled_hbm.at[:, right], joined.at[:, pl.ds(3 * half, half)]),
        (out_hbm.at[:, right], grad_out.at[:, right]),
        (grad_pooled_hbm, grad_pooled),
        (w_hbm.at[pl.ds(0, width), :], w_top),
        (q_hbm, q_full),
    ]
    loads = [pltpu.make_async_copy(a, b, load_sem.at[n]) for n, (a, b) in enumerate(loads)]
    comm_ring = ring_copies(comms, comm, comm_blocks, comm_landed, comm_send, comm_recv, lambda j: (j, sub))
    sub_ring = ring_copies(subs, sub, sub_blocks, sub_landed, sub_send, sub_recv, lambda j: (comm, j))
    bias_copies = [
        pltpu.make_async_remote_copy(
            src_ref=bias_sent.at[b],
            dst_ref=bias_got.at[b],
            send_sem=bias_send.at[b],
            recv_sem=bias_recv.at[b],
            device_id=partner(b),
            device_id_type=pl.DeviceIdType.MESH,
        )
        for b in range(bits)
    ]

    products = 8
    spreads = rows // mix_block
    spread_end = products + spreads
    q_end = spread_end + 4
    steps = q_end + rows // row_block

    def load_wait(step, which):
        @pl.when(i == step)
        def _():
            for n in which:
                loads[n].wait()

    @pl.when(i == 0)
    def _():
        for c in loads:
            c.start()
        greet(comm, sub, comms, subs)
        comm_blocks[...] = sent_grad_ref[...].astype(BF).reshape(comm_blocks.shape)
        for c in comm_ring:
            c.start()
        comm_landed[comm] = comm_blocks[comm]
        q_bias_acc[...] = jnp.zeros_like(q_bias_acc)

    load_wait(0, [0, 1])
    load_wait(1, [2])
    load_wait(2, [3])
    load_wait(3, [4])
    load_wait(4, [5])
    load_wait(products, [6])
    load_wait(q_end, [7, 8])

    @pl.when(i == 2)
    def _():
        for c in comm_ring:
            c.wait()
        moved = regroup(comm_landed[...].reshape(halo, width), comms, subs, halo // (subs * comms))
        sub_blocks[...] = moved.reshape(sub_blocks.shape)
        for c in sub_ring:
            c.start()
        sub_landed[sub] = sub_blocks[sub]

    def step_of(which, k):
        which.wait(k)
        which.absorb(k)
        if k < bits - 1:
            which.start(k + 1)

    def deal(value, which, top, rows_each):
        keep_even = mine[0] == 0
        shares = value.shape[0] // rows_each
        for p in range(shares // 2):
            even = value[2 * p * rows_each : (2 * p + 1) * rows_each]
            odd = value[(2 * p + 1) * rows_each : (2 * p + 2) * rows_each]
            at = top + tuple((p >> b) & 1 for b in range(bits - 2, -1, -1))[len(top) :]
            which.held[at] = jnp.where(keep_even, even, odd)
            which.sent[at] = jnp.where(keep_even, odd, even).astype(BF)

    def w_top_bits(j):
        return ((j // 2) % 2, j % 2)

    for n in range(2):

        @pl.when(jnp.logical_and(i >= 4 * n, i < 4 * n + 4))
        def _(n=n):
            j = i - 4 * n
            at = pl.ds(pl.multiple_of(j * half, half), half)
            columns = slice(n * half, (n + 1) * half)
            value = lax.dot_general(joined[:, at], grad_out[:, columns], tn, preferred_element_type=F32)
            deal(value, w_sets[n], w_top_bits(j), w_out.shape[0])
            for t in range(4):

                @pl.when(j == t)
                def _(t=t):
                    w_sets[n].first(t).start()

    events = {
        5: [(0, 0)],
        products + 1: [(1, 0), (0, 1)],
        products + 3: [(0, 2)],
        products + 4: [(1, 1)],
        products + 5: [(0, 3)],
        spread_end + 1: [(1, 2), (0, 4)],
        spread_end + 3: [(1, 3)],
        q_end + 1: [(1, 4)],
    }
    for step, which in events.items():

        @pl.when(i == step)
        def _(which=which):
            for n, k in which:
                step_of(w_sets[n], k)

    @pl.when(i == products)
    def _():
        for c in sub_ring:
            c.wait()

    @pl.when(jnp.logical_and(i >= products, i < spread_end))
    def _():
        start = (i - products) * mix_block
        local = lax.broadcasted_iota(jnp.int32, (mix_block, halo), 0) + start
        chosen = jnp.where(local == target_ref[...], 1.0, 0.0).astype(BF)
        back = lax.dot_general(mix_ref[...], grad_pooled[...], tn, preferred_element_type=F32)
        back += jnp.dot(chosen, sub_landed[...].reshape(halo, width), preferred_element_type=F32)
        grad = (back * slope_ref[...].astype(F32)).astype(BF)
        joined[pl.ds(pl.multiple_of(start, 128), mix_block), width:] = grad
        q_bias_acc[0:1, :] += jnp.sum(grad.astype(F32), axis=0, keepdims=True)

    @pl.when(jnp.logical_and(i >= spread_end, i < q_end))
    def _():
        for t in range(4):

            @pl.when(i == spread_end + t)
            def _(t=t):
                n, j = t % 2, t // 2
                value = lax.dot_general(
                    joined[:, j * half : (j + 1) * half],
                    joined[:, width + n * half : width + (n + 1) * half],
                    tn,
                    preferred_element_type=F32,
                )
                keep_even = mine[0] == 0
                columns = slice(n * half, (n + 1) * half)
                each = q_out.shape[0]
                for p in range(half // each // 2):
                    even = value[2 * p * each : (2 * p + 1) * each]
                    odd = value[(2 * p + 1) * each : (2 * p + 2) * each]
                    at = (j, (p >> 2) & 1, (p >> 1) & 1, p & 1, slice(None), columns)
                    q_set.held[at] = jnp.where(keep_even, even, odd)
                    q_set.sent[at] = jnp.where(keep_even, odd, even).astype(BF)
                if n == 1:
                    q_set.first(2 * j).start()
                    q_set.first(2 * j + 1).start()

    def bias_step(b):
        if b:
            bias_copies[b - 1].wait()
            total = bias_sent[b - 1] + bias_got[b - 1]
            if b == bits:
                bias_out[...] = total
                return
            bias_sent[b] = total
        bias_copies[b].start()

    @pl.when(i == spread_end)
    def _():
        pieces = [w_bias_ref[0:1, c : c + 128] for c in range(0, width, 128)]
        pieces += [q_bias_acc[0:1, c : c + 128] for c in range(0, width, 128)]
        bias_sent[0] = jnp.concatenate(pieces, axis=0)

    for b in range(bits):

        @pl.when(i == spread_end + b)
        def _(b=b):
            bias_step(b)

    q_events = {q_end + 1: 0, q_end + 4: 1}
    for step, k in q_events.items():

        @pl.when(i == step)
        def _(k=k):
            step_of(q_set, k)

    @pl.when(i >= q_end)
    def _():
        at = pl.ds(pl.multiple_of((i - q_end) * row_block, 128), row_block)
        value = lax.dot_general(grad_out[at, :], w_top[...], nt, preferred_element_type=F32)
        features_ref[...] = value + lax.dot_general(
            joined[at, width:], q_full[...], nt, preferred_element_type=F32
        )

    @pl.when(i == steps - 1)
    def _():
        for k in range(2, bits):
            step_of(q_set, k)
        for n in range(2):
            w_out[:, n * half : (n + 1) * half] = w_sets[n].result()
        q_out[...] = q_set.result()
        bias_step(bits)


def back_kernel(
    own_mix, low, slope, pooled, grad_out, grad_pooled, sent_grad, grad_wbias, q_full, w_full, send_rows
):
    comms, subs = lax.axis_size("comm"), lax.axis_size("sub")
    devices = comms * subs
    bits = devices.bit_length() - 1
    rows, width = low.shape
    per = send_rows.shape[2]
    halo = devices * per
    mix_block, row_block = 384, 384
    spreads = rows // mix_block
    spread_end = 8 + spreads
    q_end = spread_end + 4
    w_rows, q_rows = w_full.shape[0] // devices, q_full.shape[0] // devices
    targets = send_rows.reshape(comms, subs, per).transpose(1, 0, 2).reshape(1, halo)
    lead = (2,) * (bits - 1)

    def set_scratch(rows_each, columns):
        chunks = (1 << (bits - 1)) - 1
        copies = 4 + 2 * (bits - 1)
        return [
            pltpu.VMEM(lead + (rows_each, columns), F32),
            pltpu.VMEM(lead + (rows_each, columns), BF),
            pltpu.VMEM(lead + (rows_each, columns), BF),
            pltpu.VMEM((2, chunks, rows_each, columns // 2), BF),
            pltpu.VMEM((2, chunks, rows_each, columns // 2), BF),
            pltpu.SemaphoreType.DMA((copies,)),
            pltpu.SemaphoreType.DMA((copies,)),
        ]

    def spread_columns(i):
        return (0, jnp.clip(i - 8, 0, spreads - 1))

    def spread_rows(i):
        return (jnp.clip(i - 8, 0, spreads - 1), 0)

    def whole(*shape):
        return pl.BlockSpec(shape, lambda i: (0,) * len(shape), pipeline_mode=pl.Buffered(1))

    def whole_out(*shape):
        return pl.BlockSpec(shape, lambda i: (0,) * len(shape))

    anywhere = pl.BlockSpec(memory_space=pl.ANY)
    grad_features, grad_q, grad_w, biases = pl.pallas_call(
        functools.partial(
            back_body, comms=comms, subs=subs, bits=bits, mix_block=mix_block, row_block=row_block
        ),
        grid=(q_end + rows // row_block,),
        in_specs=[
            pl.BlockSpec((rows, mix_block), spread_columns),
            pl.BlockSpec((mix_block, width), spread_rows),
            whole(halo, width),
            whole(8, width),
            whole(1, halo),
        ]
        + [anywhere] * 6,
        out_specs=[
            pl.BlockSpec((row_block, width), lambda i: (jnp.maximum(i - q_end, 0), 0)),
            whole_out(q_rows, width),
            whole_out(w_rows, width),
            whole_out(16, 128),
        ],
        out_shape=[
            jax.ShapeDtypeStruct((rows, width), F32),
            jax.ShapeDtypeStruct((q_rows, width), F32),
            jax.ShapeDtypeStruct((w_rows, width), F32),
            jax.ShapeDtypeStruct((16, 128), F32),
        ],
        scratch_shapes=[
            pltpu.VMEM((rows, 2 * width), BF),
            pltpu.VMEM((rows, width), BF),
            pltpu.VMEM((rows, width), BF),
            pltpu.VMEM((width, width), BF),
            pltpu.VMEM((width, width), BF),
            pltpu.VMEM((8, width), F32),
            pltpu.VMEM((bits, 16, 128), F32),
            pltpu.VMEM((bits, 16, 128), F32),
            pltpu.VMEM((comms, halo // comms, width), BF),
            pltpu.VMEM((comms, halo // comms, width), BF),
            pltpu.VMEM((subs, halo // subs, width), BF),
            pltpu.VMEM((subs, halo // subs, width), BF),
        ]
        + set_scratch(w_rows, width // 2)
        + set_scratch(w_rows, width // 2)
        + set_scratch(q_rows, width)
        + [
            pltpu.SemaphoreType.DMA((9,)),
            pltpu.SemaphoreType.DMA((bits,)),
            pltpu.SemaphoreType.DMA((bits,)),
            pltpu.SemaphoreType.DMA((comms - 1,)),
            pltpu.SemaphoreType.DMA((comms - 1,)),
            pltpu.SemaphoreType.DMA((subs - 1,)),
            pltpu.SemaphoreType.DMA((subs - 1,)),
        ],
        compiler_params=pltpu.CompilerParams(
            collective_id=1, has_side_effects=True, vmem_limit_bytes=62 * 2**20
        ),
        name="back",
    )(own_mix, slope, sent_grad, grad_wbias, targets, low, pooled, grad_out, grad_pooled, w_full, q_full)
    share = width // devices
    sums = lax.dynamic_slice_in_dim(biases.reshape(2, width), lax.axis_index(AXES) * share, share, 1)
    return grad_features, grad_q, sums[1], grad_w, sums[0]


def shards(
    features,
    q_weight,
    q_bias,
    w_weight,
    w_bias,
    nbr_index,
    nbr_count,
    importance,
    send_rows,
    cotangent,
):
    devices = lax.axis_size(AXES)
    kernel_fits = devices == 32 and q_weight.shape[0] % 16 == 0
    gather, back = (gather_and_transform, back_kernel) if kernel_fits else (gather_plain, back_plain)
    own_mix, halo_mix, low, slope, pooled_own, incoming, q_full, w_full, qbias_full, wbias_full = gather(
        features, q_weight, q_bias, w_weight, w_bias, nbr_index, nbr_count, importance, send_rows
    )
    embedding, pooled, grad_out, grad_pooled, sent_grad, grad_wbias = combine(
        pooled_own, halo_mix, incoming, low, w_full, wbias_full, cotangent
    )
    grad_features, grad_q, grad_qbias, grad_w, grad_wbias = back(
        own_mix, low, slope, pooled, grad_out, grad_pooled, sent_grad, grad_wbias, q_full, w_full, send_rows
    )
    return embedding, grad_features, grad_q, grad_qbias, grad_w, grad_wbias


def solution(mesh):
    in_specs = (
        P(("comm", "sub"), None),
        P(("comm", "sub"), None),
        P(("comm", "sub")),
        P(("comm", "sub"), None),
        P(("comm", "sub")),
        P(("comm", "sub"), None),
        P(("comm", "sub")),
        P(("comm", "sub"), None),
        P(("comm", "sub"), None, None),
        P(("comm", "sub"), None),
    )
    out_specs = (
        P(("comm", "sub"), None),
        P(("comm", "sub"), None),
        P(("comm", "sub"), None),
        P(("comm", "sub")),
        P(("comm", "sub"), None),
        P(("comm", "sub")),
    )
    return jax.shard_map(shards, mesh=mesh, in_specs=in_specs, out_specs=out_specs, check_vma=False)
```

```python
import functools
import math

import jax
import jax.numpy as jnp
from jax import lax
from jax.experimental import pallas as pl
from jax.experimental.pallas import tpu as pltpu
from jax.sharding import PartitionSpec as P

BF = jnp.bfloat16
F32 = jnp.float32
AXES = ("comm", "sub")


def build_rows(index_ref, count_ref, importance_ref, own_ref, halo_ref, first, *, rows, halo):
    his = (rows + halo + 255) // 256
    pairs = (his + 1) // 2
    fanout = index_ref.shape[0]
    at = pl.ds(pl.multiple_of(first, 128), 128)
    lane = lax.broadcasted_iota(jnp.int32, (16, 128), 1)
    sublane = lax.broadcasted_iota(jnp.int32, (16, 128), 0)
    parity = (sublane >= 8).astype(jnp.int32)
    half = (lane >= 64).astype(jnp.int32)
    los = lax.broadcasted_iota(jnp.int32, (64, 256), 1).astype(BF)
    left = lax.broadcasted_iota(jnp.int32, (1, 128), 1) < 64
    hi_pattern = [(2 * t + parity).astype(BF) for t in range(pairs)]
    row_mask = [(sublane & 7) == 2 * c + half for c in range(4)]
    zero = jnp.zeros((), BF)
    one = jnp.ones((), BF)

    def slots(x):
        return jnp.concatenate([x, jnp.zeros((64 - fanout, 128), F32)], axis=0)

    def by_row(x):
        x = slots(x).T
        return jnp.concatenate([x, x], axis=1)

    index = index_ref[:, at]
    slot = lax.broadcasted_iota(jnp.int32, index.shape, 0)
    weight = jnp.where(slot < count_ref[:, at], importance_ref[:, at], 0.0)
    alpha = by_row(weight / jnp.sum(weight, axis=0, keepdims=True))
    hi = by_row((index >> 8).astype(F32))
    lo = slots((index & 255).astype(F32)).astype(BF)
    for g in range(0, 128, 16):
        tiles = []
        for s in range(2):
            left_parts, right_parts = [], []
            for c in range(4):
                r = g + s * 8 + 2 * c

                def pick(x):
                    return jnp.where(left, x[r : r + 1, :], x[r + 1 : r + 2, :]).astype(BF)

                kept = jnp.where(row_mask[c], jnp.broadcast_to(pick(alpha), (16, 128)), zero)
                hi_row = jnp.broadcast_to(pick(hi), (16, 128))
                left_parts.append(
                    jnp.concatenate(
                        [jnp.where(hi_row == hi_pattern[t], kept, zero) for t in range(pairs)], axis=0
                    )
                )
                for q in (r, r + 1):
                    right_parts.append(jnp.where(jnp.broadcast_to(lo[:, q : q + 1], (64, 256)) == los, one, zero))
            tiles.append(
                jnp.dot(
                    jnp.concatenate(left_parts, axis=1),
                    jnp.concatenate(right_parts, axis=0),
                    preferred_element_type=F32,
                )
            )
        for h in range(his):
            tile = jnp.concatenate([t[h * 8 : (h + 1) * 8, :] for t in tiles], axis=0).astype(BF)
            to = pl.ds(pl.multiple_of(first + g, 16), 16)
            if h * 256 < rows:
                own_ref[to, h * 256 : (h + 1) * 256] = tile
            else:
                start = h * 256 - rows
                stop = min(start + 256, halo)
                halo_ref[to, start:stop] = tile[:, : stop - start]


def build_kernel(index_ref, count_ref, importance_ref, own_ref, halo_ref, *, rows, halo):
    for first in range(0, own_ref.shape[0], 128):
        build_rows(index_ref, count_ref, importance_ref, own_ref, halo_ref, first, rows=rows, halo=halo)


def build_mixing(nbr_index, nbr_count, importance, halo):
    rows, fanout = nbr_index.shape
    block = 256
    return pl.pallas_call(
        functools.partial(build_kernel, rows=rows, halo=halo),
        grid=(rows // block,),
        in_specs=[
            pl.BlockSpec((fanout, block), lambda i: (0, i)),
            pl.BlockSpec((1, block), lambda i: (0, i)),
            pl.BlockSpec((fanout, block), lambda i: (0, i)),
        ],
        out_specs=[
            pl.BlockSpec((block, rows), lambda i: (i, 0)),
            pl.BlockSpec((block, halo), lambda i: (i, 0)),
        ],
        out_shape=[
            jax.ShapeDtypeStruct((rows, rows), BF),
            jax.ShapeDtypeStruct((rows, halo), BF),
        ],
        compiler_params=pltpu.CompilerParams(vmem_limit_bytes=40 * 2**20),
        name="build_mixing",
    )(nbr_index.T, nbr_count.reshape(1, rows), importance.T)


def gelu_pair(x):
    c = math.sqrt(2.0 / math.pi)
    square = x * x
    t = jnp.tanh(x * (c + (c * 0.044715) * square))
    half = 0.5 + 0.5 * t
    slope = x * (0.5 - 0.5 * t * t) * (c + (3.0 * c * 0.044715) * square)
    return x * half, half + slope


def hidden_rows(features_ref, q_buf, bias_ref, send_ref, low_ref, neigh_ref, slope_ref, sent_ref, at_rows, start):
    width = features_ref.shape[1]
    lead = (slice(None),) * (len(q_buf.shape) - 1)
    low_ref[at_rows, :] = features_ref[at_rows, :].astype(BF)
    for c in range(0, width, 256):
        at = slice(c, c + 256)
        q = q_buf[lead + (at,)].reshape(width, 256)
        pre = jnp.dot(low_ref[at_rows, :], q, preferred_element_type=F32) + bias_ref[0:1, at]
        value, slope = gelu_pair(pre)
        neigh_ref[at_rows, at] = value.astype(BF)
        slope_ref[at_rows, at] = slope.astype(BF)
    neigh = neigh_ref[at_rows, :]
    local = lax.broadcasted_iota(jnp.int32, (send_ref.shape[0], neigh.shape[0]), 1) + start
    chosen = jnp.where(local == send_ref[...], 1.0, 0.0).astype(BF)
    sent_ref[...] += jnp.dot(chosen, neigh, preferred_element_type=F32)


def ring_copies(groups, index, blocks_ref, landed_ref, send_sem, recv_sem, device_of):
    copies = []
    for k in range(1, groups):
        other = (index + k) % groups
        copies.append(
            pltpu.make_async_remote_copy(
                src_ref=blocks_ref.at[other],
                dst_ref=landed_ref.at[index],
                send_sem=send_sem.at[k - 1],
                recv_sem=recv_sem.at[k - 1],
                device_id=device_of(other),
                device_id_type=pl.DeviceIdType.MESH,
            )
        )
    return copies


def regroup(x, outer, inner, per):
    count = x.shape[0]
    to = lax.broadcasted_iota(jnp.int32, (count, count), 0)
    place = lax.broadcasted_iota(jnp.int32, (count, count), 1)
    source = ((to // per) % outer) * (inner * per) + (to // (per * outer)) * per + to % per
    chosen = jnp.where(place == source, 1.0, 0.0).astype(BF)
    return jnp.dot(chosen, x, preferred_element_type=F32).astype(BF)


def greet(comm, sub, comms, subs):
    barrier = pltpu.get_barrier_semaphore()
    for k in range(1, comms):
        pl.semaphore_signal(
            barrier, inc=1, device_id=((comm + k) % comms, sub), device_id_type=pl.DeviceIdType.MESH
        )
    for k in range(1, subs):
        pl.semaphore_signal(
            barrier, inc=1, device_id=(comm, (sub + k) % subs), device_id_type=pl.DeviceIdType.MESH
        )
    pl.semaphore_wait(barrier, comms + subs - 2)


def gather_kernel(
    index_ref,
    count_ref,
    importance_ref,
    q_ref,
    w_ref,
    bias_ref,
    send_ref,
    features_hbm,
    own_out,
    halo_ref,
    low_out,
    slope_out,
    pooled_out,
    incoming_ref,
    q_full,
    w_full,
    bias_out,
    features,
    own_mix,
    low,
    neigh,
    slope,
    pooled,
    q_buf,
    w_own,
    bias_buf,
    sent_acc,
    sub_blocks,
    sub_landed,
    comm_blocks,
    comm_landed,
    local_sem,
    feature_sem,
    send_sem,
    recv_sem,
    sub_send,
    sub_recv,
    comm_send,
    comm_recv,
    *,
    comms,
    subs,
    bits,
    block,
    pool_block,
):
    rows = own_mix.shape[0]
    halo = halo_ref.shape[1]
    width = neigh.shape[1]
    comm, sub = lax.axis_index("comm"), lax.axis_index("sub")
    me = comm * subs + sub
    mine = [(me // (1 << b)) % 2 for b in range(bits)]
    order = list(range(bits))[::-1]

    def partner(b):
        other = me + (1 << b) * (1 - 2 * mine[b])
        return (other // subs, other % subs)

    def spot(done, part=slice(None), columns=slice(None)):
        lead = tuple(slice(None) if b in done else mine[b] for b in order)
        return lead + (part, columns)

    high = list(range(3, bits))[::-1]
    left, right = pl.ds(0, width // 2), pl.ds(width // 2, width // 2)
    count = [0]

    def exchange(buf, b, done, part=slice(None), columns=slice(None), source=None):
        at = buf.at[spot(done, part, columns)]
        n = count[0]
        count[0] += 1
        return pltpu.make_async_remote_copy(
            src_ref=at if source is None else source,
            dst_ref=at,
            send_sem=send_sem.at[n],
            recv_sem=recv_sem.at[n],
            device_id=partner(b),
            device_id_type=pl.DeviceIdType.MESH,
        )

    def chain(buf, own, split, part=slice(None)):
        groups = []
        done = []
        for b in high:
            groups.append([exchange(buf, b, done, part, source=own if not done else None)])
            done = done + [b]
        if split:
            groups.append([exchange(buf, 1, done, part, left), exchange(buf, 2, done, part, right)])
            groups.append(
                [exchange(buf, 2, done + [1], part, left), exchange(buf, 1, done + [2], part, right)]
            )
        else:
            groups.append([exchange(buf, 1, done)])
            groups.append([exchange(buf, 2, done + [1])])
        groups.append([exchange(buf, 0, done + [1, 2], part)])
        return groups

    w_rows = w_own.shape[0]
    top, bottom = pl.ds(0, w_rows // 2), pl.ds(w_rows // 2, w_rows // 2)
    chains = {
        "q": chain(q_buf, None, True),
        "bias": chain(bias_buf, None, False),
        "w0": chain(w_full, w_own.at[top], True, top),
        "w1": chain(w_full, w_own.at[bottom], True, bottom),
        "sub": [ring_copies(subs, sub, sub_blocks, sub_landed, sub_send, sub_recv, lambda j: (comm, j))],
        "comm": [ring_copies(comms, comm, comm_blocks, comm_landed, comm_send, comm_recv, lambda j: (j, sub))],
    }
    w_local = pltpu.make_async_copy(w_own, w_full.at[spot([])], local_sem.at[0])
    q_local = pltpu.make_async_copy(q_buf, q_full, local_sem.at[1])
    last = len(chains["q"]) - 1

    def begin(name, n):
        for c in chains[name][n]:
            c.start()

    def finish(name, n):
        for c in chains[name][n]:
            c.wait()

    def place(n, size):
        return pl.ds(pl.multiple_of(n * size, size), size)

    def feature_copy(n):
        at = place(n, block)
        return pltpu.make_async_copy(features_hbm.at[at, :], features.at[at, :], feature_sem.at[n])

    outs = [(own_mix, own_out), (low, low_out), (slope, slope_out), (pooled, pooled_out)]

    def give(n, at):
        source, target = outs[n]
        pltpu.make_async_copy(source.at[at, :], target.at[at, :], local_sem.at[2 + n]).start()

    def given(n):
        pltpu.make_async_copy(*outs[n], local_sem.at[2 + n]).wait()

    events = {
        ("build", 4): [("q", 0), ("bias", 0)],
        ("build", 6): [("w0", -1)],
        ("build", 7): [("q", 1), ("bias", 1)],
        ("build", 9): [("w1", -1)],
        ("build", 10): [("q", 2), ("bias", 2), ("w0", 0)],
        ("build", 13): [("w1", 0)],
        ("build", 14): [("w0", 1)],
        ("build", 15): [("q", 3), ("bias", 3)],
        ("hidden", 0): [("w1", 1)],
        ("hidden", 1): [("w0", 2)],
        ("hidden", 6): [("w0", 3), ("w1", 2)],
        ("pool", 2): [("w1", 3)],
    }

    def happen(phase, n):
        for (when, step), names in events.items():
            if when == phase:

                @pl.when(n == step)
                def _(names=names):
                    for name, k in names:
                        if k >= 0:
                            finish(name, k)
                        begin(name, k + 1)

    q_buf[spot([])] = q_ref[...].astype(BF)
    w_own[...] = w_ref[...].astype(BF)
    bias_buf[spot([])] = bias_ref[...]
    greet(comm, sub, comms, subs)
    begin("q", 0)
    begin("bias", 0)
    w_local.start()
    sent_acc[...] = jnp.zeros_like(sent_acc)
    w_local.wait()

    @pl.loop(0, rows // block)
    def _(n):
        feature_copy(n).start()

    @pl.loop(0, rows // 128)
    def _(n):
        happen("build", n)
        build_rows(
            index_ref, count_ref, importance_ref, own_mix, halo_ref, n * 128, rows=rows, halo=halo
        )
        give(0, place(n, 128))

    finish("q", last)
    finish("bias", last)
    q_local.start()
    share = width >> bits
    for k in range(2):
        pieces = []
        for e in range(1 << bits):
            piece = bias_buf[tuple((e >> b) & 1 for b in order)]
            pieces.append(piece[0:1, k * share : (k + 1) * share])
        bias_out[k : k + 1, :] = jnp.concatenate(pieces, axis=1).astype(BF).astype(F32)
    bias_out[2:, :] = jnp.zeros((6, width), F32)

    @pl.loop(0, rows // block)
    def _(n):
        happen("hidden", n)
        feature_copy(n).wait()
        at = place(n, block)
        hidden_rows(features, q_buf, bias_out, send_ref, low, neigh, slope, sent_acc, at, n * block)
        give(1, at)
        give(2, at)

    sub_blocks[...] = sent_acc[...].astype(BF).reshape(sub_blocks.shape)
    begin("sub", 0)
    sub_landed[sub] = sub_blocks[sub]

    @pl.loop(0, rows // pool_block)
    def _(n):
        happen("pool", n)

        @pl.when(n == 2)
        def _():
            finish("sub", 0)
            moved = regroup(sub_landed[...].reshape(halo, width), subs, comms, halo // (subs * comms))
            comm_blocks[...] = moved.reshape(comm_blocks.shape)
            begin("comm", 0)
            comm_landed[comm] = comm_blocks[comm]

        at = place(n, pool_block)
        pooled[at, :] = jnp.dot(own_mix[at, :], neigh[...], preferred_element_type=F32)
        give(3, at)

    finish("w0", last)
    finish("w1", last)
    finish("comm", 0)
    incoming_ref[...] = comm_landed[...].reshape(halo, width)
    q_local.wait()
    for n in range(4):
        given(n)


def gather_and_transform(features, q_weight, q_bias, w_weight, w_bias, nbr_index, nbr_count, importance, send_rows):
    comms, subs = lax.axis_size("comm"), lax.axis_size("sub")
    devices = comms * subs
    bits = devices.bit_length() - 1
    rows, width = features.shape
    fanout = nbr_index.shape[1]
    per = send_rows.shape[2]
    halo = devices * per
    block, pool_block = 256, 384
    q_rows, w_rows = q_weight.shape[0], w_weight.shape[0]
    share = q_bias.shape[0]
    bias_tile = jnp.pad(jnp.concatenate([q_bias, w_bias])[None], ((0, 7), (0, 128 - 2 * share)))
    by_sub = send_rows.reshape(comms, subs, per).transpose(1, 0, 2).reshape(halo, 1)
    lead = (2,) * bits

    here = pl.BlockSpec(memory_space=pltpu.VMEM)
    anywhere = pl.BlockSpec(memory_space=pl.ANY)
    copies = 4 * bits + 3 * 2
    out = pl.pallas_call(
        functools.partial(
            gather_kernel, comms=comms, subs=subs, bits=bits, block=block, pool_block=pool_block
        ),
        in_specs=[here] * 7 + [anywhere],
        out_specs=[anywhere, here, anywhere, anywhere, anywhere, here, anywhere, anywhere, here],
        out_shape=[
            jax.ShapeDtypeStruct((rows, rows), BF),
            jax.ShapeDtypeStruct((rows, halo), BF),
            jax.ShapeDtypeStruct((rows, width), BF),
            jax.ShapeDtypeStruct((rows, width), BF),
            jax.ShapeDtypeStruct((rows, width), F32),
            jax.ShapeDtypeStruct((halo, width), BF),
            jax.ShapeDtypeStruct(lead + (q_rows, width), BF),
            jax.ShapeDtypeStruct(lead + (w_rows, width), BF),
            jax.ShapeDtypeStruct((8, width), F32),
        ],
        scratch_shapes=[
            pltpu.VMEM((rows, width), F32),
            pltpu.VMEM((rows, rows), BF),
            pltpu.VMEM((rows, width), BF),
            pltpu.VMEM((rows, width), BF),
            pltpu.VMEM((rows, width), BF),
            pltpu.VMEM((rows, width), F32),
            pltpu.VMEM(lead + (q_rows, width), BF),
            pltpu.VMEM((w_rows, width), BF),
            pltpu.VMEM(lead + (8, 128), F32),
            pltpu.VMEM((halo, width), F32),
            pltpu.VMEM((subs, halo // subs, width), BF),
            pltpu.VMEM((subs, halo // subs, width), BF),
            pltpu.VMEM((comms, halo // comms, width), BF),
            pltpu.VMEM((comms, halo // comms, width), BF),
            pltpu.SemaphoreType.DMA((6,)),
            pltpu.SemaphoreType.DMA((rows // block,)),
            pltpu.SemaphoreType.DMA((copies,)),
            pltpu.SemaphoreType.DMA((copies,)),
            pltpu.SemaphoreType.DMA((subs - 1,)),
            pltpu.SemaphoreType.DMA((subs - 1,)),
            pltpu.SemaphoreType.DMA((comms - 1,)),
            pltpu.SemaphoreType.DMA((comms - 1,)),
        ],
        compiler_params=pltpu.CompilerParams(
            collective_id=0, has_side_effects=True, vmem_limit_bytes=62 * 2**20
        ),
        name="gather_and_transform",
    )(
        nbr_index.T,
        nbr_count.reshape(1, rows),
        importance.T,
        q_weight,
        w_weight,
        bias_tile,
        by_sub,
        features,
    )
    own_mix, halo_mix, low, slope, pooled_own, incoming, q_full, w_full, biases = out
    return (
        own_mix,
        halo_mix,
        low,
        slope,
        pooled_own,
        incoming,
        q_full.reshape(devices * q_rows, width),
        w_full.reshape(devices * w_rows, width),
        biases[0],
        biases[1],
    )


def gather_plain(features, q_weight, q_bias, w_weight, w_bias, nbr_index, nbr_count, importance, send_rows):
    rows, width = features.shape
    devices, per_peer = send_rows.shape[1:]
    halo = devices * per_peer
    own_mix, halo_mix = build_mixing(nbr_index, nbr_count, importance, halo)
    q_full = lax.all_gather(q_weight.astype(BF), AXES, axis=0, tiled=True)
    w_full = lax.all_gather(w_weight.astype(BF), AXES, axis=0, tiled=True)
    biases = doubled(jnp.stack([q_bias, w_bias]), devices)
    qbias_full = biases[:, 0].reshape(width).astype(BF).astype(F32)
    wbias_full = biases[:, 1].reshape(width).astype(BF).astype(F32)
    low = features.astype(BF)
    neigh, slope = gelu_pair(jnp.dot(low, q_full, preferred_element_type=F32) + qbias_full)
    neigh = neigh.astype(BF)
    sent = neigh[send_rows[0]]
    incoming = lax.all_to_all(sent, AXES, split_axis=0, concat_axis=0, tiled=True).reshape(halo, width)
    pooled_own = pool_own(own_mix, neigh)
    return own_mix, halo_mix, low, slope.astype(BF), pooled_own, incoming, q_full, w_full, qbias_full, wbias_full


def resident(*shape):
    return pl.BlockSpec(shape, lambda i: (0,) * len(shape), pipeline_mode=pl.Buffered(1))


def by_rows(*shape):
    return pl.BlockSpec(shape, lambda i: (i,) + (0,) * (len(shape) - 1))


def product_kernel(mix_ref, table_ref, out_ref):
    out_ref[...] = jnp.dot(mix_ref[...], table_ref[...], preferred_element_type=F32)


def pool_own(own_mix, neigh):
    rows, width = neigh.shape
    block = 384
    return pl.pallas_call(
        product_kernel,
        grid=(rows // block,),
        in_specs=[by_rows(block, rows), resident(rows, width)],
        out_specs=by_rows(block, width),
        out_shape=jax.ShapeDtypeStruct((rows, width), F32),
        compiler_params=pltpu.CompilerParams(vmem_limit_bytes=40 * 2**20),
        cost_estimate=pl.CostEstimate(
            flops=2 * rows * rows * width, bytes_accessed=2 * rows * rows + 6 * rows * width, transcendentals=0
        ),
        name="pool_own",
    )(own_mix, neigh)


def combine_kernel(
    own_ref,
    halo_ref,
    incoming_ref,
    low_ref,
    w_ref,
    bias_ref,
    cotangent_ref,
    embedding_ref,
    pooled_ref,
    grad_ref,
    grad_pooled_ref,
    sent_ref,
    bias_grad_ref,
    act_buf,
    slope_buf,
):
    i = pl.program_id(0)
    block, width = low_ref.shape
    chunk = 256

    @pl.when(i == 0)
    def _():
        sent_ref[...] = jnp.zeros_like(sent_ref)
        bias_grad_ref[...] = jnp.zeros_like(bias_grad_ref)

    pooled = own_ref[...] + jnp.dot(halo_ref[...], incoming_ref[...], preferred_element_type=F32)
    pooled_ref[...] = pooled.astype(BF)
    squares = jnp.zeros((block, 128), F32)
    dots = jnp.zeros((block, 128), F32)
    for c in range(0, width, chunk):
        at = slice(c, c + chunk)
        pre = jnp.dot(low_ref[...], w_ref[:width, at], preferred_element_type=F32)
        pre += jnp.dot(pooled_ref[...], w_ref[width:, at], preferred_element_type=F32)
        act, slope = gelu_pair(pre + bias_ref[:, at])
        act_buf[:, at] = act
        slope_buf[:, at] = slope
        square = act * act
        dot = act * cotangent_ref[:, at]
        for k in range(0, chunk, 128):
            squares += square[:, k : k + 128]
            dots += dot[:, k : k + 128]
    scale = lax.rsqrt(jnp.sum(squares, axis=1, keepdims=True) * (1.0 / width) + 1e-06)
    pull = jnp.sum(dots, axis=1, keepdims=True) * (1.0 / width) * scale * scale * scale
    for c in range(0, width, chunk):
        at = slice(c, c + chunk)
        act = act_buf[:, at]
        embedding_ref[:, at] = act * scale
        grad = slope_buf[:, at] * (cotangent_ref[:, at] * scale - act * pull)
        grad_ref[:, at] = grad.astype(BF)
        bias_grad_ref[0:1, at] += jnp.sum(grad_ref[:, at].astype(F32), axis=0, keepdims=True)
    for c in range(0, width, chunk):
        at = slice(c, c + chunk)
        back = lax.dot_general(
            grad_ref[...],
            w_ref[width + c : width + c + chunk, :],
            (((1,), (1,)), ((), ())),
            preferred_element_type=F32,
        )
        grad_pooled_ref[:, at] = back.astype(BF)
    sent_ref[...] += lax.dot_general(
        halo_ref[...], grad_pooled_ref[...], (((0,), (0,)), ((), ())), preferred_element_type=F32
    )


def combine(pooled_own, halo_mix, incoming, low, w_full, w_bias, cotangent):
    rows, width = low.shape
    halo = incoming.shape[0]
    block = 256
    return pl.pallas_call(
        combine_kernel,
        grid=(rows // block,),
        in_specs=[
            by_rows(block, width),
            by_rows(block, halo),
            resident(halo, width),
            by_rows(block, width),
            resident(2 * width, width),
            resident(1, width),
            by_rows(block, width),
        ],
        out_specs=[
            by_rows(block, width),
            by_rows(block, width),
            by_rows(block, width),
            by_rows(block, width),
            pl.BlockSpec((halo, width), lambda i: (0, 0)),
            pl.BlockSpec((8, width), lambda i: (0, 0)),
        ],
        out_shape=[
            jax.ShapeDtypeStruct((rows, width), F32),
            jax.ShapeDtypeStruct((rows, width), BF),
            jax.ShapeDtypeStruct((rows, width), BF),
            jax.ShapeDtypeStruct((rows, width), BF),
            jax.ShapeDtypeStruct((halo, width), F32),
            jax.ShapeDtypeStruct((8, width), F32),
        ],
        scratch_shapes=[pltpu.VMEM((block, width), F32), pltpu.VMEM((block, width), F32)],
        compiler_params=pltpu.CompilerParams(vmem_limit_bytes=62 * 2**20),
        cost_estimate=pl.CostEstimate(
            flops=6 * rows * width * width, bytes_accessed=22 * rows * width, transcendentals=rows * width
        ),
        name="combine",
    )(pooled_own, halo_mix, incoming, low, w_full, w_bias.reshape(1, width), cotangent)


def swap(x, bit, devices):
    return lax.ppermute(x, AXES, [(i, i ^ (1 << bit)) for i in range(devices)])


def doubled(x, devices):
    me = lax.axis_index(AXES)
    x = x[None]
    for bit in range(devices.bit_length() - 1):
        other = swap(x, bit, devices)
        first = ((me >> bit) & 1) == 0
        x = jnp.where(first, jnp.concatenate([x, other]), jnp.concatenate([other, x]))
    return x


def summed(x, devices):
    for bit in range(devices.bit_length() - 1):
        x = x + swap(x, bit, devices)
    return x


def halve(part, left, bit, devices):
    mine = (lax.axis_index(AXES) >> bit) & 1
    axis = left.index(bit)
    keep = lax.dynamic_index_in_dim(part, mine, axis, keepdims=False)
    sent = lax.dynamic_index_in_dim(part, 1 - mine, axis, keepdims=False)
    total = keep.astype(F32) + swap(sent, bit, devices).astype(F32)
    return total, [b for b in left if b != bit]


def scatter_sum(partial, devices):
    bits = list(range(devices.bit_length() - 1))[::-1]
    width = partial.shape[1]
    part = partial.reshape([2] * len(bits) + [-1, width])
    part, left = halve(part, bits, 0, devices)
    part = part.astype(BF)
    rows = part.shape[-2] // 2
    orders = ([1, 2] + list(range(3, len(bits))), [2, 1] + list(range(3, len(bits))))
    halves = [(part[..., :rows, :], left), (part[..., rows:, :], left)]
    for step in range(len(bits) - 1):
        for s in range(2):
            total, rest = halve(halves[s][0], halves[s][1], orders[s][step], devices)
            halves[s] = (total if len(rest) == 0 else total.astype(BF), rest)
    return jnp.concatenate([h[0] for h in halves], axis=0)


def back_plain(
    own_mix, low, slope, pooled, grad_out, grad_pooled, sent_grad, grad_wbias, q_full, w_full, send_rows
):
    rows, width = low.shape
    devices, per = send_rows.shape[1:]
    contract = (((0,), (0,)), ((), ()))
    returned = lax.all_to_all(
        sent_grad.reshape(devices, per, width), AXES, split_axis=0, concat_axis=0, tiled=True
    )
    joined = jnp.concatenate([low, pooled], axis=1)
    grad_w = lax.dot_general(joined, grad_out, contract, preferred_element_type=F32)
    grad_low = lax.dot_general(grad_out, w_full[:width], (((1,), (1,)), ((), ())), preferred_element_type=F32)
    grad_neigh = lax.dot_general(own_mix, grad_pooled, contract, preferred_element_type=F32)
    grad_neigh = grad_neigh.at[send_rows.reshape(-1)].add(returned.reshape(devices * per, width))
    grad_hidden = (slope.astype(F32) * grad_neigh).astype(BF)
    grad_q = lax.dot_general(low, grad_hidden, contract, preferred_element_type=F32)
    grad_qbias = jnp.sum(grad_hidden.astype(F32), axis=0)
    grad_features = grad_low + lax.dot_general(
        grad_hidden, q_full, (((1,), (1,)), ((), ())), preferred_element_type=F32
    )
    me = lax.axis_index(AXES)
    share = width // devices
    sums = summed(jnp.stack([grad_qbias, grad_wbias[0]]), devices)
    sums = lax.dynamic_slice_in_dim(sums, me * share, share, 1)
    return (
        grad_features,
        scatter_sum(grad_q.astype(BF), devices),
        sums[0],
        scatter_sum(grad_w.astype(BF), devices),
        sums[1],
    )


class ScatterSum:
    def __init__(self, refs, orders, mine, partner):
        self.held, self.sent, self.got, self.next_sent, self.next_got, self.send_sem, self.recv_sem = refs
        self.orders, self.mine, self.partner = orders, mine, partner
        self.bits = len(mine)
        self.lead = list(range(1, self.bits))[::-1]
        self.half = self.held.shape[-1] // 2

    def copy(self, n, source, target, b):
        return pltpu.make_async_remote_copy(
            src_ref=source,
            dst_ref=target,
            send_sem=self.send_sem.at[n],
            recv_sem=self.recv_sem.at[n],
            device_id=self.partner(b),
            device_id_type=pl.DeviceIdType.MESH,
        )

    def first(self, top):
        return self.copy(top, self.sent.at[self.top_index(top)], self.got.at[self.top_index(top)], 0)

    def top_index(self, top):
        return ((top // 2) % 2, top % 2)

    def later(self, k):
        out = []
        for h in range(2):
            n = 4 + 2 * (k - 1) + h
            at = (h,) + (slice(self.offset(k), self.offset(k) + (1 << (self.bits - 1 - k))),)
            out.append(self.copy(n, self.next_sent.at[at], self.next_got.at[at], self.orders[h][k - 1]))
        return out

    def offset(self, k):
        return (1 << (self.bits - 1)) - (1 << (self.bits - k))

    def spot(self, chosen):
        return tuple(chosen[b] for b in self.lead)

    def absorb(self, k):
        for h in range(2):
            order = self.orders[h]
            fixed = order[:k]
            free = [b for b in self.lead if b not in fixed]
            columns = slice(h * self.half, (h + 1) * self.half)

            def total(chosen, h=h, free=free, columns=columns):
                at = self.spot(chosen)
                if k == 0:
                    came = self.got[at + (slice(None), columns)]
                else:
                    place = self.offset(k)
                    for p, b in enumerate(free[::-1]):
                        place = place + chosen[b] * (1 << p)
                    came = self.next_got[h, place]
                return at, self.held[at + (slice(None), columns)] + came.astype(F32)

            if not free:
                at, value = total({b: self.mine[b] for b in fixed})
                self.held[at + (slice(None), columns)] = value
                continue
            split = order[k]
            others = [b for b in free if b != split]

            def body(n, carry, total=total, split=split, others=others, fixed=fixed, columns=columns, h=h):
                chosen = {b: self.mine[b] for b in fixed}
                for p, b in enumerate(others[::-1]):
                    chosen[b] = (n // (1 << p)) % 2
                chosen[split] = self.mine[split]
                at, value = total(chosen)
                self.held[at + (slice(None), columns)] = value
                chosen[split] = 1 - self.mine[split]
                _, value = total(chosen)
                self.next_sent[h, self.offset(k + 1) + n] = value.astype(BF)
                return carry

            lax.fori_loop(0, 1 << len(others), body, 0)

    def start(self, k):
        for c in self.later(k):
            c.start()

    def wait(self, k):
        for c in [self.first(t) for t in range(4)] if k == 0 else self.later(k):
            c.wait()

    def result(self):
        return self.held[self.spot({b: self.mine[b] for b in self.lead})]


def back_body(
    sent_grad_ref,
    w_bias_ref,
    target_ref,
    mix_hbm,
    slope_hbm,
    low_hbm,
    pooled_hbm,
    out_hbm,
    grad_pooled_hbm,
    w_hbm,
    q_hbm,
    features_out,
    q_out,
    w_out,
    bias_out,
    joined,
    grad_out,
    grad_pooled,
    slope,
    w_top,
    q_full,
    mix,
    features,
    q_bias_acc,
    bias_sent,
    bias_got,
    comm_blocks,
    comm_landed,
    sub_blocks,
    sub_landed,
    *rest,
    comms,
    subs,
    bits,
    mix_block,
    row_block,
):
    sets = [rest[7 * k : 7 * k + 7] for k in range(3)]
    load_sem, mix_sem, out_sem, bias_send, bias_recv, comm_send, comm_recv, sub_send, sub_recv = rest[21:]
    rows, width = grad_out.shape
    halo = sent_grad_ref.shape[0]
    half = width // 2
    comm, sub = lax.axis_index("comm"), lax.axis_index("sub")
    me = comm * subs + sub
    mine = [(me // (1 << b)) % 2 for b in range(bits)]
    tn = (((0,), (0,)), ((), ()))
    nt = (((1,), (1,)), ((), ()))

    def partner(b):
        other = me + (1 << b) * (1 - 2 * mine[b])
        return (other // subs, other % subs)

    high = list(range(3, bits))
    orders = ([1, 2] + high, [2, 1] + high)
    w_sets = [ScatterSum(sets[k], orders, mine, partner) for k in range(2)]
    q_set = ScatterSum(sets[2], orders, mine, partner)

    left, right = pl.ds(0, half), pl.ds(half, half)
    loads = [
        (out_hbm.at[:, left], grad_out.at[:, left]),
        (low_hbm.at[:, left], joined.at[:, pl.ds(0, half)]),
        (low_hbm.at[:, right], joined.at[:, pl.ds(half, half)]),
        (pooled_hbm.at[:, left], joined.at[:, pl.ds(2 * half, half)]),
        (pooled_hbm.at[:, right], joined.at[:, pl.ds(3 * half, half)]),
        (out_hbm.at[:, right], grad_out.at[:, right]),
        (grad_pooled_hbm, grad_pooled),
        (slope_hbm, slope),
        (w_hbm.at[pl.ds(0, width), :], w_top),
        (q_hbm, q_full),
    ]
    loads = [pltpu.make_async_copy(a, b, load_sem.at[n]) for n, (a, b) in enumerate(loads)]
    comm_ring = ring_copies(comms, comm, comm_blocks, comm_landed, comm_send, comm_recv, lambda j: (j, sub))
    sub_ring = ring_copies(subs, sub, sub_blocks, sub_landed, sub_send, sub_recv, lambda j: (comm, j))
    bias_copies = [
        pltpu.make_async_remote_copy(
            src_ref=bias_sent.at[b],
            dst_ref=bias_got.at[b],
            send_sem=bias_send.at[b],
            recv_sem=bias_recv.at[b],
            device_id=partner(b),
            device_id_type=pl.DeviceIdType.MESH,
        )
        for b in range(bits)
    ]

    spreads = rows // mix_block
    rounds = rows // row_block

    def mix_copy(n):
        at = pl.ds(pl.multiple_of(n * mix_block, mix_block), mix_block)
        return pltpu.make_async_copy(mix_hbm.at[:, at], mix.at[n % 2], mix_sem.at[n % 2])

    def out_copy(n):
        at = pl.ds(pl.multiple_of(n * row_block, row_block), row_block)
        return pltpu.make_async_copy(features.at[n % 2], features_out.at[at, :], out_sem.at[n % 2])

    def step_of(which, k):
        which.wait(k)
        which.absorb(k)
        if k < bits - 1:
            which.start(k + 1)

    def deal(value, which, top, rows_each):
        keep_even = mine[0] == 0
        shares = value.shape[0] // rows_each
        for p in range(shares // 2):
            even = value[2 * p * rows_each : (2 * p + 1) * rows_each]
            odd = value[(2 * p + 1) * rows_each : (2 * p + 2) * rows_each]
            at = top + tuple((p >> b) & 1 for b in range(bits - 2, -1, -1))[len(top) :]
            which.held[at] = jnp.where(keep_even, even, odd)
            which.sent[at] = jnp.where(keep_even, odd, even).astype(BF)

    def w_top_bits(j):
        return ((j // 2) % 2, j % 2)

    events = {
        ("w1", 1): [(0, 0)],
        ("spread", 1): [(1, 0), (0, 1)],
        ("spread", 3): [(0, 2)],
        ("spread", 4): [(1, 1)],
        ("spread", 5): [(0, 3)],
        ("q", 1): [(1, 2), (0, 4)],
        ("q", 3): [(1, 3)],
        ("features", 1): [(1, 4), (2, 0)],
        ("features", 4): [(2, 1)],
    }
    all_sets = w_sets + [q_set]

    def happen(phase, n):
        for (when, step), which in events.items():
            if when == phase:

                @pl.when(n == step)
                def _(which=which):
                    for m, k in which:
                        step_of(all_sets[m], k)

    def load_when(step, n, begin=(), need=()):
        @pl.when(n == step)
        def _():
            for m in need:
                loads[m].wait()
            for m in begin:
                loads[m].start()

    for n in range(3):
        loads[n].start()
    comm_blocks[...] = sent_grad_ref[...].astype(BF).reshape(comm_blocks.shape)
    q_bias_acc[...] = jnp.zeros_like(q_bias_acc)
    greet(comm, sub, comms, subs)
    for c in comm_ring:
        c.start()
    comm_landed[comm] = comm_blocks[comm]

    for n in range(2):

        @pl.loop(0, 4)
        def _(j, n=n):
            if n == 0:
                load_when(0, j, [3], [0, 1])
                load_when(1, j, [4], [2])
                load_when(2, j, [5], [3])
                load_when(3, j, [6], [4])
            else:
                load_when(0, j, [7], [5])
                load_when(1, j, [8])
                load_when(2, j, [9])

                @pl.when(j == 3)
                def _():
                    mix_copy(0).start()

            at = pl.ds(pl.multiple_of(j * half, half), half)
            columns = slice(n * half, (n + 1) * half)
            value = lax.dot_general(joined[:, at], grad_out[:, columns], tn, preferred_element_type=F32)
            deal(value, w_sets[n], w_top_bits(j), w_out.shape[0])
            w_sets[n].first(j).start()
            happen("w" + str(n), j)

        if n == 0:
            for c in comm_ring:
                c.wait()
            moved = regroup(comm_landed[...].reshape(halo, width), comms, subs, halo // (subs * comms))
            sub_blocks[...] = moved.reshape(sub_blocks.shape)
            for c in sub_ring:
                c.start()
            sub_landed[sub] = sub_blocks[sub]

    for c in sub_ring:
        c.wait()
    for n in (6, 7):
        loads[n].wait()

    @pl.loop(0, spreads)
    def _(n):
        @pl.when(n + 1 < spreads)
        def _():
            mix_copy(n + 1).start()

        happen("spread", n)
        mix_copy(n).wait()
        start = n * mix_block
        at = pl.ds(pl.multiple_of(start, mix_block), mix_block)
        local = lax.broadcasted_iota(jnp.int32, (mix_block, halo), 0) + start
        chosen = jnp.where(local == target_ref[...], 1.0, 0.0).astype(BF)
        back = lax.dot_general(mix[n % 2], grad_pooled[...], tn, preferred_element_type=F32)
        back += jnp.dot(chosen, sub_landed[...].reshape(halo, width), preferred_element_type=F32)
        grad = (back * slope[at, :].astype(F32)).astype(BF)
        joined[at, width:] = grad
        q_bias_acc[0:1, :] += jnp.sum(grad.astype(F32), axis=0, keepdims=True)

    def bias_step(b):
        if b:
            bias_copies[b - 1].wait()
            total = bias_sent[b - 1] + bias_got[b - 1]
            if b == bits:
                bias_out[...] = total
                return
            bias_sent[b] = total
        bias_copies[b].start()

    pieces = [w_bias_ref[0:1, c : c + 128] for c in range(0, width, 128)]
    pieces += [q_bias_acc[0:1, c : c + 128] for c in range(0, width, 128)]
    bias_sent[0] = jnp.concatenate(pieces, axis=0)

    for t in range(4):
        bias_step(t)
        n, j = t % 2, t // 2
        value = lax.dot_general(
            joined[:, j * half : (j + 1) * half],
            joined[:, width + n * half : width + (n + 1) * half],
            tn,
            preferred_element_type=F32,
        )
        keep_even = mine[0] == 0
        columns = slice(n * half, (n + 1) * half)
        each = q_out.shape[0]
        for p in range(half // each // 2):
            even = value[2 * p * each : (2 * p + 1) * each]
            odd = value[(2 * p + 1) * each : (2 * p + 2) * each]
            at = (j, (p >> 2) & 1, (p >> 1) & 1, p & 1, slice(None), columns)
            q_set.held[at] = jnp.where(keep_even, even, odd)
            q_set.sent[at] = jnp.where(keep_even, odd, even).astype(BF)
        if n == 1:
            q_set.first(2 * j).start()
            q_set.first(2 * j + 1).start()
        for m, k in events.get(("q", t), []):
            step_of(all_sets[m], k)
    bias_step(4)
    for n in (8, 9):
        loads[n].wait()

    @pl.loop(0, rounds)
    def _(n):
        happen("features", n)

        @pl.when(n >= 2)
        def _():
            out_copy(n - 2).wait()

        at = pl.ds(pl.multiple_of(n * row_block, row_block), row_block)
        value = lax.dot_general(grad_out[at, :], w_top[...], nt, preferred_element_type=F32)
        features[n % 2] = value + lax.dot_general(
            joined[at, width:], q_full[...], nt, preferred_element_type=F32
        )
        out_copy(n).start()

    for k in range(2, bits):
        step_of(q_set, k)
    for n in range(2):
        w_out[:, n * half : (n + 1) * half] = w_sets[n].result()
    q_out[...] = q_set.result()
    bias_step(bits)
    for n in range(rounds - 2, rounds):
        out_copy(n).wait()


def back_kernel(
    own_mix, low, slope, pooled, grad_out, grad_pooled, sent_grad, grad_wbias, q_full, w_full, send_rows
):
    comms, subs = lax.axis_size("comm"), lax.axis_size("sub")
    devices = comms * subs
    bits = devices.bit_length() - 1
    rows, width = low.shape
    per = send_rows.shape[2]
    halo = devices * per
    mix_block, row_block = 384, 384
    w_rows, q_rows = w_full.shape[0] // devices, q_full.shape[0] // devices
    targets = send_rows.reshape(comms, subs, per).transpose(1, 0, 2).reshape(1, halo)
    lead = (2,) * (bits - 1)

    def set_scratch(rows_each, columns):
        chunks = (1 << (bits - 1)) - 1
        copies = 4 + 2 * (bits - 1)
        return [
            pltpu.VMEM(lead + (rows_each, columns), F32),
            pltpu.VMEM(lead + (rows_each, columns), BF),
            pltpu.VMEM(lead + (rows_each, columns), BF),
            pltpu.VMEM((2, chunks, rows_each, columns // 2), BF),
            pltpu.VMEM((2, chunks, rows_each, columns // 2), BF),
            pltpu.SemaphoreType.DMA((copies,)),
            pltpu.SemaphoreType.DMA((copies,)),
        ]

    here = pl.BlockSpec(memory_space=pltpu.VMEM)
    anywhere = pl.BlockSpec(memory_space=pl.ANY)
    grad_features, grad_q, grad_w, biases = pl.pallas_call(
        functools.partial(
            back_body, comms=comms, subs=subs, bits=bits, mix_block=mix_block, row_block=row_block
        ),
        in_specs=[here] * 3 + [anywhere] * 8,
        out_specs=[anywhere] + [here] * 3,
        out_shape=[
            jax.ShapeDtypeStruct((rows, width), F32),
            jax.ShapeDtypeStruct((q_rows, width), F32),
            jax.ShapeDtypeStruct((w_rows, width), F32),
            jax.ShapeDtypeStruct((16, 128), F32),
        ],
        scratch_shapes=[
            pltpu.VMEM((rows, 2 * width), BF),
            pltpu.VMEM((rows, width), BF),
            pltpu.VMEM((rows, width), BF),
            pltpu.VMEM((rows, width), BF),
            pltpu.VMEM((width, width), BF),
            pltpu.VMEM((width, width), BF),
            pltpu.VMEM((2, rows, mix_block), BF),
            pltpu.VMEM((2, row_block, width), F32),
            pltpu.VMEM((8, width), F32),
            pltpu.VMEM((bits, 16, 128), F32),
            pltpu.VMEM((bits, 16, 128), F32),
            pltpu.VMEM((comms, halo // comms, width), BF),
            pltpu.VMEM((comms, halo // comms, width), BF),
            pltpu.VMEM((subs, halo // subs, width), BF),
            pltpu.VMEM((subs, halo // subs, width), BF),
        ]
        + set_scratch(w_rows, width // 2)
        + set_scratch(w_rows, width // 2)
        + set_scratch(q_rows, width)
        + [
            pltpu.SemaphoreType.DMA((10,)),
            pltpu.SemaphoreType.DMA((2,)),
            pltpu.SemaphoreType.DMA((2,)),
            pltpu.SemaphoreType.DMA((bits,)),
            pltpu.SemaphoreType.DMA((bits,)),
            pltpu.SemaphoreType.DMA((comms - 1,)),
            pltpu.SemaphoreType.DMA((comms - 1,)),
            pltpu.SemaphoreType.DMA((subs - 1,)),
            pltpu.SemaphoreType.DMA((subs - 1,)),
        ],
        compiler_params=pltpu.CompilerParams(
            collective_id=1, has_side_effects=True, vmem_limit_bytes=62 * 2**20
        ),
        name="back",
    )(sent_grad, grad_wbias, targets, own_mix, slope, low, pooled, grad_out, grad_pooled, w_full, q_full)
    share = width // devices
    sums = lax.dynamic_slice_in_dim(biases.reshape(2, width), lax.axis_index(AXES) * share, share, 1)
    return grad_features, grad_q, sums[1], grad_w, sums[0]


def shards(
    features,
    q_weight,
    q_bias,
    w_weight,
    w_bias,
    nbr_index,
    nbr_count,
    importance,
    send_rows,
    cotangent,
):
    devices = lax.axis_size(AXES)
    kernel_fits = devices == 32 and q_weight.shape[0] % 16 == 0
    gather, back = (gather_and_transform, back_kernel) if kernel_fits else (gather_plain, back_plain)
    own_mix, halo_mix, low, slope, pooled_own, incoming, q_full, w_full, qbias_full, wbias_full = gather(
        features, q_weight, q_bias, w_weight, w_bias, nbr_index, nbr_count, importance, send_rows
    )
    embedding, pooled, grad_out, grad_pooled, sent_grad, grad_wbias = combine(
        pooled_own, halo_mix, incoming, low, w_full, wbias_full, cotangent
    )
    grad_features, grad_q, grad_qbias, grad_w, grad_wbias = back(
        own_mix, low, slope, pooled, grad_out, grad_pooled, sent_grad, grad_wbias, q_full, w_full, send_rows
    )
    return embedding, grad_features, grad_q, grad_qbias, grad_w, grad_wbias


def solution(mesh):
    in_specs = (
        P(("comm", "sub"), None),
        P(("comm", "sub"), None),
        P(("comm", "sub")),
        P(("comm", "sub"), None),
        P(("comm", "sub")),
        P(("comm", "sub"), None),
        P(("comm", "sub")),
        P(("comm", "sub"), None),
        P(("comm", "sub"), None, None),
        P(("comm", "sub"), None),
    )
    out_specs = (
        P(("comm", "sub"), None),
        P(("comm", "sub"), None),
        P(("comm", "sub"), None),
        P(("comm", "sub")),
        P(("comm", "sub"), None),
        P(("comm", "sub")),
    )
    return jax.shard_map(shards, mesh=mesh, in_specs=in_specs, out_specs=out_specs, check_vma=False)
```

```python
import functools
import math

import jax
import jax.numpy as jnp
from jax import lax
from jax.experimental import pallas as pl
from jax.experimental.pallas import tpu as pltpu
from jax.sharding import PartitionSpec as P

BF = jnp.bfloat16
F32 = jnp.float32
AXES = ("comm", "sub")


def build_rows(index_ref, counts, importance_ref, own_ref, halo_ref, first, *, rows, halo):
    his = (rows + halo + 255) // 256
    pairs = (his + 1) // 2
    fanout = index_ref.shape[0]
    at = pl.ds(pl.multiple_of(first, 128), 128)
    lane = lax.broadcasted_iota(jnp.int32, (16, 128), 1)
    sublane = lax.broadcasted_iota(jnp.int32, (16, 128), 0)
    parity = (sublane >= 8).astype(jnp.int32)
    half = (lane >= 64).astype(jnp.int32)
    los = lax.broadcasted_iota(jnp.int32, (64, 256), 1).astype(BF)
    left = lax.broadcasted_iota(jnp.int32, (1, 128), 1) < 64
    hi_pattern = [(2 * t + parity).astype(BF) for t in range(pairs)]
    row_mask = [(sublane & 7) == 2 * c + half for c in range(4)]
    zero = jnp.zeros((), BF)
    one = jnp.ones((), BF)

    def slots(x):
        return jnp.concatenate([x, jnp.zeros((64 - fanout, 128), F32)], axis=0)

    def by_row(x):
        x = slots(x).T
        return jnp.concatenate([x, x], axis=1)

    index = index_ref[:, at]
    slot = lax.broadcasted_iota(jnp.int32, index.shape, 0)
    weight = jnp.where(slot < counts, importance_ref[:, at], 0.0)
    alpha = by_row(weight / jnp.sum(weight, axis=0, keepdims=True))
    hi = by_row((index >> 8).astype(F32))
    lo = slots((index & 255).astype(F32)).astype(BF)
    for g in range(0, 128, 16):
        tiles = []
        for s in range(2):
            left_parts, right_parts = [], []
            for c in range(4):
                r = g + s * 8 + 2 * c

                def pick(x):
                    return jnp.where(left, x[r : r + 1, :], x[r + 1 : r + 2, :]).astype(BF)

                kept = jnp.where(row_mask[c], jnp.broadcast_to(pick(alpha), (16, 128)), zero)
                hi_row = jnp.broadcast_to(pick(hi), (16, 128))
                left_parts.append(
                    jnp.concatenate(
                        [jnp.where(hi_row == hi_pattern[t], kept, zero) for t in range(pairs)], axis=0
                    )
                )
                for q in (r, r + 1):
                    right_parts.append(jnp.where(jnp.broadcast_to(lo[:, q : q + 1], (64, 256)) == los, one, zero))
            tiles.append(
                jnp.dot(
                    jnp.concatenate(left_parts, axis=1),
                    jnp.concatenate(right_parts, axis=0),
                    preferred_element_type=F32,
                )
            )
        for h in range(his):
            tile = jnp.concatenate([t[h * 8 : (h + 1) * 8, :] for t in tiles], axis=0).astype(BF)
            to = pl.ds(pl.multiple_of(first + g, 16), 16)
            if h * 256 < rows:
                own_ref[to, h * 256 : (h + 1) * 256] = tile
            else:
                start = h * 256 - rows
                stop = min(start + 256, halo)
                halo_ref[to, start:stop] = tile[:, : stop - start]


def build_kernel(index_ref, count_ref, importance_ref, own_ref, halo_ref, *, rows, halo):
    for first in range(0, own_ref.shape[0], 128):
        counts = count_ref[:, first : first + 128]
        build_rows(index_ref, counts, importance_ref, own_ref, halo_ref, first, rows=rows, halo=halo)


def build_mixing(nbr_index, nbr_count, importance, halo):
    rows, fanout = nbr_index.shape
    block = 256
    return pl.pallas_call(
        functools.partial(build_kernel, rows=rows, halo=halo),
        grid=(rows // block,),
        in_specs=[
            pl.BlockSpec((fanout, block), lambda i: (0, i)),
            pl.BlockSpec((1, block), lambda i: (0, i)),
            pl.BlockSpec((fanout, block), lambda i: (0, i)),
        ],
        out_specs=[
            pl.BlockSpec((block, rows), lambda i: (i, 0)),
            pl.BlockSpec((block, halo), lambda i: (i, 0)),
        ],
        out_shape=[
            jax.ShapeDtypeStruct((rows, rows), BF),
            jax.ShapeDtypeStruct((rows, halo), BF),
        ],
        compiler_params=pltpu.CompilerParams(vmem_limit_bytes=40 * 2**20),
        name="build_mixing",
    )(nbr_index.T, nbr_count.reshape(1, rows), importance.T)


def gelu_pair(x):
    c = math.sqrt(2.0 / math.pi)
    square = x * x
    t = jnp.tanh(x * (c + (c * 0.044715) * square))
    half = 0.5 + 0.5 * t
    slope = x * (0.5 - 0.5 * t * t) * (c + (3.0 * c * 0.044715) * square)
    return x * half, half + slope


def hidden_rows(features_ref, q_buf, bias_ref, send_ref, low_ref, neigh_ref, slope_ref, sent_ref, at_rows, start):
    width = features_ref.shape[1]
    lead = (slice(None),) * (len(q_buf.shape) - 1)
    low_ref[at_rows, :] = features_ref[at_rows, :].astype(BF)
    for c in range(0, width, 256):
        at = slice(c, c + 256)
        q = q_buf[lead + (at,)].reshape(width, 256)
        pre = jnp.dot(low_ref[at_rows, :], q, preferred_element_type=F32) + bias_ref[0:1, at]
        value, slope = gelu_pair(pre)
        neigh_ref[at_rows, at] = value.astype(BF)
        slope_ref[at_rows, at] = slope.astype(BF)
    neigh = neigh_ref[at_rows, :]
    local = lax.broadcasted_iota(jnp.int32, (neigh.shape[0], send_ref.shape[1]), 0) + start
    chosen = jnp.where(local == send_ref[...], 1.0, 0.0).astype(BF)
    sent_ref[...] += lax.dot_general(chosen, neigh, (((0,), (0,)), ((), ())), preferred_element_type=F32)


def ring_copies(groups, index, blocks_ref, landed_ref, send_sem, recv_sem, device_of):
    copies = []
    for k in range(1, groups):
        other = (index + k) % groups
        copies.append(
            pltpu.make_async_remote_copy(
                src_ref=blocks_ref.at[other],
                dst_ref=landed_ref.at[index],
                send_sem=send_sem.at[k - 1],
                recv_sem=recv_sem.at[k - 1],
                device_id=device_of(other),
                device_id_type=pl.DeviceIdType.MESH,
            )
        )
    return copies


def regroup(x, outer, inner, per):
    count = x.shape[0]
    to = lax.broadcasted_iota(jnp.int32, (count, count), 0)
    place = lax.broadcasted_iota(jnp.int32, (count, count), 1)
    source = ((to // per) % outer) * (inner * per) + (to // (per * outer)) * per + to % per
    chosen = jnp.where(place == source, 1.0, 0.0).astype(BF)
    return jnp.dot(chosen, x, preferred_element_type=F32).astype(BF)


def greet(comm, sub, comms, subs):
    barrier = pltpu.get_barrier_semaphore()
    for k in range(1, comms):
        pl.semaphore_signal(
            barrier, inc=1, device_id=((comm + k) % comms, sub), device_id_type=pl.DeviceIdType.MESH
        )
    for k in range(1, subs):
        pl.semaphore_signal(
            barrier, inc=1, device_id=(comm, (sub + k) % subs), device_id_type=pl.DeviceIdType.MESH
        )
    pl.semaphore_wait(barrier, comms + subs - 2)


def send_targets(send_rows, comms, subs):
    per = send_rows.shape[2]
    return send_rows.reshape(comms, subs, per).transpose(1, 0, 2).reshape(1, comms * subs * per)


def gather_kernel(
    index_ref,
    count_ref,
    importance_ref,
    q_ref,
    w_ref,
    q_bias_ref,
    w_bias_ref,
    send_ref,
    features_hbm,
    own_out,
    halo_ref,
    low_out,
    slope_out,
    pooled_out,
    incoming_ref,
    q_full,
    w_full,
    bias_out,
    features,
    own_mix,
    low,
    neigh,
    slope,
    pooled,
    q_buf,
    w_own,
    bias_buf,
    sent_acc,
    sub_blocks,
    sub_landed,
    comm_blocks,
    comm_landed,
    local_sem,
    feature_sem,
    send_sem,
    recv_sem,
    sub_send,
    sub_recv,
    comm_send,
    comm_recv,
    *,
    comms,
    subs,
    bits,
    block,
    pool_block,
):
    rows = own_mix.shape[0]
    halo = halo_ref.shape[1]
    width = neigh.shape[1]
    comm, sub = lax.axis_index("comm"), lax.axis_index("sub")
    me = comm * subs + sub
    mine = [(me // (1 << b)) % 2 for b in range(bits)]
    order = list(range(bits))[::-1]

    def partner(b):
        other = me + (1 << b) * (1 - 2 * mine[b])
        return (other // subs, other % subs)

    def spot(done, part=slice(None), columns=slice(None)):
        lead = tuple(slice(None) if b in done else mine[b] for b in order)
        return lead + (part, columns)

    high = list(range(3, bits))[::-1]
    left, right = pl.ds(0, width // 2), pl.ds(width // 2, width // 2)
    count = [0]

    def exchange(buf, b, done, part=slice(None), columns=slice(None), source=None):
        at = buf.at[spot(done, part, columns)]
        n = count[0]
        count[0] += 1
        return pltpu.make_async_remote_copy(
            src_ref=at if source is None else source,
            dst_ref=at,
            send_sem=send_sem.at[n],
            recv_sem=recv_sem.at[n],
            device_id=partner(b),
            device_id_type=pl.DeviceIdType.MESH,
        )

    def chain(buf, own, split, part=slice(None)):
        groups = []
        done = []
        for b in high:
            groups.append([exchange(buf, b, done, part, source=own if not done else None)])
            done = done + [b]
        if split:
            groups.append([exchange(buf, 1, done, part, left), exchange(buf, 2, done, part, right)])
            groups.append(
                [exchange(buf, 2, done + [1], part, left), exchange(buf, 1, done + [2], part, right)]
            )
        else:
            groups.append([exchange(buf, 1, done)])
            groups.append([exchange(buf, 2, done + [1])])
        groups.append([exchange(buf, 0, done + [1, 2], part)])
        return groups

    w_rows = w_own.shape[0]
    top, bottom = pl.ds(0, w_rows // 2), pl.ds(w_rows // 2, w_rows // 2)
    chains = {
        "q": chain(q_buf, None, True),
        "bias": chain(bias_buf, None, False),
        "w0": chain(w_full, w_own.at[top], True, top),
        "w1": chain(w_full, w_own.at[bottom], True, bottom),
        "sub": [ring_copies(subs, sub, sub_blocks, sub_landed, sub_send, sub_recv, lambda j: (comm, j))],
        "comm": [ring_copies(comms, comm, comm_blocks, comm_landed, comm_send, comm_recv, lambda j: (j, sub))],
    }
    w_local = pltpu.make_async_copy(w_own, w_full.at[spot([])], local_sem.at[0])
    q_local = pltpu.make_async_copy(q_buf, q_full, local_sem.at[1])
    last = len(chains["q"]) - 1

    def begin(name, n):
        for c in chains[name][n]:
            c.start()

    def finish(name, n):
        for c in chains[name][n]:
            c.wait()

    def place(n, size):
        return pl.ds(pl.multiple_of(n * size, size), size)

    def feature_copy(n):
        at = place(n, block)
        return pltpu.make_async_copy(features_hbm.at[at, :], features.at[at, :], feature_sem.at[n])

    outs = [(own_mix, own_out), (low, low_out), (slope, slope_out), (pooled, pooled_out)]

    def give(n, at):
        source, target = outs[n]
        pltpu.make_async_copy(source.at[at, :], target.at[at, :], local_sem.at[2 + n]).start()

    def given(n):
        pltpu.make_async_copy(*outs[n], local_sem.at[2 + n]).wait()

    events = {
        ("build", 4): [("q", 0), ("bias", 0)],
        ("build", 6): [("w0", -1)],
        ("build", 7): [("q", 1), ("bias", 1)],
        ("build", 9): [("w1", -1)],
        ("build", 10): [("q", 2), ("bias", 2), ("w0", 0)],
        ("build", 13): [("w1", 0)],
        ("build", 14): [("w0", 1)],
        ("build", 15): [("q", 3), ("bias", 3)],
        ("hidden", 0): [("w1", 1)],
        ("hidden", 1): [("w0", 2)],
        ("hidden", 6): [("w0", 3), ("w1", 2)],
        ("pool", 2): [("w1", 3)],
    }

    def happen(phase, n):
        for (when, step), names in events.items():
            if when == phase:

                @pl.when(n == step)
                def _(names=names):
                    for name, k in names:
                        if k >= 0:
                            finish(name, k)
                        begin(name, k + 1)

    q_buf[spot([])] = q_ref[...].astype(BF)
    w_own[...] = w_ref[...].astype(BF)
    share = q_bias_ref.shape[1]
    bias_own = jnp.concatenate(
        [q_bias_ref[...], w_bias_ref[...], jnp.zeros((1, 128 - 2 * share), F32)], axis=1
    )
    bias_buf[spot([])] = jnp.broadcast_to(bias_own, (8, 128))
    greet(comm, sub, comms, subs)
    begin("q", 0)
    begin("bias", 0)
    w_local.start()
    sent_acc[...] = jnp.zeros_like(sent_acc)
    w_local.wait()

    @pl.loop(0, rows // block)
    def _(n):
        feature_copy(n).start()

    @pl.loop(0, rows // 128)
    def _(n):
        happen("build", n)
        build_rows(
            index_ref,
            count_ref[pl.ds(n, 1), :],
            importance_ref,
            own_mix,
            halo_ref,
            n * 128,
            rows=rows,
            halo=halo,
        )
        give(0, place(n, 128))

    finish("q", last)
    finish("bias", last)
    q_local.start()
    for k in range(2):
        pieces = []
        for e in range(1 << bits):
            piece = bias_buf[tuple((e >> b) & 1 for b in order)]
            pieces.append(piece[0:1, k * share : (k + 1) * share])
        bias_out[k : k + 1, :] = jnp.concatenate(pieces, axis=1).astype(BF).astype(F32)
    bias_out[2:, :] = jnp.zeros((6, width), F32)

    @pl.loop(0, rows // block)
    def _(n):
        happen("hidden", n)
        feature_copy(n).wait()
        at = place(n, block)
        hidden_rows(features, q_buf, bias_out, send_ref, low, neigh, slope, sent_acc, at, n * block)
        give(1, at)
        give(2, at)

    sub_blocks[...] = sent_acc[...].astype(BF).reshape(sub_blocks.shape)
    begin("sub", 0)
    sub_landed[sub] = sub_blocks[sub]

    @pl.loop(0, rows // pool_block)
    def _(n):
        happen("pool", n)

        @pl.when(n == 2)
        def _():
            finish("sub", 0)
            moved = regroup(sub_landed[...].reshape(halo, width), subs, comms, halo // (subs * comms))
            comm_blocks[...] = moved.reshape(comm_blocks.shape)
            begin("comm", 0)
            comm_landed[comm] = comm_blocks[comm]

        at = place(n, pool_block)
        pooled[at, :] = jnp.dot(own_mix[at, :], neigh[...], preferred_element_type=F32)
        give(3, at)

    finish("w0", last)
    finish("w1", last)
    finish("comm", 0)
    incoming_ref[...] = comm_landed[...].reshape(halo, width)
    q_local.wait()
    for n in range(4):
        given(n)


def gather_and_transform(features, q_weight, q_bias, w_weight, w_bias, nbr_index, nbr_count, importance, send_rows):
    comms, subs = lax.axis_size("comm"), lax.axis_size("sub")
    devices = comms * subs
    bits = devices.bit_length() - 1
    rows, width = features.shape
    fanout = nbr_index.shape[1]
    per = send_rows.shape[2]
    halo = devices * per
    block, pool_block = 256, 384
    q_rows, w_rows = q_weight.shape[0], w_weight.shape[0]
    share = q_bias.shape[0]
    targets = send_targets(send_rows, comms, subs)
    lead = (2,) * bits

    here = pl.BlockSpec(memory_space=pltpu.VMEM)
    anywhere = pl.BlockSpec(memory_space=pl.ANY)
    copies = 4 * bits + 3 * 2
    out = pl.pallas_call(
        functools.partial(
            gather_kernel, comms=comms, subs=subs, bits=bits, block=block, pool_block=pool_block
        ),
        in_specs=[here] * 8 + [anywhere],
        out_specs=[anywhere, here, anywhere, anywhere, anywhere, here, anywhere, anywhere, here],
        out_shape=[
            jax.ShapeDtypeStruct((rows, rows), BF),
            jax.ShapeDtypeStruct((rows, halo), BF),
            jax.ShapeDtypeStruct((rows, width), BF),
            jax.ShapeDtypeStruct((rows, width), BF),
            jax.ShapeDtypeStruct((rows, width), F32),
            jax.ShapeDtypeStruct((halo, width), BF),
            jax.ShapeDtypeStruct(lead + (q_rows, width), BF),
            jax.ShapeDtypeStruct(lead + (w_rows, width), BF),
            jax.ShapeDtypeStruct((8, width), F32),
        ],
        scratch_shapes=[
            pltpu.VMEM((rows, width), F32),
            pltpu.VMEM((rows, rows), BF),
            pltpu.VMEM((rows, width), BF),
            pltpu.VMEM((rows, width), BF),
            pltpu.VMEM((rows, width), BF),
            pltpu.VMEM((rows, width), F32),
            pltpu.VMEM(lead + (q_rows, width), BF),
            pltpu.VMEM((w_rows, width), BF),
            pltpu.VMEM(lead + (8, 128), F32),
            pltpu.VMEM((halo, width), F32),
            pltpu.VMEM((subs, halo // subs, width), BF),
            pltpu.VMEM((subs, halo // subs, width), BF),
            pltpu.VMEM((comms, halo // comms, width), BF),
            pltpu.VMEM((comms, halo // comms, width), BF),
            pltpu.SemaphoreType.DMA((6,)),
            pltpu.SemaphoreType.DMA((rows // block,)),
            pltpu.SemaphoreType.DMA((copies,)),
            pltpu.SemaphoreType.DMA((copies,)),
            pltpu.SemaphoreType.DMA((subs - 1,)),
            pltpu.SemaphoreType.DMA((subs - 1,)),
            pltpu.SemaphoreType.DMA((comms - 1,)),
            pltpu.SemaphoreType.DMA((comms - 1,)),
        ],
        compiler_params=pltpu.CompilerParams(
            collective_id=0, has_side_effects=True, vmem_limit_bytes=62 * 2**20
        ),
        name="gather_and_transform",
    )(
        nbr_index.T,
        nbr_count.reshape(rows // 128, 128),
        importance.T,
        q_weight,
        w_weight,
        q_bias.reshape(1, share),
        w_bias.reshape(1, share),
        targets,
        features,
    )
    own_mix, halo_mix, low, slope, pooled_own, incoming, q_full, w_full, biases = out
    return (
        own_mix,
        halo_mix,
        low,
        slope,
        pooled_own,
        incoming,
        q_full.reshape(devices * q_rows, width),
        w_full.reshape(devices * w_rows, width),
        biases,
    )


def gather_plain(features, q_weight, q_bias, w_weight, w_bias, nbr_index, nbr_count, importance, send_rows):
    rows, width = features.shape
    devices, per_peer = send_rows.shape[1:]
    halo = devices * per_peer
    own_mix, halo_mix = build_mixing(nbr_index, nbr_count, importance, halo)
    q_full = lax.all_gather(q_weight.astype(BF), AXES, axis=0, tiled=True)
    w_full = lax.all_gather(w_weight.astype(BF), AXES, axis=0, tiled=True)
    biases = doubled(jnp.stack([q_bias, w_bias]), devices)
    qbias_full = biases[:, 0].reshape(width).astype(BF).astype(F32)
    wbias_full = biases[:, 1].reshape(width).astype(BF).astype(F32)
    low = features.astype(BF)
    neigh, slope = gelu_pair(jnp.dot(low, q_full, preferred_element_type=F32) + qbias_full)
    neigh = neigh.astype(BF)
    sent = neigh[send_rows[0]]
    incoming = lax.all_to_all(sent, AXES, split_axis=0, concat_axis=0, tiled=True).reshape(halo, width)
    pooled_own = pool_own(own_mix, neigh)
    biases = jnp.pad(jnp.stack([qbias_full, wbias_full]), ((0, 6), (0, 0)))
    return own_mix, halo_mix, low, slope.astype(BF), pooled_own, incoming, q_full, w_full, biases


def resident(*shape):
    return pl.BlockSpec(shape, lambda i: (0,) * len(shape), pipeline_mode=pl.Buffered(1))


def by_rows(*shape):
    return pl.BlockSpec(shape, lambda i: (i,) + (0,) * (len(shape) - 1))


def product_kernel(mix_ref, table_ref, out_ref):
    out_ref[...] = jnp.dot(mix_ref[...], table_ref[...], preferred_element_type=F32)


def pool_own(own_mix, neigh):
    rows, width = neigh.shape
    block = 384
    return pl.pallas_call(
        product_kernel,
        grid=(rows // block,),
        in_specs=[by_rows(block, rows), resident(rows, width)],
        out_specs=by_rows(block, width),
        out_shape=jax.ShapeDtypeStruct((rows, width), F32),
        compiler_params=pltpu.CompilerParams(vmem_limit_bytes=40 * 2**20),
        cost_estimate=pl.CostEstimate(
            flops=2 * rows * rows * width, bytes_accessed=2 * rows * rows + 6 * rows * width, transcendentals=0
        ),
        name="pool_own",
    )(own_mix, neigh)


def combine_kernel(
    own_ref,
    halo_ref,
    incoming_ref,
    low_ref,
    w_ref,
    bias_ref,
    cotangent_ref,
    embedding_ref,
    pooled_ref,
    grad_ref,
    grad_pooled_ref,
    sent_ref,
    bias_grad_ref,
    act_buf,
    slope_buf,
):
    i = pl.program_id(0)
    block, width = low_ref.shape
    chunk = 256

    @pl.when(i == 0)
    def _():
        sent_ref[...] = jnp.zeros_like(sent_ref)
        bias_grad_ref[...] = jnp.zeros_like(bias_grad_ref)

    pooled = own_ref[...] + jnp.dot(halo_ref[...], incoming_ref[...], preferred_element_type=F32)
    pooled_ref[...] = pooled.astype(BF)
    squares = jnp.zeros((block, 128), F32)
    dots = jnp.zeros((block, 128), F32)
    for c in range(0, width, chunk):
        at = slice(c, c + chunk)
        pre = jnp.dot(low_ref[...], w_ref[:width, at], preferred_element_type=F32)
        pre += jnp.dot(pooled_ref[...], w_ref[width:, at], preferred_element_type=F32)
        act, slope = gelu_pair(pre + bias_ref[1:2, at])
        act_buf[:, at] = act
        slope_buf[:, at] = slope
        square = act * act
        dot = act * cotangent_ref[:, at]
        for k in range(0, chunk, 128):
            squares += square[:, k : k + 128]
            dots += dot[:, k : k + 128]
    scale = lax.rsqrt(jnp.sum(squares, axis=1, keepdims=True) * (1.0 / width) + 1e-06)
    pull = jnp.sum(dots, axis=1, keepdims=True) * (1.0 / width) * scale * scale * scale
    for c in range(0, width, chunk):
        at = slice(c, c + chunk)
        act = act_buf[:, at]
        embedding_ref[:, at] = act * scale
        grad = slope_buf[:, at] * (cotangent_ref[:, at] * scale - act * pull)
        grad_ref[:, at] = grad.astype(BF)
        bias_grad_ref[0:1, at] += jnp.sum(grad_ref[:, at].astype(F32), axis=0, keepdims=True)
    for c in range(0, width, chunk):
        at = slice(c, c + chunk)
        back = lax.dot_general(
            grad_ref[...],
            w_ref[width + c : width + c + chunk, :],
            (((1,), (1,)), ((), ())),
            preferred_element_type=F32,
        )
        grad_pooled_ref[:, at] = back.astype(BF)
    sent_ref[...] += lax.dot_general(
        halo_ref[...], grad_pooled_ref[...], (((0,), (0,)), ((), ())), preferred_element_type=F32
    )


def combine(pooled_own, halo_mix, incoming, low, w_full, biases, cotangent):
    rows, width = low.shape
    halo = incoming.shape[0]
    block = 768
    return pl.pallas_call(
        combine_kernel,
        grid=(rows // block,),
        in_specs=[
            by_rows(block, width),
            by_rows(block, halo),
            resident(halo, width),
            by_rows(block, width),
            resident(2 * width, width),
            resident(8, width),
            by_rows(block, width),
        ],
        out_specs=[
            by_rows(block, width),
            by_rows(block, width),
            by_rows(block, width),
            by_rows(block, width),
            pl.BlockSpec((halo, width), lambda i: (0, 0)),
            pl.BlockSpec((8, width), lambda i: (0, 0)),
        ],
        out_shape=[
            jax.ShapeDtypeStruct((rows, width), F32),
            jax.ShapeDtypeStruct((rows, width), BF),
            jax.ShapeDtypeStruct((rows, width), BF),
            jax.ShapeDtypeStruct((rows, width), BF),
            jax.ShapeDtypeStruct((halo, width), F32),
            jax.ShapeDtypeStruct((8, width), F32),
        ],
        scratch_shapes=[pltpu.VMEM((block, width), F32), pltpu.VMEM((block, width), F32)],
        compiler_params=pltpu.CompilerParams(vmem_limit_bytes=62 * 2**20),
        cost_estimate=pl.CostEstimate(
            flops=6 * rows * width * width, bytes_accessed=22 * rows * width, transcendentals=rows * width
        ),
        name="combine",
    )(pooled_own, halo_mix, incoming, low, w_full, biases, cotangent)


def swap(x, bit, devices):
    return lax.ppermute(x, AXES, [(i, i ^ (1 << bit)) for i in range(devices)])


def doubled(x, devices):
    me = lax.axis_index(AXES)
    x = x[None]
    for bit in range(devices.bit_length() - 1):
        other = swap(x, bit, devices)
        first = ((me >> bit) & 1) == 0
        x = jnp.where(first, jnp.concatenate([x, other]), jnp.concatenate([other, x]))
    return x


def summed(x, devices):
    for bit in range(devices.bit_length() - 1):
        x = x + swap(x, bit, devices)
    return x


def halve(part, left, bit, devices):
    mine = (lax.axis_index(AXES) >> bit) & 1
    axis = left.index(bit)
    keep = lax.dynamic_index_in_dim(part, mine, axis, keepdims=False)
    sent = lax.dynamic_index_in_dim(part, 1 - mine, axis, keepdims=False)
    total = keep.astype(F32) + swap(sent, bit, devices).astype(F32)
    return total, [b for b in left if b != bit]


def scatter_sum(partial, devices):
    bits = list(range(devices.bit_length() - 1))[::-1]
    width = partial.shape[1]
    part = partial.reshape([2] * len(bits) + [-1, width])
    part, left = halve(part, bits, 0, devices)
    part = part.astype(BF)
    rows = part.shape[-2] // 2
    orders = ([1, 2] + list(range(3, len(bits))), [2, 1] + list(range(3, len(bits))))
    halves = [(part[..., :rows, :], left), (part[..., rows:, :], left)]
    for step in range(len(bits) - 1):
        for s in range(2):
            total, rest = halve(halves[s][0], halves[s][1], orders[s][step], devices)
            halves[s] = (total if len(rest) == 0 else total.astype(BF), rest)
    return jnp.concatenate([h[0] for h in halves], axis=0)


def back_plain(
    own_mix, low, slope, pooled, grad_out, grad_pooled, sent_grad, grad_wbias, q_full, w_full, send_rows
):
    rows, width = low.shape
    devices, per = send_rows.shape[1:]
    contract = (((0,), (0,)), ((), ()))
    returned = lax.all_to_all(
        sent_grad.reshape(devices, per, width), AXES, split_axis=0, concat_axis=0, tiled=True
    )
    joined = jnp.concatenate([low, pooled], axis=1)
    grad_w = lax.dot_general(joined, grad_out, contract, preferred_element_type=F32)
    grad_low = lax.dot_general(grad_out, w_full[:width], (((1,), (1,)), ((), ())), preferred_element_type=F32)
    grad_neigh = lax.dot_general(own_mix, grad_pooled, contract, preferred_element_type=F32)
    grad_neigh = grad_neigh.at[send_rows.reshape(-1)].add(returned.reshape(devices * per, width))
    grad_hidden = (slope.astype(F32) * grad_neigh).astype(BF)
    grad_q = lax.dot_general(low, grad_hidden, contract, preferred_element_type=F32)
    grad_qbias = jnp.sum(grad_hidden.astype(F32), axis=0)
    grad_features = grad_low + lax.dot_general(
        grad_hidden, q_full, (((1,), (1,)), ((), ())), preferred_element_type=F32
    )
    me = lax.axis_index(AXES)
    share = width // devices
    sums = summed(jnp.stack([grad_qbias, grad_wbias[0]]), devices)
    sums = lax.dynamic_slice_in_dim(sums, me * share, share, 1)
    return (
        grad_features,
        scatter_sum(grad_q.astype(BF), devices),
        sums[0],
        scatter_sum(grad_w.astype(BF), devices),
        sums[1],
    )


class ScatterSum:
    def __init__(self, refs, orders, mine, partner):
        self.held, self.sent, self.got, self.next_sent, self.next_got, self.send_sem, self.recv_sem = refs
        self.orders, self.mine, self.partner = orders, mine, partner
        self.bits = len(mine)
        self.lead = list(range(1, self.bits))[::-1]
        self.half = self.held.shape[-1] // 2

    def copy(self, n, source, target, b):
        return pltpu.make_async_remote_copy(
            src_ref=source,
            dst_ref=target,
            send_sem=self.send_sem.at[n],
            recv_sem=self.recv_sem.at[n],
            device_id=self.partner(b),
            device_id_type=pl.DeviceIdType.MESH,
        )

    def first(self, top):
        return self.copy(top, self.sent.at[self.top_index(top)], self.got.at[self.top_index(top)], 0)

    def top_index(self, top):
        return ((top // 2) % 2, top % 2)

    def later(self, k, h):
        n = 4 + 2 * (k - 1) + h
        at = (h, slice(self.offset(k), self.offset(k) + (1 << (self.bits - 1 - k))))
        return self.copy(n, self.next_sent.at[at], self.next_got.at[at], self.orders[h][k - 1])

    def offset(self, k):
        return (1 << (self.bits - 1)) - (1 << (self.bits - k))

    def spot(self, chosen):
        return tuple(chosen[b] for b in self.lead)

    def absorb(self, k, halves):
        for h in halves:
            order = self.orders[h]
            fixed = order[:k]
            free = [b for b in self.lead if b not in fixed]
            columns = slice(h * self.half, (h + 1) * self.half)

            def total(chosen, h=h, free=free, columns=columns):
                at = self.spot(chosen)
                if k == 0:
                    came = self.got[at + (slice(None), columns)]
                else:
                    place = self.offset(k)
                    for p, b in enumerate(free[::-1]):
                        place = place + chosen[b] * (1 << p)
                    came = self.next_got[h, place]
                return at, self.held[at + (slice(None), columns)] + came.astype(F32)

            if not free:
                at, value = total({b: self.mine[b] for b in fixed})
                self.held[at + (slice(None), columns)] = value
                continue
            split = order[k]
            others = [b for b in free if b != split]

            def body(n, carry, total=total, split=split, others=others, fixed=fixed, columns=columns, h=h):
                chosen = {b: self.mine[b] for b in fixed}
                for p, b in enumerate(others[::-1]):
                    chosen[b] = (n // (1 << p)) % 2
                chosen[split] = self.mine[split]
                at, value = total(chosen)
                self.held[at + (slice(None), columns)] = value
                chosen[split] = 1 - self.mine[split]
                _, value = total(chosen)
                self.next_sent[h, self.offset(k + 1) + n] = value.astype(BF)
                return carry

            lax.fori_loop(0, 1 << len(others), body, 0)

    def advance(self, k):
        if k == 0:
            for t in range(4):
                self.first(t).wait()
        for h in range(2):
            if k > 0:
                self.later(k, h).wait()
            self.absorb(k, [h])
            if k < self.bits - 1:
                self.later(k + 1, h).start()

    def result(self):
        return self.held[self.spot({b: self.mine[b] for b in self.lead})]


def back_body(
    sent_grad_ref,
    w_bias_ref,
    target_ref,
    mix_hbm,
    slope_hbm,
    low_hbm,
    pooled_hbm,
    out_hbm,
    grad_pooled_hbm,
    w_hbm,
    q_hbm,
    features_out,
    q_out,
    w_out,
    bias_out,
    joined,
    grad_out,
    grad_pooled,
    slope,
    w_top,
    q_full,
    mix,
    features,
    q_bias_acc,
    bias_sent,
    bias_got,
    comm_blocks,
    comm_landed,
    sub_blocks,
    sub_landed,
    *rest,
    comms,
    subs,
    bits,
    mix_block,
    row_block,
):
    sets = [rest[7 * k : 7 * k + 7] for k in range(3)]
    load_sem, mix_sem, out_sem, bias_send, bias_recv, comm_send, comm_recv, sub_send, sub_recv = rest[21:]
    rows, width = grad_out.shape
    halo = sent_grad_ref.shape[0]
    half = width // 2
    comm, sub = lax.axis_index("comm"), lax.axis_index("sub")
    me = comm * subs + sub
    mine = [(me // (1 << b)) % 2 for b in range(bits)]
    tn = (((0,), (0,)), ((), ()))
    nt = (((1,), (1,)), ((), ()))

    def partner(b):
        other = me + (1 << b) * (1 - 2 * mine[b])
        return (other // subs, other % subs)

    high = list(range(3, bits))
    orders = ([1, 2] + high, [2, 1] + high)
    w_sets = [ScatterSum(sets[k], orders, mine, partner) for k in range(2)]
    q_set = ScatterSum(sets[2], orders, mine, partner)

    left, right = pl.ds(0, half), pl.ds(half, half)
    loads = [
        (out_hbm.at[:, left], grad_out.at[:, left]),
        (low_hbm.at[:, left], joined.at[:, pl.ds(0, half)]),
        (low_hbm.at[:, right], joined.at[:, pl.ds(half, half)]),
        (pooled_hbm.at[:, left], joined.at[:, pl.ds(2 * half, half)]),
        (pooled_hbm.at[:, right], joined.at[:, pl.ds(3 * half, half)]),
        (out_hbm.at[:, right], grad_out.at[:, right]),
        (grad_pooled_hbm, grad_pooled),
        (slope_hbm, slope),
        (w_hbm.at[pl.ds(0, width), :], w_top),
        (q_hbm, q_full),
    ]
    loads = [pltpu.make_async_copy(a, b, load_sem.at[n]) for n, (a, b) in enumerate(loads)]
    comm_ring = ring_copies(comms, comm, comm_blocks, comm_landed, comm_send, comm_recv, lambda j: (j, sub))
    sub_ring = ring_copies(subs, sub, sub_blocks, sub_landed, sub_send, sub_recv, lambda j: (comm, j))
    bias_copies = [
        pltpu.make_async_remote_copy(
            src_ref=bias_sent.at[b],
            dst_ref=bias_got.at[b],
            send_sem=bias_send.at[b],
            recv_sem=bias_recv.at[b],
            device_id=partner(b),
            device_id_type=pl.DeviceIdType.MESH,
        )
        for b in range(bits)
    ]

    spreads = rows // mix_block
    rounds = rows // row_block

    def mix_copy(n):
        at = pl.ds(pl.multiple_of(n * mix_block, mix_block), mix_block)
        return pltpu.make_async_copy(mix_hbm.at[:, at], mix.at[n % 2], mix_sem.at[n % 2])

    def out_copy(n):
        at = pl.ds(pl.multiple_of(n * row_block, row_block), row_block)
        return pltpu.make_async_copy(features.at[n % 2], features_out.at[at, :], out_sem.at[n % 2])

    def deal(value, which, top, rows_each):
        keep_even = mine[0] == 0
        shares = value.shape[0] // rows_each
        for p in range(shares // 2):
            even = value[2 * p * rows_each : (2 * p + 1) * rows_each]
            odd = value[(2 * p + 1) * rows_each : (2 * p + 2) * rows_each]
            at = top + tuple((p >> b) & 1 for b in range(bits - 2, -1, -1))[len(top) :]
            which.held[at] = jnp.where(keep_even, even, odd)
            which.sent[at] = jnp.where(keep_even, odd, even).astype(BF)

    def w_top_bits(j):
        return ((j // 2) % 2, j % 2)

    events = {
        ("w1", 1): [(0, 0)],
        ("spread", 1): [(1, 0), (0, 1)],
        ("spread", 3): [(0, 2)],
        ("spread", 4): [(1, 1)],
        ("spread", 5): [(0, 3)],
        ("q", 1): [(1, 2), (0, 4)],
        ("q", 3): [(1, 3)],
        ("features", 1): [(2, 0)],
        ("features", 3): [(1, 4)],
        ("features", 5): [(2, 1)],
    }
    all_sets = w_sets + [q_set]

    def happen(phase, n):
        for (when, step), which in events.items():
            if when == phase:

                @pl.when(n == step)
                def _(which=which):
                    for m, k in which:
                        all_sets[m].advance(k)

    def load_when(step, n, begin=(), need=()):
        @pl.when(n == step)
        def _():
            for m in need:
                loads[m].wait()
            for m in begin:
                loads[m].start()

    for n in range(3):
        loads[n].start()
    comm_blocks[...] = sent_grad_ref[...].astype(BF).reshape(comm_blocks.shape)
    q_bias_acc[...] = jnp.zeros_like(q_bias_acc)
    greet(comm, sub, comms, subs)
    for c in comm_ring:
        c.start()
    comm_landed[comm] = comm_blocks[comm]

    for n in range(2):

        @pl.loop(0, 4)
        def _(j, n=n):
            if n == 0:
                load_when(0, j, [3], [0, 1])
                load_when(1, j, [4], [2])
                load_when(2, j, [5], [3])
                load_when(3, j, [6], [4])
            else:
                load_when(0, j, [7], [5])
                load_when(1, j, [8])
                load_when(2, j, [9])

                @pl.when(j == 3)
                def _():
                    mix_copy(0).start()

            at = pl.ds(pl.multiple_of(j * half, half), half)
            columns = slice(n * half, (n + 1) * half)
            value = lax.dot_general(joined[:, at], grad_out[:, columns], tn, preferred_element_type=F32)
            deal(value, w_sets[n], w_top_bits(j), w_out.shape[0])
            w_sets[n].first(j).start()
            happen("w" + str(n), j)

        if n == 0:
            for c in comm_ring:
                c.wait()
            moved = regroup(comm_landed[...].reshape(halo, width), comms, subs, halo // (subs * comms))
            sub_blocks[...] = moved.reshape(sub_blocks.shape)
            for c in sub_ring:
                c.start()
            sub_landed[sub] = sub_blocks[sub]

    for c in sub_ring:
        c.wait()
    for n in (6, 7):
        loads[n].wait()

    @pl.loop(0, spreads)
    def _(n):
        @pl.when(n + 1 < spreads)
        def _():
            mix_copy(n + 1).start()

        happen("spread", n)
        mix_copy(n).wait()
        start = n * mix_block
        at = pl.ds(pl.multiple_of(start, mix_block), mix_block)
        local = lax.broadcasted_iota(jnp.int32, (mix_block, halo), 0) + start
        chosen = jnp.where(local == target_ref[...], 1.0, 0.0).astype(BF)
        back = lax.dot_general(mix[n % 2], grad_pooled[...], tn, preferred_element_type=F32)
        back += jnp.dot(chosen, sub_landed[...].reshape(halo, width), preferred_element_type=F32)
        grad = (back * slope[at, :].astype(F32)).astype(BF)
        joined[at, width:] = grad
        q_bias_acc[0:1, :] += jnp.sum(grad.astype(F32), axis=0, keepdims=True)

    def bias_step(b):
        if b:
            bias_copies[b - 1].wait()
            total = bias_sent[b - 1] + bias_got[b - 1]
            if b == bits:
                bias_out[...] = total
                return
            bias_sent[b] = total
        bias_copies[b].start()

    pieces = [w_bias_ref[0:1, c : c + 128] for c in range(0, width, 128)]
    pieces += [q_bias_acc[0:1, c : c + 128] for c in range(0, width, 128)]
    bias_sent[0] = jnp.concatenate(pieces, axis=0)

    for t in range(4):
        bias_step(t)
        n, j = t % 2, t // 2
        value = lax.dot_general(
            joined[:, j * half : (j + 1) * half],
            joined[:, width + n * half : width + (n + 1) * half],
            tn,
            preferred_element_type=F32,
        )
        keep_even = mine[0] == 0
        columns = slice(n * half, (n + 1) * half)
        each = q_out.shape[0]
        for p in range(half // each // 2):
            even = value[2 * p * each : (2 * p + 1) * each]
            odd = value[(2 * p + 1) * each : (2 * p + 2) * each]
            at = (j, (p >> 2) & 1, (p >> 1) & 1, p & 1, slice(None), columns)
            q_set.held[at] = jnp.where(keep_even, even, odd)
            q_set.sent[at] = jnp.where(keep_even, odd, even).astype(BF)
        if n == 1:
            q_set.first(2 * j).start()
            q_set.first(2 * j + 1).start()
        for m, k in events.get(("q", t), []):
            all_sets[m].advance(k)
    bias_step(4)
    for n in (8, 9):
        loads[n].wait()

    @pl.loop(0, rounds)
    def _(n):
        happen("features", n)

        @pl.when(n >= 2)
        def _():
            out_copy(n - 2).wait()

        at = pl.ds(pl.multiple_of(n * row_block, row_block), row_block)
        value = lax.dot_general(grad_out[at, :], w_top[...], nt, preferred_element_type=F32)
        features[n % 2] = value + lax.dot_general(
            joined[at, width:], q_full[...], nt, preferred_element_type=F32
        )
        out_copy(n).start()

    for k in range(2, bits):
        q_set.advance(k)
    for n in range(2):
        w_out[:, n * half : (n + 1) * half] = w_sets[n].result()
    q_out[...] = q_set.result()
    bias_step(bits)
    for n in range(rounds - 2, rounds):
        out_copy(n).wait()


def settle_kernel(source_ref, target_ref):
    target_ref[...] = source_ref[...]


def settle(x):
    rows, width = x.shape
    block = 384
    return pl.pallas_call(
        settle_kernel,
        grid=(rows // block,),
        in_specs=[by_rows(block, width)],
        out_specs=by_rows(block, width),
        out_shape=jax.ShapeDtypeStruct(x.shape, x.dtype),
        compiler_params=pltpu.CompilerParams(vmem_limit_bytes=62 * 2**20),
        name="settle",
    )(x)


def back_kernel(
    own_mix, low, slope, pooled, grad_out, grad_pooled, sent_grad, grad_wbias, q_full, w_full, send_rows
):
    comms, subs = lax.axis_size("comm"), lax.axis_size("sub")
    devices = comms * subs
    bits = devices.bit_length() - 1
    rows, width = low.shape
    per = send_rows.shape[2]
    halo = devices * per
    mix_block, row_block = 384, 384
    w_rows, q_rows = w_full.shape[0] // devices, q_full.shape[0] // devices
    targets = send_targets(send_rows, comms, subs)
    lead = (2,) * (bits - 1)

    def set_scratch(rows_each, columns):
        chunks = (1 << (bits - 1)) - 1
        copies = 4 + 2 * (bits - 1)
        return [
            pltpu.VMEM(lead + (rows_each, columns), F32),
            pltpu.VMEM(lead + (rows_each, columns), BF),
            pltpu.VMEM(lead + (rows_each, columns), BF),
            pltpu.VMEM((2, chunks, rows_each, columns // 2), BF),
            pltpu.VMEM((2, chunks, rows_each, columns // 2), BF),
            pltpu.SemaphoreType.DMA((copies,)),
            pltpu.SemaphoreType.DMA((copies,)),
        ]

    here = pl.BlockSpec(memory_space=pltpu.VMEM)
    anywhere = pl.BlockSpec(memory_space=pl.ANY)
    grad_features, grad_q, grad_w, biases = pl.pallas_call(
        functools.partial(
            back_body, comms=comms, subs=subs, bits=bits, mix_block=mix_block, row_block=row_block
        ),
        in_specs=[here] * 3 + [anywhere] * 8,
        out_specs=[anywhere] + [here] * 3,
        out_shape=[
            jax.ShapeDtypeStruct((rows, width), F32),
            jax.ShapeDtypeStruct((q_rows, width), F32),
            jax.ShapeDtypeStruct((w_rows, width), F32),
            jax.ShapeDtypeStruct((16, 128), F32),
        ],
        scratch_shapes=[
            pltpu.VMEM((rows, 2 * width), BF),
            pltpu.VMEM((rows, width), BF),
            pltpu.VMEM((rows, width), BF),
            pltpu.VMEM((rows, width), BF),
            pltpu.VMEM((width, width), BF),
            pltpu.VMEM((width, width), BF),
            pltpu.VMEM((2, rows, mix_block), BF),
            pltpu.VMEM((2, row_block, width), F32),
            pltpu.VMEM((8, width), F32),
            pltpu.VMEM((bits, 16, 128), F32),
            pltpu.VMEM((bits, 16, 128), F32),
            pltpu.VMEM((comms, halo // comms, width), BF),
            pltpu.VMEM((comms, halo // comms, width), BF),
            pltpu.VMEM((subs, halo // subs, width), BF),
            pltpu.VMEM((subs, halo // subs, width), BF),
        ]
        + set_scratch(w_rows, width // 2)
        + set_scratch(w_rows, width // 2)
        + set_scratch(q_rows, width)
        + [
            pltpu.SemaphoreType.DMA((10,)),
            pltpu.SemaphoreType.DMA((2,)),
            pltpu.SemaphoreType.DMA((2,)),
            pltpu.SemaphoreType.DMA((bits,)),
            pltpu.SemaphoreType.DMA((bits,)),
            pltpu.SemaphoreType.DMA((comms - 1,)),
            pltpu.SemaphoreType.DMA((comms - 1,)),
            pltpu.SemaphoreType.DMA((subs - 1,)),
            pltpu.SemaphoreType.DMA((subs - 1,)),
        ],
        compiler_params=pltpu.CompilerParams(
            collective_id=1, has_side_effects=True, vmem_limit_bytes=62 * 2**20
        ),
        name="back",
    )(sent_grad, grad_wbias, targets, own_mix, slope, low, pooled, grad_out, grad_pooled, w_full, q_full)
    share = width // devices
    sums = lax.dynamic_slice_in_dim(biases.reshape(2, width), lax.axis_index(AXES) * share, share, 1)
    return settle(grad_features), grad_q, sums[1], grad_w, sums[0]


def shards(
    features,
    q_weight,
    q_bias,
    w_weight,
    w_bias,
    nbr_index,
    nbr_count,
    importance,
    send_rows,
    cotangent,
):
    devices = lax.axis_size(AXES)
    kernel_fits = devices == 32 and q_weight.shape[0] % 16 == 0
    gather, back = (gather_and_transform, back_kernel) if kernel_fits else (gather_plain, back_plain)
    own_mix, halo_mix, low, slope, pooled_own, incoming, q_full, w_full, biases = gather(
        features, q_weight, q_bias, w_weight, w_bias, nbr_index, nbr_count, importance, send_rows
    )
    embedding, pooled, grad_out, grad_pooled, sent_grad, grad_wbias = combine(
        pooled_own, halo_mix, incoming, low, w_full, biases, cotangent
    )
    grad_features, grad_q, grad_qbias, grad_w, grad_wbias = back(
        own_mix, low, slope, pooled, grad_out, grad_pooled, sent_grad, grad_wbias, q_full, w_full, send_rows
    )
    return embedding, grad_features, grad_q, grad_qbias, grad_w, grad_wbias


def solution(mesh):
    in_specs = (
        P(("comm", "sub"), None),
        P(("comm", "sub"), None),
        P(("comm", "sub")),
        P(("comm", "sub"), None),
        P(("comm", "sub")),
        P(("comm", "sub"), None),
        P(("comm", "sub")),
        P(("comm", "sub"), None),
        P(("comm", "sub"), None, None),
        P(("comm", "sub"), None),
    )
    out_specs = (
        P(("comm", "sub"), None),
        P(("comm", "sub"), None),
        P(("comm", "sub"), None),
        P(("comm", "sub")),
        P(("comm", "sub"), None),
        P(("comm", "sub")),
    )
    return jax.shard_map(shards, mesh=mesh, in_specs=in_specs, out_specs=out_specs, check_vma=False)
```

```python
import functools
import math

import jax
import jax.numpy as jnp
from jax import lax
from jax.experimental import pallas as pl
from jax.experimental.pallas import tpu as pltpu
from jax.sharding import PartitionSpec as P

BF = jnp.bfloat16
F32 = jnp.float32
AXES = ("comm", "sub")


def build_rows(index_ref, counts, importance_ref, own_ref, halo_ref, first, *, rows, halo):
    his = (rows + halo + 255) // 256
    pairs = (his + 1) // 2
    fanout = index_ref.shape[0]
    at = pl.ds(pl.multiple_of(first, 128), 128)
    lane = lax.broadcasted_iota(jnp.int32, (16, 128), 1)
    sublane = lax.broadcasted_iota(jnp.int32, (16, 128), 0)
    parity = (sublane >= 8).astype(jnp.int32)
    half = (lane >= 64).astype(jnp.int32)
    los = lax.broadcasted_iota(jnp.int32, (64, 256), 1).astype(BF)
    left = lax.broadcasted_iota(jnp.int32, (1, 128), 1) < 64
    hi_pattern = [(2 * t + parity).astype(BF) for t in range(pairs)]
    row_mask = [(sublane & 7) == 2 * c + half for c in range(4)]
    zero = jnp.zeros((), BF)
    one = jnp.ones((), BF)

    def slots(x):
        return jnp.concatenate([x, jnp.zeros((64 - fanout, 128), F32)], axis=0)

    def by_row(x):
        x = slots(x).T
        return jnp.concatenate([x, x], axis=1)

    index = index_ref[:, at]
    slot = lax.broadcasted_iota(jnp.int32, index.shape, 0)
    weight = jnp.where(slot < counts, importance_ref[:, at], 0.0)
    alpha = by_row(weight / jnp.sum(weight, axis=0, keepdims=True))
    hi = by_row((index >> 8).astype(F32))
    lo = slots((index & 255).astype(F32)).astype(BF)
    for g in range(0, 128, 16):
        tiles = []
        for s in range(2):
            left_parts, right_parts = [], []
            for c in range(4):
                r = g + s * 8 + 2 * c

                def pick(x):
                    return jnp.where(left, x[r : r + 1, :], x[r + 1 : r + 2, :]).astype(BF)

                kept = jnp.where(row_mask[c], jnp.broadcast_to(pick(alpha), (16, 128)), zero)
                hi_row = jnp.broadcast_to(pick(hi), (16, 128))
                left_parts.append(
                    jnp.concatenate(
                        [jnp.where(hi_row == hi_pattern[t], kept, zero) for t in range(pairs)], axis=0
                    )
                )
                for q in (r, r + 1):
                    right_parts.append(jnp.where(jnp.broadcast_to(lo[:, q : q + 1], (64, 256)) == los, one, zero))
            tiles.append(
                jnp.dot(
                    jnp.concatenate(left_parts, axis=1),
                    jnp.concatenate(right_parts, axis=0),
                    preferred_element_type=F32,
                )
            )
        for h in range(his):
            tile = jnp.concatenate([t[h * 8 : (h + 1) * 8, :] for t in tiles], axis=0).astype(BF)
            to = pl.ds(pl.multiple_of(first + g, 16), 16)
            if h * 256 < rows:
                own_ref[to, h * 256 : (h + 1) * 256] = tile
            else:
                start = h * 256 - rows
                stop = min(start + 256, halo)
                halo_ref[to, start:stop] = tile[:, : stop - start]


def build_kernel(index_ref, count_ref, importance_ref, own_ref, halo_ref, *, rows, halo):
    for first in range(0, own_ref.shape[0], 128):
        counts = count_ref[:, first : first + 128]
        build_rows(index_ref, counts, importance_ref, own_ref, halo_ref, first, rows=rows, halo=halo)


def build_mixing(nbr_index, nbr_count, importance, halo):
    rows, fanout = nbr_index.shape
    block = 256
    return pl.pallas_call(
        functools.partial(build_kernel, rows=rows, halo=halo),
        grid=(rows // block,),
        in_specs=[
            pl.BlockSpec((fanout, block), lambda i: (0, i)),
            pl.BlockSpec((1, block), lambda i: (0, i)),
            pl.BlockSpec((fanout, block), lambda i: (0, i)),
        ],
        out_specs=[
            pl.BlockSpec((block, rows), lambda i: (i, 0)),
            pl.BlockSpec((block, halo), lambda i: (i, 0)),
        ],
        out_shape=[
            jax.ShapeDtypeStruct((rows, rows), BF),
            jax.ShapeDtypeStruct((rows, halo), BF),
        ],
        compiler_params=pltpu.CompilerParams(vmem_limit_bytes=40 * 2**20),
        name="build_mixing",
    )(nbr_index.T, nbr_count.reshape(1, rows), importance.T)


def gelu_pair(x):
    c = math.sqrt(2.0 / math.pi)
    square = x * x
    half = 0.5 + 0.5 * jnp.tanh(x * (c + (c * 0.044715) * square))
    value = x * half
    return value, half + value * (1.0 - half) * (2.0 * c + (6.0 * c * 0.044715) * square)


def hidden_rows(features_ref, q_buf, bias_ref, send_ref, low_ref, neigh_ref, slope_ref, sent_ref, at_rows, start):
    width = features_ref.shape[1]
    lead = (slice(None),) * (len(q_buf.shape) - 1)
    low_ref[at_rows, :] = features_ref[at_rows, :].astype(BF)
    for c in range(0, width, 256):
        at = slice(c, c + 256)
        q = q_buf[lead + (at,)].reshape(width, 256)
        pre = jnp.dot(low_ref[at_rows, :], q, preferred_element_type=F32) + bias_ref[0:1, at]
        value, slope = gelu_pair(pre)
        neigh_ref[at_rows, at] = value.astype(BF)
        slope_ref[at_rows, at] = slope.astype(BF)
    neigh = neigh_ref[at_rows, :]
    local = lax.broadcasted_iota(jnp.int32, (neigh.shape[0], send_ref.shape[1]), 0) + start
    chosen = jnp.where(local == send_ref[...], 1.0, 0.0).astype(BF)
    sent_ref[...] += lax.dot_general(chosen, neigh, (((0,), (0,)), ((), ())), preferred_element_type=F32)


def ring_copies(groups, index, blocks_ref, landed_ref, send_sem, recv_sem, device_of):
    copies = []
    for k in range(1, groups):
        other = (index + k) % groups
        copies.append(
            pltpu.make_async_remote_copy(
                src_ref=blocks_ref.at[other],
                dst_ref=landed_ref.at[index],
                send_sem=send_sem.at[k - 1],
                recv_sem=recv_sem.at[k - 1],
                device_id=device_of(other),
                device_id_type=pl.DeviceIdType.MESH,
            )
        )
    return copies


def regroup(x, outer, inner, per):
    count = x.shape[0]
    to = lax.broadcasted_iota(jnp.int32, (count, count), 0)
    place = lax.broadcasted_iota(jnp.int32, (count, count), 1)
    source = ((to // per) % outer) * (inner * per) + (to // (per * outer)) * per + to % per
    chosen = jnp.where(place == source, 1.0, 0.0).astype(BF)
    return jnp.dot(chosen, x, preferred_element_type=F32).astype(BF)


def greet(comm, sub, comms, subs):
    barrier = pltpu.get_barrier_semaphore()
    for k in range(1, comms):
        pl.semaphore_signal(
            barrier, inc=1, device_id=((comm + k) % comms, sub), device_id_type=pl.DeviceIdType.MESH
        )
    for k in range(1, subs):
        pl.semaphore_signal(
            barrier, inc=1, device_id=(comm, (sub + k) % subs), device_id_type=pl.DeviceIdType.MESH
        )
    pl.semaphore_wait(barrier, comms + subs - 2)


def send_targets(send_rows, comms, subs):
    per = send_rows.shape[2]
    return send_rows.reshape(comms, subs, per).transpose(1, 0, 2).reshape(1, comms * subs * per)


def gather_kernel(
    index_ref,
    count_ref,
    importance_ref,
    q_ref,
    w_ref,
    q_bias_ref,
    w_bias_ref,
    send_ref,
    features_hbm,
    own_out,
    halo_ref,
    low_out,
    slope_out,
    pooled_out,
    q_full,
    w_full,
    bias_out,
    features,
    own_mix,
    low,
    neigh,
    slope,
    pooled,
    pooled_low,
    q_buf,
    w_own,
    bias_buf,
    sent_acc,
    sub_blocks,
    sub_landed,
    comm_blocks,
    comm_landed,
    local_sem,
    feature_sem,
    send_sem,
    recv_sem,
    sub_send,
    sub_recv,
    comm_send,
    comm_recv,
    *,
    comms,
    subs,
    bits,
    block,
    pool_block,
):
    rows = own_mix.shape[0]
    halo = halo_ref.shape[1]
    width = neigh.shape[1]
    comm, sub = lax.axis_index("comm"), lax.axis_index("sub")
    me = comm * subs + sub
    mine = [(me // (1 << b)) % 2 for b in range(bits)]
    order = list(range(bits))[::-1]

    def partner(b):
        other = me + (1 << b) * (1 - 2 * mine[b])
        return (other // subs, other % subs)

    def spot(done, part=slice(None), columns=slice(None)):
        lead = tuple(slice(None) if b in done else mine[b] for b in order)
        return lead + (part, columns)

    high = list(range(3, bits))[::-1]
    left, right = pl.ds(0, width // 2), pl.ds(width // 2, width // 2)
    count = [0]

    def exchange(buf, b, done, part=slice(None), columns=slice(None), source=None):
        at = buf.at[spot(done, part, columns)]
        n = count[0]
        count[0] += 1
        return pltpu.make_async_remote_copy(
            src_ref=at if source is None else source,
            dst_ref=at,
            send_sem=send_sem.at[n],
            recv_sem=recv_sem.at[n],
            device_id=partner(b),
            device_id_type=pl.DeviceIdType.MESH,
        )

    def chain(buf, own, split, part=slice(None)):
        groups = []
        done = []
        for b in high:
            groups.append([exchange(buf, b, done, part, source=own if not done else None)])
            done = done + [b]
        if split:
            groups.append([exchange(buf, 1, done, part, left), exchange(buf, 2, done, part, right)])
            groups.append(
                [exchange(buf, 2, done + [1], part, left), exchange(buf, 1, done + [2], part, right)]
            )
        else:
            groups.append([exchange(buf, 1, done)])
            groups.append([exchange(buf, 2, done + [1])])
        groups.append([exchange(buf, 0, done + [1, 2], part)])
        return groups

    w_rows = w_own.shape[0]
    top, bottom = pl.ds(0, w_rows // 2), pl.ds(w_rows // 2, w_rows // 2)
    chains = {
        "q": chain(q_buf, None, True),
        "bias": chain(bias_buf, None, False),
        "w0": chain(w_full, w_own.at[top], True, top),
        "w1": chain(w_full, w_own.at[bottom], True, bottom),
        "sub": [ring_copies(subs, sub, sub_blocks, sub_landed, sub_send, sub_recv, lambda j: (comm, j))],
        "comm": [ring_copies(comms, comm, comm_blocks, comm_landed, comm_send, comm_recv, lambda j: (j, sub))],
    }
    w_local = pltpu.make_async_copy(w_own, w_full.at[spot([])], local_sem.at[0])
    q_local = pltpu.make_async_copy(q_buf, q_full, local_sem.at[1])
    last = len(chains["q"]) - 1

    def begin(name, n):
        for c in chains[name][n]:
            c.start()

    def finish(name, n):
        for c in chains[name][n]:
            c.wait()

    def place(n, size):
        return pl.ds(pl.multiple_of(n * size, size), size)

    def feature_copy(n):
        at = place(n, block)
        return pltpu.make_async_copy(features_hbm.at[at, :], features.at[at, :], feature_sem.at[n])

    outs = [(own_mix, own_out), (low, low_out), (slope, slope_out), (pooled_low, pooled_out)]

    def give(n, at):
        source, target = outs[n]
        pltpu.make_async_copy(source.at[at, :], target.at[at, :], local_sem.at[2 + n]).start()

    def given(n):
        pltpu.make_async_copy(*outs[n], local_sem.at[2 + n]).wait()

    events = {
        ("build", 4): [("q", 0), ("bias", 0)],
        ("build", 6): [("w0", -1)],
        ("build", 7): [("q", 1), ("bias", 1)],
        ("build", 9): [("w1", -1)],
        ("build", 10): [("q", 2), ("bias", 2), ("w0", 0)],
        ("build", 13): [("w1", 0)],
        ("build", 14): [("w0", 1)],
        ("build", 15): [("q", 3), ("bias", 3)],
        ("hidden", 0): [("w1", 1)],
        ("hidden", 1): [("w0", 2)],
        ("hidden", 6): [("w0", 3), ("w1", 2)],
        ("pool", 2): [("w1", 3)],
    }

    def happen(phase, n):
        for (when, step), names in events.items():
            if when == phase:

                @pl.when(n == step)
                def _(names=names):
                    for name, k in names:
                        if k >= 0:
                            finish(name, k)
                        begin(name, k + 1)

    q_buf[spot([])] = q_ref[...].astype(BF)
    w_own[...] = w_ref[...].astype(BF)
    share = q_bias_ref.shape[1]
    bias_own = jnp.concatenate(
        [q_bias_ref[...], w_bias_ref[...], jnp.zeros((1, 128 - 2 * share), F32)], axis=1
    )
    bias_buf[spot([])] = jnp.broadcast_to(bias_own, (8, 128))
    greet(comm, sub, comms, subs)
    begin("q", 0)
    begin("bias", 0)
    w_local.start()
    sent_acc[...] = jnp.zeros_like(sent_acc)
    w_local.wait()

    @pl.loop(0, rows // block)
    def _(n):
        feature_copy(n).start()

    @pl.loop(0, rows // 128)
    def _(n):
        happen("build", n)
        build_rows(
            index_ref,
            count_ref[pl.ds(n, 1), :],
            importance_ref,
            own_mix,
            halo_ref,
            n * 128,
            rows=rows,
            halo=halo,
        )
        give(0, place(n, 128))

    finish("q", last)
    finish("bias", last)
    q_local.start()
    for k in range(2):
        pieces = []
        for e in range(1 << bits):
            piece = bias_buf[tuple((e >> b) & 1 for b in order)]
            pieces.append(piece[0:1, k * share : (k + 1) * share])
        bias_out[k : k + 1, :] = jnp.concatenate(pieces, axis=1).astype(BF).astype(F32)
    bias_out[2:, :] = jnp.zeros((6, width), F32)

    @pl.loop(0, rows // block)
    def _(n):
        happen("hidden", n)
        feature_copy(n).wait()
        at = place(n, block)
        hidden_rows(features, q_buf, bias_out, send_ref, low, neigh, slope, sent_acc, at, n * block)
        give(1, at)
        give(2, at)

    sub_blocks[...] = sent_acc[...].astype(BF).reshape(sub_blocks.shape)
    begin("sub", 0)
    sub_landed[sub] = sub_blocks[sub]

    @pl.loop(0, rows // pool_block)
    def _(n):
        happen("pool", n)

        @pl.when(n == 2)
        def _():
            finish("sub", 0)
            moved = regroup(sub_landed[...].reshape(halo, width), subs, comms, halo // (subs * comms))
            comm_blocks[...] = moved.reshape(comm_blocks.shape)
            begin("comm", 0)
            comm_landed[comm] = comm_blocks[comm]

        at = place(n, pool_block)
        pooled[at, :] = jnp.dot(own_mix[at, :], neigh[...], preferred_element_type=F32)

    finish("comm", 0)

    @pl.loop(0, rows // pool_block)
    def _(n):
        at = place(n, pool_block)
        received = comm_landed[...].reshape(halo, width)
        total = pooled[at, :] + jnp.dot(halo_ref[at, :], received, preferred_element_type=F32)
        pooled_low[at, :] = total.astype(BF)
        give(3, at)

    finish("w0", last)
    finish("w1", last)
    q_local.wait()
    for n in range(4):
        given(n)


def gather_and_transform(features, q_weight, q_bias, w_weight, w_bias, nbr_index, nbr_count, importance, send_rows):
    comms, subs = lax.axis_size("comm"), lax.axis_size("sub")
    devices = comms * subs
    bits = devices.bit_length() - 1
    rows, width = features.shape
    fanout = nbr_index.shape[1]
    per = send_rows.shape[2]
    halo = devices * per
    block, pool_block = 256, 384
    q_rows, w_rows = q_weight.shape[0], w_weight.shape[0]
    share = q_bias.shape[0]
    targets = send_targets(send_rows, comms, subs)
    lead = (2,) * bits

    here = pl.BlockSpec(memory_space=pltpu.VMEM)
    anywhere = pl.BlockSpec(memory_space=pl.ANY)
    copies = 4 * bits + 3 * 2
    out = pl.pallas_call(
        functools.partial(
            gather_kernel, comms=comms, subs=subs, bits=bits, block=block, pool_block=pool_block
        ),
        in_specs=[here] * 8 + [anywhere],
        out_specs=[anywhere, here, anywhere, anywhere, anywhere, anywhere, anywhere, here],
        out_shape=[
            jax.ShapeDtypeStruct((rows, rows), BF),
            jax.ShapeDtypeStruct((rows, halo), BF),
            jax.ShapeDtypeStruct((rows, width), BF),
            jax.ShapeDtypeStruct((rows, width), BF),
            jax.ShapeDtypeStruct((rows, width), BF),
            jax.ShapeDtypeStruct(lead + (q_rows, width), BF),
            jax.ShapeDtypeStruct(lead + (w_rows, width), BF),
            jax.ShapeDtypeStruct((8, width), F32),
        ],
        scratch_shapes=[
            pltpu.VMEM((rows, width), F32),
            pltpu.VMEM((rows, rows), BF),
            pltpu.VMEM((rows, width), BF),
            pltpu.VMEM((rows, width), BF),
            pltpu.VMEM((rows, width), BF),
            pltpu.VMEM((rows, width), F32),
            pltpu.VMEM((rows, width), BF),
            pltpu.VMEM(lead + (q_rows, width), BF),
            pltpu.VMEM((w_rows, width), BF),
            pltpu.VMEM(lead + (8, 128), F32),
            pltpu.VMEM((halo, width), F32),
            pltpu.VMEM((subs, halo // subs, width), BF),
            pltpu.VMEM((subs, halo // subs, width), BF),
            pltpu.VMEM((comms, halo // comms, width), BF),
            pltpu.VMEM((comms, halo // comms, width), BF),
            pltpu.SemaphoreType.DMA((6,)),
            pltpu.SemaphoreType.DMA((rows // block,)),
            pltpu.SemaphoreType.DMA((copies,)),
            pltpu.SemaphoreType.DMA((copies,)),
            pltpu.SemaphoreType.DMA((subs - 1,)),
            pltpu.SemaphoreType.DMA((subs - 1,)),
            pltpu.SemaphoreType.DMA((comms - 1,)),
            pltpu.SemaphoreType.DMA((comms - 1,)),
        ],
        compiler_params=pltpu.CompilerParams(
            collective_id=0, has_side_effects=True, vmem_limit_bytes=62 * 2**20
        ),
        name="gather_and_transform",
    )(
        nbr_index.T,
        nbr_count.reshape(rows // 128, 128),
        importance.T,
        q_weight,
        w_weight,
        q_bias.reshape(1, share),
        w_bias.reshape(1, share),
        targets,
        features,
    )
    own_mix, halo_mix, low, slope, pooled, q_full, w_full, biases = out
    return (
        own_mix,
        halo_mix,
        low,
        slope,
        pooled,
        q_full.reshape(devices * q_rows, width),
        w_full.reshape(devices * w_rows, width),
        biases,
    )


def gather_plain(features, q_weight, q_bias, w_weight, w_bias, nbr_index, nbr_count, importance, send_rows):
    rows, width = features.shape
    devices, per_peer = send_rows.shape[1:]
    halo = devices * per_peer
    own_mix, halo_mix = build_mixing(nbr_index, nbr_count, importance, halo)
    q_full = lax.all_gather(q_weight.astype(BF), AXES, axis=0, tiled=True)
    w_full = lax.all_gather(w_weight.astype(BF), AXES, axis=0, tiled=True)
    biases = doubled(jnp.stack([q_bias, w_bias]), devices)
    qbias_full = biases[:, 0].reshape(width).astype(BF).astype(F32)
    wbias_full = biases[:, 1].reshape(width).astype(BF).astype(F32)
    low = features.astype(BF)
    neigh, slope = gelu_pair(jnp.dot(low, q_full, preferred_element_type=F32) + qbias_full)
    neigh = neigh.astype(BF)
    sent = neigh[send_rows[0]]
    incoming = lax.all_to_all(sent, AXES, split_axis=0, concat_axis=0, tiled=True).reshape(halo, width)
    pooled = pool_own(own_mix, neigh) + jnp.dot(halo_mix, incoming, preferred_element_type=F32)
    biases = jnp.pad(jnp.stack([qbias_full, wbias_full]), ((0, 6), (0, 0)))
    return own_mix, halo_mix, low, slope.astype(BF), pooled.astype(BF), q_full, w_full, biases


def resident(*shape):
    return pl.BlockSpec(shape, lambda i: (0,) * len(shape), pipeline_mode=pl.Buffered(1))


def by_rows(*shape):
    return pl.BlockSpec(shape, lambda i: (i,) + (0,) * (len(shape) - 1))


def product_kernel(mix_ref, table_ref, out_ref):
    out_ref[...] = jnp.dot(mix_ref[...], table_ref[...], preferred_element_type=F32)


def pool_own(own_mix, neigh):
    rows, width = neigh.shape
    block = 384
    return pl.pallas_call(
        product_kernel,
        grid=(rows // block,),
        in_specs=[by_rows(block, rows), resident(rows, width)],
        out_specs=by_rows(block, width),
        out_shape=jax.ShapeDtypeStruct((rows, width), F32),
        compiler_params=pltpu.CompilerParams(vmem_limit_bytes=40 * 2**20),
        cost_estimate=pl.CostEstimate(
            flops=2 * rows * rows * width, bytes_accessed=2 * rows * rows + 6 * rows * width, transcendentals=0
        ),
        name="pool_own",
    )(own_mix, neigh)


def combine_kernel(
    pooled_ref,
    halo_ref,
    low_ref,
    w_ref,
    bias_ref,
    cotangent_ref,
    embedding_ref,
    grad_ref,
    grad_pooled_ref,
    sent_ref,
    bias_grad_ref,
    act_buf,
    slope_buf,
):
    i = pl.program_id(0)
    block, width = low_ref.shape
    chunk = 256

    @pl.when(i == 0)
    def _():
        sent_ref[...] = jnp.zeros_like(sent_ref)
        bias_grad_ref[...] = jnp.zeros_like(bias_grad_ref)

    squares = jnp.zeros((block, 128), F32)
    dots = jnp.zeros((block, 128), F32)
    for c in range(0, width, chunk):
        at = slice(c, c + chunk)
        pre = jnp.dot(low_ref[...], w_ref[:width, at], preferred_element_type=F32)
        pre += jnp.dot(pooled_ref[...], w_ref[width:, at], preferred_element_type=F32)
        act, slope = gelu_pair(pre + bias_ref[1:2, at])
        act_buf[:, at] = act
        slope_buf[:, at] = slope
        square = act * act
        dot = act * cotangent_ref[:, at]
        for k in range(0, chunk, 128):
            squares += square[:, k : k + 128]
            dots += dot[:, k : k + 128]
    scale = lax.rsqrt(jnp.sum(squares, axis=1, keepdims=True) * (1.0 / width) + 1e-06)
    pull = jnp.sum(dots, axis=1, keepdims=True) * (1.0 / width) * scale * scale * scale
    for c in range(0, width, chunk):
        at = slice(c, c + chunk)
        act = act_buf[:, at]
        embedding_ref[:, at] = act * scale
        grad = slope_buf[:, at] * (cotangent_ref[:, at] * scale - act * pull)
        grad_ref[:, at] = grad.astype(BF)
        bias_grad_ref[0:1, at] += jnp.sum(grad_ref[:, at].astype(F32), axis=0, keepdims=True)
    for c in range(0, width, chunk):
        at = slice(c, c + chunk)
        back = lax.dot_general(
            grad_ref[...],
            w_ref[width + c : width + c + chunk, :],
            (((1,), (1,)), ((), ())),
            preferred_element_type=F32,
        )
        grad_pooled_ref[:, at] = back.astype(BF)
    sent_ref[...] += lax.dot_general(
        halo_ref[...], grad_pooled_ref[...], (((0,), (0,)), ((), ())), preferred_element_type=F32
    )


def combine(pooled, halo_mix, low, w_full, biases, cotangent):
    rows, width = low.shape
    halo = halo_mix.shape[1]
    block = 768
    return pl.pallas_call(
        combine_kernel,
        grid=(rows // block,),
        in_specs=[
            by_rows(block, width),
            by_rows(block, halo),
            by_rows(block, width),
            resident(2 * width, width),
            resident(8, width),
            by_rows(block, width),
        ],
        out_specs=[
            by_rows(block, width),
            by_rows(block, width),
            by_rows(block, width),
            pl.BlockSpec((halo, width), lambda i: (0, 0)),
            pl.BlockSpec((8, width), lambda i: (0, 0)),
        ],
        out_shape=[
            jax.ShapeDtypeStruct((rows, width), F32),
            jax.ShapeDtypeStruct((rows, width), BF),
            jax.ShapeDtypeStruct((rows, width), BF),
            jax.ShapeDtypeStruct((halo, width), F32),
            jax.ShapeDtypeStruct((8, width), F32),
        ],
        scratch_shapes=[pltpu.VMEM((block, width), F32), pltpu.VMEM((block, width), F32)],
        compiler_params=pltpu.CompilerParams(vmem_limit_bytes=62 * 2**20),
        cost_estimate=pl.CostEstimate(
            flops=6 * rows * width * width, bytes_accessed=22 * rows * width, transcendentals=rows * width
        ),
        name="combine",
    )(pooled, halo_mix, low, w_full, biases, cotangent)


def swap(x, bit, devices):
    return lax.ppermute(x, AXES, [(i, i ^ (1 << bit)) for i in range(devices)])


def doubled(x, devices):
    me = lax.axis_index(AXES)
    x = x[None]
    for bit in range(devices.bit_length() - 1):
        other = swap(x, bit, devices)
        first = ((me >> bit) & 1) == 0
        x = jnp.where(first, jnp.concatenate([x, other]), jnp.concatenate([other, x]))
    return x


def summed(x, devices):
    for bit in range(devices.bit_length() - 1):
        x = x + swap(x, bit, devices)
    return x


def halve(part, left, bit, devices):
    mine = (lax.axis_index(AXES) >> bit) & 1
    axis = left.index(bit)
    keep = lax.dynamic_index_in_dim(part, mine, axis, keepdims=False)
    sent = lax.dynamic_index_in_dim(part, 1 - mine, axis, keepdims=False)
    total = keep.astype(F32) + swap(sent, bit, devices).astype(F32)
    return total, [b for b in left if b != bit]


def scatter_sum(partial, devices):
    bits = list(range(devices.bit_length() - 1))[::-1]
    width = partial.shape[1]
    part = partial.reshape([2] * len(bits) + [-1, width])
    part, left = halve(part, bits, 0, devices)
    part = part.astype(BF)
    rows = part.shape[-2] // 2
    orders = ([1, 2] + list(range(3, len(bits))), [2, 1] + list(range(3, len(bits))))
    halves = [(part[..., :rows, :], left), (part[..., rows:, :], left)]
    for step in range(len(bits) - 1):
        for s in range(2):
            total, rest = halve(halves[s][0], halves[s][1], orders[s][step], devices)
            halves[s] = (total if len(rest) == 0 else total.astype(BF), rest)
    return jnp.concatenate([h[0] for h in halves], axis=0)


def back_plain(
    own_mix, low, slope, pooled, grad_out, grad_pooled, sent_grad, grad_wbias, q_full, w_full, send_rows
):
    rows, width = low.shape
    devices, per = send_rows.shape[1:]
    contract = (((0,), (0,)), ((), ()))
    returned = lax.all_to_all(
        sent_grad.reshape(devices, per, width), AXES, split_axis=0, concat_axis=0, tiled=True
    )
    joined = jnp.concatenate([low, pooled], axis=1)
    grad_w = lax.dot_general(joined, grad_out, contract, preferred_element_type=F32)
    grad_low = lax.dot_general(grad_out, w_full[:width], (((1,), (1,)), ((), ())), preferred_element_type=F32)
    grad_neigh = lax.dot_general(own_mix, grad_pooled, contract, preferred_element_type=F32)
    grad_neigh = grad_neigh.at[send_rows.reshape(-1)].add(returned.reshape(devices * per, width))
    grad_hidden = (slope.astype(F32) * grad_neigh).astype(BF)
    grad_q = lax.dot_general(low, grad_hidden, contract, preferred_element_type=F32)
    grad_qbias = jnp.sum(grad_hidden.astype(F32), axis=0)
    grad_features = grad_low + lax.dot_general(
        grad_hidden, q_full, (((1,), (1,)), ((), ())), preferred_element_type=F32
    )
    me = lax.axis_index(AXES)
    share = width // devices
    sums = summed(jnp.stack([grad_qbias, grad_wbias[0]]), devices)
    sums = lax.dynamic_slice_in_dim(sums, me * share, share, 1)
    return (
        grad_features,
        scatter_sum(grad_q.astype(BF), devices),
        sums[0],
        scatter_sum(grad_w.astype(BF), devices),
        sums[1],
    )


class ScatterSum:
    def __init__(self, refs, orders, mine, partner):
        self.held, self.sent, self.got, self.next_sent, self.next_got, self.send_sem, self.recv_sem = refs
        self.orders, self.mine, self.partner = orders, mine, partner
        self.bits = len(mine)
        self.lead = list(range(1, self.bits))[::-1]
        self.half = self.held.shape[-1] // 2

    def copy(self, n, source, target, b):
        return pltpu.make_async_remote_copy(
            src_ref=source,
            dst_ref=target,
            send_sem=self.send_sem.at[n],
            recv_sem=self.recv_sem.at[n],
            device_id=self.partner(b),
            device_id_type=pl.DeviceIdType.MESH,
        )

    def first(self, top):
        return self.copy(top, self.sent.at[self.top_index(top)], self.got.at[self.top_index(top)], 0)

    def top_index(self, top):
        return ((top // 2) % 2, top % 2)

    def later(self, k, h):
        n = 4 + 2 * (k - 1) + h
        at = (h, slice(self.offset(k), self.offset(k) + (1 << (self.bits - 1 - k))))
        return self.copy(n, self.next_sent.at[at], self.next_got.at[at], self.orders[h][k - 1])

    def offset(self, k):
        return (1 << (self.bits - 1)) - (1 << (self.bits - k))

    def spot(self, chosen):
        return tuple(chosen[b] for b in self.lead)

    def absorb(self, k, halves):
        for h in halves:
            order = self.orders[h]
            fixed = order[:k]
            free = [b for b in self.lead if b not in fixed]
            columns = slice(h * self.half, (h + 1) * self.half)

            def total(chosen, h=h, free=free, columns=columns):
                at = self.spot(chosen)
                if k == 0:
                    came = self.got[at + (slice(None), columns)]
                else:
                    place = self.offset(k)
                    for p, b in enumerate(free[::-1]):
                        place = place + chosen[b] * (1 << p)
                    came = self.next_got[h, place]
                return at, self.held[at + (slice(None), columns)] + came.astype(F32)

            if not free:
                at, value = total({b: self.mine[b] for b in fixed})
                self.held[at + (slice(None), columns)] = value
                continue
            split = order[k]
            others = [b for b in free if b != split]

            def body(n, carry, total=total, split=split, others=others, fixed=fixed, columns=columns, h=h):
                chosen = {b: self.mine[b] for b in fixed}
                for p, b in enumerate(others[::-1]):
                    chosen[b] = (n // (1 << p)) % 2
                chosen[split] = self.mine[split]
                at, value = total(chosen)
                self.held[at + (slice(None), columns)] = value
                chosen[split] = 1 - self.mine[split]
                _, value = total(chosen)
                self.next_sent[h, self.offset(k + 1) + n] = value.astype(BF)
                return carry

            lax.fori_loop(0, 1 << len(others), body, 0)

    def advance(self, k):
        if k == 0:
            for t in range(4):
                self.first(t).wait()
        for h in range(2):
            if k > 0:
                self.later(k, h).wait()
            self.absorb(k, [h])
            if k < self.bits - 1:
                self.later(k + 1, h).start()

    def result(self):
        return self.held[self.spot({b: self.mine[b] for b in self.lead})]


def back_body(
    sent_grad_ref,
    w_bias_ref,
    target_ref,
    mix_hbm,
    slope_hbm,
    low_hbm,
    pooled_hbm,
    out_hbm,
    grad_pooled_hbm,
    w_hbm,
    q_hbm,
    features_out,
    q_out,
    w_out,
    bias_out,
    joined,
    grad_out,
    grad_pooled,
    slope,
    w_top,
    q_full,
    mix,
    features,
    q_bias_acc,
    bias_sent,
    bias_got,
    comm_blocks,
    comm_landed,
    sub_blocks,
    sub_landed,
    *rest,
    comms,
    subs,
    bits,
    mix_block,
    row_block,
):
    sets = [rest[7 * k : 7 * k + 7] for k in range(4)]
    load_sem, mix_sem, out_sem, bias_send, bias_recv, comm_send, comm_recv, sub_send, sub_recv = rest[28:]
    rows, width = grad_out.shape
    halo = sent_grad_ref.shape[0]
    half = width // 2
    comm, sub = lax.axis_index("comm"), lax.axis_index("sub")
    me = comm * subs + sub
    mine = [(me // (1 << b)) % 2 for b in range(bits)]
    tn = (((0,), (0,)), ((), ()))
    nt = (((1,), (1,)), ((), ()))

    def partner(b):
        other = me + (1 << b) * (1 - 2 * mine[b])
        return (other // subs, other % subs)

    high = list(range(3, bits))
    orders = ([1, 2] + high, [2, 1] + high)
    w_sets = [ScatterSum(sets[k], orders, mine, partner) for k in range(2)]
    q_sets = [ScatterSum(sets[2 + k], orders, mine, partner) for k in range(2)]

    left, right = pl.ds(0, half), pl.ds(half, half)
    loads = [
        (out_hbm.at[:, left], grad_out.at[:, left]),
        (low_hbm.at[:, left], joined.at[:, pl.ds(0, half)]),
        (low_hbm.at[:, right], joined.at[:, pl.ds(half, half)]),
        (pooled_hbm.at[:, left], joined.at[:, pl.ds(2 * half, half)]),
        (pooled_hbm.at[:, right], joined.at[:, pl.ds(3 * half, half)]),
        (out_hbm.at[:, right], grad_out.at[:, right]),
        (grad_pooled_hbm, grad_pooled),
        (slope_hbm, slope),
        (w_hbm.at[pl.ds(0, width), :], w_top),
        (q_hbm, q_full),
    ]
    loads = [pltpu.make_async_copy(a, b, load_sem.at[n]) for n, (a, b) in enumerate(loads)]
    comm_ring = ring_copies(comms, comm, comm_blocks, comm_landed, comm_send, comm_recv, lambda j: (j, sub))
    sub_ring = ring_copies(subs, sub, sub_blocks, sub_landed, sub_send, sub_recv, lambda j: (comm, j))
    bias_copies = [
        pltpu.make_async_remote_copy(
            src_ref=bias_sent.at[b],
            dst_ref=bias_got.at[b],
            send_sem=bias_send.at[b],
            recv_sem=bias_recv.at[b],
            device_id=partner(b),
            device_id_type=pl.DeviceIdType.MESH,
        )
        for b in range(bits)
    ]

    spreads = rows // mix_block
    rounds = rows // row_block

    def mix_copy(n):
        at = pl.ds(pl.multiple_of(n * mix_block, mix_block), mix_block)
        return pltpu.make_async_copy(mix_hbm.at[:, at], mix.at[n % 2], mix_sem.at[n % 2])

    def out_copy(n):
        at = pl.ds(pl.multiple_of(n * row_block, row_block), row_block)
        return pltpu.make_async_copy(features.at[n % 2], features_out.at[at, :], out_sem.at[n % 2])

    def deal(value, which, top, rows_each):
        keep_even = mine[0] == 0
        shares = value.shape[0] // rows_each
        for p in range(shares // 2):
            even = value[2 * p * rows_each : (2 * p + 1) * rows_each]
            odd = value[(2 * p + 1) * rows_each : (2 * p + 2) * rows_each]
            at = top + tuple((p >> b) & 1 for b in range(bits - 2, -1, -1))[len(top) :]
            which.held[at] = jnp.where(keep_even, even, odd)
            which.sent[at] = jnp.where(keep_even, odd, even).astype(BF)

    def w_top_bits(j):
        return ((j // 2) % 2, j % 2)

    events = {
        ("w1", 1): [(0, 0)],
        ("spread", 1): [(0, 1), (1, 0)],
        ("spread", 3): [(0, 2)],
        ("spread", 5): [(1, 1), (0, 3)],
        ("q", 1): [(0, 4)],
        ("q", 2): [(2, 0), (1, 2)],
        ("features", 0): [(3, 0)],
        ("features", 2): [(1, 3), (2, 1)],
        ("features", 4): [(3, 1), (2, 2)],
        ("features", 5): [(1, 4)],
    }
    all_sets = w_sets + q_sets

    def happen(phase, n):
        for (when, step), which in events.items():
            if when == phase:

                @pl.when(n == step)
                def _(which=which):
                    for m, k in which:
                        all_sets[m].advance(k)

    def load_when(step, n, begin=(), need=()):
        @pl.when(n == step)
        def _():
            for m in need:
                loads[m].wait()
            for m in begin:
                loads[m].start()

    for n in range(3):
        loads[n].start()
    comm_blocks[...] = sent_grad_ref[...].astype(BF).reshape(comm_blocks.shape)
    q_bias_acc[...] = jnp.zeros_like(q_bias_acc)
    greet(comm, sub, comms, subs)
    for c in comm_ring:
        c.start()
    comm_landed[comm] = comm_blocks[comm]

    for n in range(2):

        @pl.loop(0, 4)
        def _(j, n=n):
            if n == 0:
                load_when(0, j, [3], [0, 1])
                load_when(1, j, [4], [2])
                load_when(2, j, [5], [3])
                load_when(3, j, [6], [4])
            else:
                load_when(0, j, [7], [5])
                load_when(1, j, [8])
                load_when(2, j, [9])

                @pl.when(j == 3)
                def _():
                    mix_copy(0).start()

            at = pl.ds(pl.multiple_of(j * half, half), half)
            columns = slice(n * half, (n + 1) * half)
            value = lax.dot_general(joined[:, at], grad_out[:, columns], tn, preferred_element_type=F32)
            deal(value, w_sets[n], w_top_bits(j), w_out.shape[0])
            w_sets[n].first(j).start()
            happen("w" + str(n), j)

        if n == 0:
            for c in comm_ring:
                c.wait()
            moved = regroup(comm_landed[...].reshape(halo, width), comms, subs, halo // (subs * comms))
            sub_blocks[...] = moved.reshape(sub_blocks.shape)
            for c in sub_ring:
                c.start()
            sub_landed[sub] = sub_blocks[sub]

    for c in sub_ring:
        c.wait()
    for n in (6, 7):
        loads[n].wait()

    @pl.loop(0, spreads)
    def _(n):
        @pl.when(n + 1 < spreads)
        def _():
            mix_copy(n + 1).start()

        happen("spread", n)
        mix_copy(n).wait()
        start = n * mix_block
        at = pl.ds(pl.multiple_of(start, mix_block), mix_block)
        local = lax.broadcasted_iota(jnp.int32, (mix_block, halo), 0) + start
        chosen = jnp.where(local == target_ref[...], 1.0, 0.0).astype(BF)
        back = lax.dot_general(mix[n % 2], grad_pooled[...], tn, preferred_element_type=F32)
        back += jnp.dot(chosen, sub_landed[...].reshape(halo, width), preferred_element_type=F32)
        grad = (back * slope[at, :].astype(F32)).astype(BF)
        joined[at, width:] = grad
        q_bias_acc[0:1, :] += jnp.sum(grad.astype(F32), axis=0, keepdims=True)

    def bias_step(b):
        if b:
            bias_copies[b - 1].wait()
            total = bias_sent[b - 1] + bias_got[b - 1]
            if b == bits:
                bias_out[...] = total
                return
            bias_sent[b] = total
        bias_copies[b].start()

    pieces = [w_bias_ref[0:1, c : c + 128] for c in range(0, width, 128)]
    pieces += [q_bias_acc[0:1, c : c + 128] for c in range(0, width, 128)]
    bias_sent[0] = jnp.concatenate(pieces, axis=0)

    for t in range(4):
        bias_step(t)
        n, j = t // 2, t % 2
        value = lax.dot_general(
            joined[:, j * half : (j + 1) * half],
            joined[:, width + n * half : width + (n + 1) * half],
            tn,
            preferred_element_type=F32,
        )
        deal(value, q_sets[n], (j,), q_out.shape[0])
        q_sets[n].first(2 * j).start()
        q_sets[n].first(2 * j + 1).start()
        for m, k in events.get(("q", t), []):
            all_sets[m].advance(k)
    bias_step(4)
    for n in (8, 9):
        loads[n].wait()

    @pl.loop(0, rounds)
    def _(n):
        happen("features", n)

        @pl.when(n >= 2)
        def _():
            out_copy(n - 2).wait()

        at = pl.ds(pl.multiple_of(n * row_block, row_block), row_block)
        value = lax.dot_general(grad_out[at, :], w_top[...], nt, preferred_element_type=F32)
        features[n % 2] = value + lax.dot_general(
            joined[at, width:], q_full[...], nt, preferred_element_type=F32
        )
        out_copy(n).start()

    for n, k in ((1, 2), (0, 3), (1, 3), (0, 4), (1, 4)):
        q_sets[n].advance(k)
    for n in range(2):
        w_out[:, n * half : (n + 1) * half] = w_sets[n].result()
        q_out[:, n * half : (n + 1) * half] = q_sets[n].result()
    bias_step(bits)
    for n in range(rounds - 2, rounds):
        out_copy(n).wait()


def settle_kernel(source_ref, target_ref):
    target_ref[...] = source_ref[...]


def settle(x):
    rows, width = x.shape
    block = rows // 2
    return pl.pallas_call(
        settle_kernel,
        grid=(rows // block,),
        in_specs=[by_rows(block, width)],
        out_specs=by_rows(block, width),
        out_shape=jax.ShapeDtypeStruct(x.shape, x.dtype),
        compiler_params=pltpu.CompilerParams(vmem_limit_bytes=62 * 2**20),
        name="settle",
    )(x)


def back_kernel(
    own_mix, low, slope, pooled, grad_out, grad_pooled, sent_grad, grad_wbias, q_full, w_full, send_rows
):
    comms, subs = lax.axis_size("comm"), lax.axis_size("sub")
    devices = comms * subs
    bits = devices.bit_length() - 1
    rows, width = low.shape
    per = send_rows.shape[2]
    halo = devices * per
    mix_block, row_block = 384, 384
    w_rows, q_rows = w_full.shape[0] // devices, q_full.shape[0] // devices
    targets = send_targets(send_rows, comms, subs)
    lead = (2,) * (bits - 1)

    def set_scratch(rows_each, columns):
        chunks = (1 << (bits - 1)) - 1
        copies = 4 + 2 * (bits - 1)
        return [
            pltpu.VMEM(lead + (rows_each, columns), F32),
            pltpu.VMEM(lead + (rows_each, columns), BF),
            pltpu.VMEM(lead + (rows_each, columns), BF),
            pltpu.VMEM((2, chunks, rows_each, columns // 2), BF),
            pltpu.VMEM((2, chunks, rows_each, columns // 2), BF),
            pltpu.SemaphoreType.DMA((copies,)),
            pltpu.SemaphoreType.DMA((copies,)),
        ]

    here = pl.BlockSpec(memory_space=pltpu.VMEM)
    anywhere = pl.BlockSpec(memory_space=pl.ANY)
    grad_features, grad_q, grad_w, biases = pl.pallas_call(
        functools.partial(
            back_body, comms=comms, subs=subs, bits=bits, mix_block=mix_block, row_block=row_block
        ),
        in_specs=[here] * 3 + [anywhere] * 8,
        out_specs=[anywhere] + [here] * 3,
        out_shape=[
            jax.ShapeDtypeStruct((rows, width), F32),
            jax.ShapeDtypeStruct((q_rows, width), F32),
            jax.ShapeDtypeStruct((w_rows, width), F32),
            jax.ShapeDtypeStruct((16, 128), F32),
        ],
        scratch_shapes=[
            pltpu.VMEM((rows, 2 * width), BF),
            pltpu.VMEM((rows, width), BF),
            pltpu.VMEM((rows, width), BF),
            pltpu.VMEM((rows, width), BF),
            pltpu.VMEM((width, width), BF),
            pltpu.VMEM((width, width), BF),
            pltpu.VMEM((2, rows, mix_block), BF),
            pltpu.VMEM((2, row_block, width), F32),
            pltpu.VMEM((8, width), F32),
            pltpu.VMEM((bits, 16, 128), F32),
            pltpu.VMEM((bits, 16, 128), F32),
            pltpu.VMEM((comms, halo // comms, width), BF),
            pltpu.VMEM((comms, halo // comms, width), BF),
            pltpu.VMEM((subs, halo // subs, width), BF),
            pltpu.VMEM((subs, halo // subs, width), BF),
        ]
        + set_scratch(w_rows, width // 2)
        + set_scratch(w_rows, width // 2)
        + set_scratch(q_rows, width // 2)
        + set_scratch(q_rows, width // 2)
        + [
            pltpu.SemaphoreType.DMA((10,)),
            pltpu.SemaphoreType.DMA((2,)),
            pltpu.SemaphoreType.DMA((2,)),
            pltpu.SemaphoreType.DMA((bits,)),
            pltpu.SemaphoreType.DMA((bits,)),
            pltpu.SemaphoreType.DMA((comms - 1,)),
            pltpu.SemaphoreType.DMA((comms - 1,)),
            pltpu.SemaphoreType.DMA((subs - 1,)),
            pltpu.SemaphoreType.DMA((subs - 1,)),
        ],
        compiler_params=pltpu.CompilerParams(
            collective_id=1, has_side_effects=True, vmem_limit_bytes=62 * 2**20
        ),
        name="back",
    )(sent_grad, grad_wbias, targets, own_mix, slope, low, pooled, grad_out, grad_pooled, w_full, q_full)
    share = width // devices
    sums = lax.dynamic_slice_in_dim(biases.reshape(2, width), lax.axis_index(AXES) * share, share, 1)
    return settle(grad_features), grad_q, sums[1], grad_w, sums[0]


def shards(
    features,
    q_weight,
    q_bias,
    w_weight,
    w_bias,
    nbr_index,
    nbr_count,
    importance,
    send_rows,
    cotangent,
):
    devices = lax.axis_size(AXES)
    kernel_fits = devices == 32 and q_weight.shape[0] % 16 == 0
    gather, back = (gather_and_transform, back_kernel) if kernel_fits else (gather_plain, back_plain)
    own_mix, halo_mix, low, slope, pooled, q_full, w_full, biases = gather(
        features, q_weight, q_bias, w_weight, w_bias, nbr_index, nbr_count, importance, send_rows
    )
    embedding, grad_out, grad_pooled, sent_grad, grad_wbias = combine(
        pooled, halo_mix, low, w_full, biases, cotangent
    )
    grad_features, grad_q, grad_qbias, grad_w, grad_wbias = back(
        own_mix, low, slope, pooled, grad_out, grad_pooled, sent_grad, grad_wbias, q_full, w_full, send_rows
    )
    return embedding, grad_features, grad_q, grad_qbias, grad_w, grad_wbias


def solution(mesh):
    in_specs = (
        P(("comm", "sub"), None),
        P(("comm", "sub"), None),
        P(("comm", "sub")),
        P(("comm", "sub"), None),
        P(("comm", "sub")),
        P(("comm", "sub"), None),
        P(("comm", "sub")),
        P(("comm", "sub"), None),
        P(("comm", "sub"), None, None),
        P(("comm", "sub"), None),
    )
    out_specs = (
        P(("comm", "sub"), None),
        P(("comm", "sub"), None),
        P(("comm", "sub"), None),
        P(("comm", "sub")),
        P(("comm", "sub"), None),
        P(("comm", "sub")),
    )
    return jax.shard_map(shards, mesh=mesh, in_specs=in_specs, out_specs=out_specs, check_vma=False)
```

```python
import functools
import math

import jax
import jax.numpy as jnp
from jax import lax
from jax.experimental import pallas as pl
from jax.experimental.pallas import tpu as pltpu
from jax.sharding import PartitionSpec as P

BF = jnp.bfloat16
F32 = jnp.float32
AXES = ("comm", "sub")


def build_rows(index_ref, counts, importance_ref, own_ref, halo_ref, first, *, rows, halo):
    his = (rows + halo + 255) // 256
    pairs = (his + 1) // 2
    fanout = index_ref.shape[0]
    at = pl.ds(pl.multiple_of(first, 128), 128)
    lane = lax.broadcasted_iota(jnp.int32, (16, 128), 1)
    sublane = lax.broadcasted_iota(jnp.int32, (16, 128), 0)
    parity = (sublane >= 8).astype(jnp.int32)
    half = (lane >= 64).astype(jnp.int32)
    los = lax.broadcasted_iota(jnp.int32, (64, 256), 1).astype(BF)
    left = lax.broadcasted_iota(jnp.int32, (1, 128), 1) < 64
    hi_pattern = [(2 * t + parity).astype(BF) for t in range(pairs)]
    row_mask = [(sublane & 7) == 2 * c + half for c in range(4)]
    zero = jnp.zeros((), BF)
    one = jnp.ones((), BF)

    def slots(x):
        return jnp.concatenate([x, jnp.zeros((64 - fanout, 128), F32)], axis=0)

    def by_row(x):
        x = slots(x).T
        return jnp.concatenate([x, x], axis=1)

    index = index_ref[:, at]
    slot = lax.broadcasted_iota(jnp.int32, index.shape, 0)
    weight = jnp.where(slot < counts, importance_ref[:, at], 0.0)
    alpha = by_row(weight / jnp.sum(weight, axis=0, keepdims=True))
    hi = by_row((index >> 8).astype(F32))
    lo = slots((index & 255).astype(F32)).astype(BF)
    for g in range(0, 128, 16):
        tiles = []
        for s in range(2):
            left_parts, right_parts = [], []
            for c in range(4):
                r = g + s * 8 + 2 * c

                def pick(x):
                    return jnp.where(left, x[r : r + 1, :], x[r + 1 : r + 2, :]).astype(BF)

                kept = jnp.where(row_mask[c], jnp.broadcast_to(pick(alpha), (16, 128)), zero)
                hi_row = jnp.broadcast_to(pick(hi), (16, 128))
                left_parts.append(
                    jnp.concatenate(
                        [jnp.where(hi_row == hi_pattern[t], kept, zero) for t in range(pairs)], axis=0
                    )
                )
                for q in (r, r + 1):
                    right_parts.append(jnp.where(jnp.broadcast_to(lo[:, q : q + 1], (64, 256)) == los, one, zero))
            tiles.append(
                jnp.dot(
                    jnp.concatenate(left_parts, axis=1),
                    jnp.concatenate(right_parts, axis=0),
                    preferred_element_type=F32,
                )
            )
        for h in range(his):
            tile = jnp.concatenate([t[h * 8 : (h + 1) * 8, :] for t in tiles], axis=0).astype(BF)
            to = pl.ds(pl.multiple_of(first + g, 16), 16)
            if h * 256 < rows:
                own_ref[to, h * 256 : (h + 1) * 256] = tile
            else:
                start = h * 256 - rows
                stop = min(start + 256, halo)
                halo_ref[to, start:stop] = tile[:, : stop - start]


def build_kernel(index_ref, count_ref, importance_ref, own_ref, halo_ref, *, rows, halo):
    for first in range(0, own_ref.shape[0], 128):
        counts = count_ref[:, first : first + 128]
        build_rows(index_ref, counts, importance_ref, own_ref, halo_ref, first, rows=rows, halo=halo)


def build_mixing(nbr_index, nbr_count, importance, halo):
    rows, fanout = nbr_index.shape
    block = 256
    return pl.pallas_call(
        functools.partial(build_kernel, rows=rows, halo=halo),
        grid=(rows // block,),
        in_specs=[
            pl.BlockSpec((fanout, block), lambda i: (0, i)),
            pl.BlockSpec((1, block), lambda i: (0, i)),
            pl.BlockSpec((fanout, block), lambda i: (0, i)),
        ],
        out_specs=[
            pl.BlockSpec((block, rows), lambda i: (i, 0)),
            pl.BlockSpec((block, halo), lambda i: (i, 0)),
        ],
        out_shape=[
            jax.ShapeDtypeStruct((rows, rows), BF),
            jax.ShapeDtypeStruct((rows, halo), BF),
        ],
        compiler_params=pltpu.CompilerParams(vmem_limit_bytes=40 * 2**20),
        name="build_mixing",
    )(nbr_index.T, nbr_count.reshape(1, rows), importance.T)


def gelu_pair(x):
    c = math.sqrt(2.0 / math.pi)
    square = x * x
    half = 0.5 + 0.5 * jnp.tanh(x * (c + (c * 0.044715) * square))
    value = x * half
    return value, half + value * (1.0 - half) * (2.0 * c + (6.0 * c * 0.044715) * square)


def hidden_rows(features_ref, q_buf, bias_ref, send_ref, low_ref, neigh_ref, slope_ref, sent_ref, at_rows, start):
    width = features_ref.shape[1]
    lead = (slice(None),) * (len(q_buf.shape) - 1)
    low_ref[at_rows, :] = features_ref[at_rows, :].astype(BF)
    for c in range(0, width, 256):
        at = slice(c, c + 256)
        q = q_buf[lead + (at,)].reshape(width, 256)
        pre = jnp.dot(low_ref[at_rows, :], q, preferred_element_type=F32) + bias_ref[0:1, at]
        value, slope = gelu_pair(pre)
        neigh_ref[at_rows, at] = value.astype(BF)
        slope_ref[at_rows, at] = slope.astype(BF)
    neigh = neigh_ref[at_rows, :]
    local = lax.broadcasted_iota(jnp.int32, (neigh.shape[0], send_ref.shape[1]), 0) + start
    chosen = jnp.where(local == send_ref[...], 1.0, 0.0).astype(BF)
    sent_ref[...] += lax.dot_general(chosen, neigh, (((0,), (0,)), ((), ())), preferred_element_type=F32)


def ring_copies(groups, index, blocks_ref, landed_ref, send_sem, recv_sem, device_of):
    copies = []
    for k in range(1, groups):
        other = (index + k) % groups
        copies.append(
            pltpu.make_async_remote_copy(
                src_ref=blocks_ref.at[other],
                dst_ref=landed_ref.at[index],
                send_sem=send_sem.at[k - 1],
                recv_sem=recv_sem.at[k - 1],
                device_id=device_of(other),
                device_id_type=pl.DeviceIdType.MESH,
            )
        )
    return copies


def regroup(x, outer, inner, per):
    count = x.shape[0]
    to = lax.broadcasted_iota(jnp.int32, (count, count), 0)
    place = lax.broadcasted_iota(jnp.int32, (count, count), 1)
    source = ((to // per) % outer) * (inner * per) + (to // (per * outer)) * per + to % per
    chosen = jnp.where(place == source, 1.0, 0.0).astype(BF)
    return jnp.dot(chosen, x, preferred_element_type=F32).astype(BF)


def greet(comm, sub, comms, subs):
    barrier = pltpu.get_barrier_semaphore()
    for k in range(1, comms):
        pl.semaphore_signal(
            barrier, inc=1, device_id=((comm + k) % comms, sub), device_id_type=pl.DeviceIdType.MESH
        )
    for k in range(1, subs):
        pl.semaphore_signal(
            barrier, inc=1, device_id=(comm, (sub + k) % subs), device_id_type=pl.DeviceIdType.MESH
        )
    pl.semaphore_wait(barrier, comms + subs - 2)


def send_targets(send_rows, comms, subs):
    per = send_rows.shape[2]
    return send_rows.reshape(comms, subs, per).transpose(1, 0, 2).reshape(1, comms * subs * per)


def gather_kernel(
    index_ref,
    count_ref,
    importance_ref,
    q_ref,
    w_ref,
    q_bias_ref,
    w_bias_ref,
    send_ref,
    features_hbm,
    own_out,
    halo_ref,
    low_out,
    slope_out,
    pooled_out,
    q_full,
    w_full,
    bias_out,
    features,
    own_mix,
    low,
    neigh,
    slope,
    pooled,
    pooled_low,
    q_buf,
    w_own,
    bias_buf,
    sent_acc,
    sub_blocks,
    sub_landed,
    comm_blocks,
    comm_landed,
    local_sem,
    feature_sem,
    send_sem,
    recv_sem,
    sub_send,
    sub_recv,
    comm_send,
    comm_recv,
    *,
    comms,
    subs,
    bits,
    block,
    pool_block,
):
    rows = own_mix.shape[0]
    halo = halo_ref.shape[1]
    width = neigh.shape[1]
    comm, sub = lax.axis_index("comm"), lax.axis_index("sub")
    me = comm * subs + sub
    mine = [(me // (1 << b)) % 2 for b in range(bits)]
    order = list(range(bits))[::-1]

    def partner(b):
        other = me + (1 << b) * (1 - 2 * mine[b])
        return (other // subs, other % subs)

    def spot(done, part=slice(None), columns=slice(None)):
        lead = tuple(slice(None) if b in done else mine[b] for b in order)
        return lead + (part, columns)

    high = list(range(3, bits))[::-1]
    left, right = pl.ds(0, width // 2), pl.ds(width // 2, width // 2)
    count = [0]

    def exchange(buf, b, done, part=slice(None), columns=slice(None), source=None):
        at = buf.at[spot(done, part, columns)]
        n = count[0]
        count[0] += 1
        return pltpu.make_async_remote_copy(
            src_ref=at if source is None else source,
            dst_ref=at,
            send_sem=send_sem.at[n],
            recv_sem=recv_sem.at[n],
            device_id=partner(b),
            device_id_type=pl.DeviceIdType.MESH,
        )

    def chain(buf, own, split, part=slice(None)):
        groups = []
        done = []
        for b in high:
            groups.append([exchange(buf, b, done, part, source=own if not done else None)])
            done = done + [b]
        if split:
            groups.append([exchange(buf, 1, done, part, left), exchange(buf, 2, done, part, right)])
            groups.append(
                [exchange(buf, 2, done + [1], part, left), exchange(buf, 1, done + [2], part, right)]
            )
        else:
            groups.append([exchange(buf, 1, done)])
            groups.append([exchange(buf, 2, done + [1])])
        groups.append([exchange(buf, 0, done + [1, 2], part)])
        return groups

    def chain_xy(buf, own, part):
        groups = [
            [
                exchange(buf, 1, [], part, left, own.at[part, left]),
                exchange(buf, 2, [], part, right, own.at[part, right]),
            ],
            [exchange(buf, 2, [1], part, left), exchange(buf, 1, [2], part, right)],
        ]
        done = [1, 2]
        for b in high:
            groups.append([exchange(buf, b, done, part)])
            done = done + [b]
        groups.append([exchange(buf, 0, done, part)])
        return groups

    w_rows = w_own.shape[0]
    top, bottom = pl.ds(0, w_rows // 2), pl.ds(w_rows // 2, w_rows // 2)
    chains = {
        "q": chain(q_buf, None, True),
        "bias": chain(bias_buf, None, False),
        "w0": chain(w_full, w_own.at[top], True, top),
        "w1": chain_xy(w_full, w_own, bottom),
        "sub": [ring_copies(subs, sub, sub_blocks, sub_landed, sub_send, sub_recv, lambda j: (comm, j))],
        "comm": [ring_copies(comms, comm, comm_blocks, comm_landed, comm_send, comm_recv, lambda j: (j, sub))],
    }
    w_local = pltpu.make_async_copy(w_own, w_full.at[spot([])], local_sem.at[0])
    q_local = pltpu.make_async_copy(q_buf, q_full, local_sem.at[1])
    last = len(chains["q"]) - 1

    def begin(name, n):
        for c in chains[name][n]:
            c.start()

    def finish(name, n):
        for c in chains[name][n]:
            c.wait()

    def place(n, size):
        return pl.ds(pl.multiple_of(n * size, size), size)

    def feature_copy(n):
        at = place(n, block)
        return pltpu.make_async_copy(features_hbm.at[at, :], features.at[at, :], feature_sem.at[n])

    outs = [(own_mix, own_out), (low, low_out), (slope, slope_out), (pooled_low, pooled_out)]

    def give(n, at):
        source, target = outs[n]
        pltpu.make_async_copy(source.at[at, :], target.at[at, :], local_sem.at[2 + n]).start()

    def given(n):
        pltpu.make_async_copy(*outs[n], local_sem.at[2 + n]).wait()

    events = {
        ("build", 1): [("w1", -1)],
        ("build", 4): [("q", 0), ("bias", 0), ("w1", 0)],
        ("build", 6): [("w0", -1)],
        ("build", 7): [("q", 1), ("bias", 1)],
        ("build", 9): [("w1", 1)],
        ("build", 10): [("q", 2), ("bias", 2), ("w0", 0)],
        ("build", 15): [("q", 3), ("bias", 3)],
        ("build", 16): [("w0", 1)],
        ("hidden", 1): [("w1", 2), ("w0", 2)],
        ("hidden", 6): [("w0", 3)],
        ("pool", 1): [("w1", 3)],
    }

    def happen(phase, n):
        for (when, step), names in events.items():
            if when == phase:

                @pl.when(n == step)
                def _(names=names):
                    for name, k in names:
                        if k >= 0:
                            finish(name, k)
                        begin(name, k + 1)

    q_buf[spot([])] = q_ref[...].astype(BF)
    w_own[...] = w_ref[...].astype(BF)
    share = q_bias_ref.shape[1]
    bias_own = jnp.concatenate(
        [q_bias_ref[...], w_bias_ref[...], jnp.zeros((1, 128 - 2 * share), F32)], axis=1
    )
    bias_buf[spot([])] = jnp.broadcast_to(bias_own, (8, 128))
    greet(comm, sub, comms, subs)
    begin("q", 0)
    begin("bias", 0)
    w_local.start()
    sent_acc[...] = jnp.zeros_like(sent_acc)
    w_local.wait()

    @pl.loop(0, rows // block)
    def _(n):
        feature_copy(n).start()

    @pl.loop(0, rows // 128)
    def _(n):
        happen("build", n)
        build_rows(
            index_ref,
            count_ref[pl.ds(n, 1), :],
            importance_ref,
            own_mix,
            halo_ref,
            n * 128,
            rows=rows,
            halo=halo,
        )
        give(0, place(n, 128))

    finish("q", last)
    finish("bias", last)
    q_local.start()
    for k in range(2):
        pieces = []
        for e in range(1 << bits):
            piece = bias_buf[tuple((e >> b) & 1 for b in order)]
            pieces.append(piece[0:1, k * share : (k + 1) * share])
        bias_out[k : k + 1, :] = jnp.concatenate(pieces, axis=1).astype(BF).astype(F32)
    bias_out[2:, :] = jnp.zeros((6, width), F32)

    @pl.loop(0, rows // block)
    def _(n):
        happen("hidden", n)
        feature_copy(n).wait()
        at = place(n, block)
        hidden_rows(features, q_buf, bias_out, send_ref, low, neigh, slope, sent_acc, at, n * block)
        give(1, at)
        give(2, at)

    sub_blocks[...] = sent_acc[...].astype(BF).reshape(sub_blocks.shape)
    begin("sub", 0)
    sub_landed[sub] = sub_blocks[sub]

    @pl.loop(0, rows // pool_block)
    def _(n):
        happen("pool", n)

        @pl.when(n == 2)
        def _():
            finish("sub", 0)
            moved = regroup(sub_landed[...].reshape(halo, width), subs, comms, halo // (subs * comms))
            comm_blocks[...] = moved.reshape(comm_blocks.shape)
            begin("comm", 0)
            comm_landed[comm] = comm_blocks[comm]

        at = place(n, pool_block)
        pooled[at, :] = jnp.dot(own_mix[at, :], neigh[...], preferred_element_type=F32)

    finish("comm", 0)

    @pl.loop(0, rows // pool_block)
    def _(n):
        at = place(n, pool_block)
        received = comm_landed[...].reshape(halo, width)
        total = pooled[at, :] + jnp.dot(halo_ref[at, :], received, preferred_element_type=F32)
        pooled_low[at, :] = total.astype(BF)
        give(3, at)

    finish("w0", last)
    finish("w1", last)
    q_local.wait()
    for n in range(4):
        given(n)


def gather_and_transform(features, q_weight, q_bias, w_weight, w_bias, nbr_index, nbr_count, importance, send_rows):
    comms, subs = lax.axis_size("comm"), lax.axis_size("sub")
    devices = comms * subs
    bits = devices.bit_length() - 1
    rows, width = features.shape
    fanout = nbr_index.shape[1]
    per = send_rows.shape[2]
    halo = devices * per
    block, pool_block = 256, 384
    q_rows, w_rows = q_weight.shape[0], w_weight.shape[0]
    share = q_bias.shape[0]
    targets = send_targets(send_rows, comms, subs)
    lead = (2,) * bits

    here = pl.BlockSpec(memory_space=pltpu.VMEM)
    anywhere = pl.BlockSpec(memory_space=pl.ANY)
    copies = 4 * bits + 3 * 2
    out = pl.pallas_call(
        functools.partial(
            gather_kernel, comms=comms, subs=subs, bits=bits, block=block, pool_block=pool_block
        ),
        in_specs=[here] * 8 + [anywhere],
        out_specs=[anywhere, here, anywhere, anywhere, anywhere, anywhere, anywhere, here],
        out_shape=[
            jax.ShapeDtypeStruct((rows, rows), BF),
            jax.ShapeDtypeStruct((rows, halo), BF),
            jax.ShapeDtypeStruct((rows, width), BF),
            jax.ShapeDtypeStruct((rows, width), BF),
            jax.ShapeDtypeStruct((rows, width), BF),
            jax.ShapeDtypeStruct(lead + (q_rows, width), BF),
            jax.ShapeDtypeStruct(lead + (w_rows, width), BF),
            jax.ShapeDtypeStruct((8, width), F32),
        ],
        scratch_shapes=[
            pltpu.VMEM((rows, width), F32),
            pltpu.VMEM((rows, rows), BF),
            pltpu.VMEM((rows, width), BF),
            pltpu.VMEM((rows, width), BF),
            pltpu.VMEM((rows, width), BF),
            pltpu.VMEM((rows, width), F32),
            pltpu.VMEM((rows, width), BF),
            pltpu.VMEM(lead + (q_rows, width), BF),
            pltpu.VMEM((w_rows, width), BF),
            pltpu.VMEM(lead + (8, 128), F32),
            pltpu.VMEM((halo, width), F32),
            pltpu.VMEM((subs, halo // subs, width), BF),
            pltpu.VMEM((subs, halo // subs, width), BF),
            pltpu.VMEM((comms, halo // comms, width), BF),
            pltpu.VMEM((comms, halo // comms, width), BF),
            pltpu.SemaphoreType.DMA((6,)),
            pltpu.SemaphoreType.DMA((rows // block,)),
            pltpu.SemaphoreType.DMA((copies,)),
            pltpu.SemaphoreType.DMA((copies,)),
            pltpu.SemaphoreType.DMA((subs - 1,)),
            pltpu.SemaphoreType.DMA((subs - 1,)),
            pltpu.SemaphoreType.DMA((comms - 1,)),
            pltpu.SemaphoreType.DMA((comms - 1,)),
        ],
        compiler_params=pltpu.CompilerParams(
            collective_id=0, has_side_effects=True, vmem_limit_bytes=62 * 2**20
        ),
        name="gather_and_transform",
    )(
        nbr_index.T,
        nbr_count.reshape(rows // 128, 128),
        importance.T,
        q_weight,
        w_weight,
        q_bias.reshape(1, share),
        w_bias.reshape(1, share),
        targets,
        features,
    )
    own_mix, halo_mix, low, slope, pooled, q_full, w_full, biases = out
    return (
        own_mix,
        halo_mix,
        low,
        slope,
        pooled,
        q_full.reshape(devices * q_rows, width),
        w_full.reshape(devices * w_rows, width),
        biases,
    )


def gather_plain(features, q_weight, q_bias, w_weight, w_bias, nbr_index, nbr_count, importance, send_rows):
    rows, width = features.shape
    devices, per_peer = send_rows.shape[1:]
    halo = devices * per_peer
    own_mix, halo_mix = build_mixing(nbr_index, nbr_count, importance, halo)
    q_full = lax.all_gather(q_weight.astype(BF), AXES, axis=0, tiled=True)
    w_full = lax.all_gather(w_weight.astype(BF), AXES, axis=0, tiled=True)
    biases = doubled(jnp.stack([q_bias, w_bias]), devices)
    qbias_full = biases[:, 0].reshape(width).astype(BF).astype(F32)
    wbias_full = biases[:, 1].reshape(width).astype(BF).astype(F32)
    low = features.astype(BF)
    neigh, slope = gelu_pair(jnp.dot(low, q_full, preferred_element_type=F32) + qbias_full)
    neigh = neigh.astype(BF)
    sent = neigh[send_rows[0]]
    incoming = lax.all_to_all(sent, AXES, split_axis=0, concat_axis=0, tiled=True).reshape(halo, width)
    pooled = pool_own(own_mix, neigh) + jnp.dot(halo_mix, incoming, preferred_element_type=F32)
    biases = jnp.pad(jnp.stack([qbias_full, wbias_full]), ((0, 6), (0, 0)))
    return own_mix, halo_mix, low, slope.astype(BF), pooled.astype(BF), q_full, w_full, biases


def resident(*shape):
    return pl.BlockSpec(shape, lambda i: (0,) * len(shape), pipeline_mode=pl.Buffered(1))


def by_rows(*shape):
    return pl.BlockSpec(shape, lambda i: (i,) + (0,) * (len(shape) - 1))


def product_kernel(mix_ref, table_ref, out_ref):
    out_ref[...] = jnp.dot(mix_ref[...], table_ref[...], preferred_element_type=F32)


def pool_own(own_mix, neigh):
    rows, width = neigh.shape
    block = 384
    return pl.pallas_call(
        product_kernel,
        grid=(rows // block,),
        in_specs=[by_rows(block, rows), resident(rows, width)],
        out_specs=by_rows(block, width),
        out_shape=jax.ShapeDtypeStruct((rows, width), F32),
        compiler_params=pltpu.CompilerParams(vmem_limit_bytes=40 * 2**20),
        cost_estimate=pl.CostEstimate(
            flops=2 * rows * rows * width, bytes_accessed=2 * rows * rows + 6 * rows * width, transcendentals=0
        ),
        name="pool_own",
    )(own_mix, neigh)


def combine_kernel(
    pooled_ref,
    halo_ref,
    low_ref,
    w_ref,
    bias_ref,
    cotangent_ref,
    embedding_ref,
    grad_ref,
    grad_pooled_ref,
    sent_ref,
    bias_grad_ref,
    act_buf,
    slope_buf,
):
    i = pl.program_id(0)
    block, width = low_ref.shape
    chunk = 256

    @pl.when(i == 0)
    def _():
        sent_ref[...] = jnp.zeros_like(sent_ref)
        bias_grad_ref[...] = jnp.zeros_like(bias_grad_ref)

    squares = jnp.zeros((block, 128), F32)
    dots = jnp.zeros((block, 128), F32)
    for c in range(0, width, chunk):
        at = slice(c, c + chunk)
        pre = jnp.dot(low_ref[...], w_ref[:width, at], preferred_element_type=F32)
        pre += jnp.dot(pooled_ref[...], w_ref[width:, at], preferred_element_type=F32)
        act, slope = gelu_pair(pre + bias_ref[1:2, at])
        act_buf[:, at] = act
        slope_buf[:, at] = slope
        square = act * act
        dot = act * cotangent_ref[:, at]
        for k in range(0, chunk, 128):
            squares += square[:, k : k + 128]
            dots += dot[:, k : k + 128]
    scale = lax.rsqrt(jnp.sum(squares, axis=1, keepdims=True) * (1.0 / width) + 1e-06)
    pull = jnp.sum(dots, axis=1, keepdims=True) * (1.0 / width) * scale * scale * scale
    for c in range(0, width, chunk):
        at = slice(c, c + chunk)
        act = act_buf[:, at]
        embedding_ref[:, at] = act * scale
        grad = slope_buf[:, at] * (cotangent_ref[:, at] * scale - act * pull)
        grad_ref[:, at] = grad.astype(BF)
        bias_grad_ref[0:1, at] += jnp.sum(grad_ref[:, at].astype(F32), axis=0, keepdims=True)
    for c in range(0, width, chunk):
        at = slice(c, c + chunk)
        back = lax.dot_general(
            grad_ref[...],
            w_ref[width + c : width + c + chunk, :],
            (((1,), (1,)), ((), ())),
            preferred_element_type=F32,
        )
        grad_pooled_ref[:, at] = back.astype(BF)
    sent_ref[...] += lax.dot_general(
        halo_ref[...], grad_pooled_ref[...], (((0,), (0,)), ((), ())), preferred_element_type=F32
    )


def combine(pooled, halo_mix, low, w_full, biases, cotangent):
    rows, width = low.shape
    halo = halo_mix.shape[1]
    block = 768
    return pl.pallas_call(
        combine_kernel,
        grid=(rows // block,),
        in_specs=[
            by_rows(block, width),
            by_rows(block, halo),
            by_rows(block, width),
            resident(2 * width, width),
            resident(8, width),
            by_rows(block, width),
        ],
        out_specs=[
            by_rows(block, width),
            by_rows(block, width),
            by_rows(block, width),
            pl.BlockSpec((halo, width), lambda i: (0, 0)),
            pl.BlockSpec((8, width), lambda i: (0, 0)),
        ],
        out_shape=[
            jax.ShapeDtypeStruct((rows, width), F32),
            jax.ShapeDtypeStruct((rows, width), BF),
            jax.ShapeDtypeStruct((rows, width), BF),
            jax.ShapeDtypeStruct((halo, width), F32),
            jax.ShapeDtypeStruct((8, width), F32),
        ],
        scratch_shapes=[pltpu.VMEM((block, width), F32), pltpu.VMEM((block, width), F32)],
        compiler_params=pltpu.CompilerParams(vmem_limit_bytes=62 * 2**20),
        cost_estimate=pl.CostEstimate(
            flops=6 * rows * width * width, bytes_accessed=22 * rows * width, transcendentals=rows * width
        ),
        name="combine",
    )(pooled, halo_mix, low, w_full, biases, cotangent)


def swap(x, bit, devices):
    return lax.ppermute(x, AXES, [(i, i ^ (1 << bit)) for i in range(devices)])


def doubled(x, devices):
    me = lax.axis_index(AXES)
    x = x[None]
    for bit in range(devices.bit_length() - 1):
        other = swap(x, bit, devices)
        first = ((me >> bit) & 1) == 0
        x = jnp.where(first, jnp.concatenate([x, other]), jnp.concatenate([other, x]))
    return x


def summed(x, devices):
    for bit in range(devices.bit_length() - 1):
        x = x + swap(x, bit, devices)
    return x


def halve(part, left, bit, devices):
    mine = (lax.axis_index(AXES) >> bit) & 1
    axis = left.index(bit)
    keep = lax.dynamic_index_in_dim(part, mine, axis, keepdims=False)
    sent = lax.dynamic_index_in_dim(part, 1 - mine, axis, keepdims=False)
    total = keep.astype(F32) + swap(sent, bit, devices).astype(F32)
    return total, [b for b in left if b != bit]


def scatter_sum(partial, devices):
    bits = list(range(devices.bit_length() - 1))[::-1]
    width = partial.shape[1]
    part = partial.reshape([2] * len(bits) + [-1, width])
    part, left = halve(part, bits, 0, devices)
    part = part.astype(BF)
    rows = part.shape[-2] // 2
    orders = ([1, 2] + list(range(3, len(bits))), [2, 1] + list(range(3, len(bits))))
    halves = [(part[..., :rows, :], left), (part[..., rows:, :], left)]
    for step in range(len(bits) - 1):
        for s in range(2):
            total, rest = halve(halves[s][0], halves[s][1], orders[s][step], devices)
            halves[s] = (total if len(rest) == 0 else total.astype(BF), rest)
    return jnp.concatenate([h[0] for h in halves], axis=0)


def back_plain(
    own_mix, low, slope, pooled, grad_out, grad_pooled, sent_grad, grad_wbias, q_full, w_full, send_rows
):
    rows, width = low.shape
    devices, per = send_rows.shape[1:]
    contract = (((0,), (0,)), ((), ()))
    returned = lax.all_to_all(
        sent_grad.reshape(devices, per, width), AXES, split_axis=0, concat_axis=0, tiled=True
    )
    joined = jnp.concatenate([low, pooled], axis=1)
    grad_w = lax.dot_general(joined, grad_out, contract, preferred_element_type=F32)
    grad_low = lax.dot_general(grad_out, w_full[:width], (((1,), (1,)), ((), ())), preferred_element_type=F32)
    grad_neigh = lax.dot_general(own_mix, grad_pooled, contract, preferred_element_type=F32)
    grad_neigh = grad_neigh.at[send_rows.reshape(-1)].add(returned.reshape(devices * per, width))
    grad_hidden = (slope.astype(F32) * grad_neigh).astype(BF)
    grad_q = lax.dot_general(low, grad_hidden, contract, preferred_element_type=F32)
    grad_qbias = jnp.sum(grad_hidden.astype(F32), axis=0)
    grad_features = grad_low + lax.dot_general(
        grad_hidden, q_full, (((1,), (1,)), ((), ())), preferred_element_type=F32
    )
    me = lax.axis_index(AXES)
    share = width // devices
    sums = summed(jnp.stack([grad_qbias, grad_wbias[0]]), devices)
    sums = lax.dynamic_slice_in_dim(sums, me * share, share, 1)
    return (
        grad_features,
        scatter_sum(grad_q.astype(BF), devices),
        sums[0],
        scatter_sum(grad_w.astype(BF), devices),
        sums[1],
    )


class ScatterSum:
    def __init__(self, refs, orders, mine, partner):
        self.held, self.sent, self.got, self.next_sent, self.next_got, self.send_sem, self.recv_sem = refs
        self.orders, self.mine, self.partner = orders, mine, partner
        self.bits = len(mine)
        self.lead = list(range(1, self.bits))[::-1]
        self.half = self.held.shape[-1] // 2

    def copy(self, n, source, target, b):
        return pltpu.make_async_remote_copy(
            src_ref=source,
            dst_ref=target,
            send_sem=self.send_sem.at[n],
            recv_sem=self.recv_sem.at[n],
            device_id=self.partner(b),
            device_id_type=pl.DeviceIdType.MESH,
        )

    def first(self, top):
        return self.copy(top, self.sent.at[self.top_index(top)], self.got.at[self.top_index(top)], 0)

    def top_index(self, top):
        return ((top // 2) % 2, top % 2)

    def later(self, k, h):
        n = 4 + 2 * (k - 1) + h
        at = (h, slice(self.offset(k), self.offset(k) + (1 << (self.bits - 1 - k))))
        return self.copy(n, self.next_sent.at[at], self.next_got.at[at], self.orders[h][k - 1])

    def offset(self, k):
        return (1 << (self.bits - 1)) - (1 << (self.bits - k))

    def spot(self, chosen):
        return tuple(chosen[b] for b in self.lead)

    def absorb(self, k, halves):
        for h in halves:
            order = self.orders[h]
            fixed = order[:k]
            free = [b for b in self.lead if b not in fixed]
            columns = slice(h * self.half, (h + 1) * self.half)

            def total(chosen, h=h, free=free, columns=columns):
                at = self.spot(chosen)
                if k == 0:
                    came = self.got[at + (slice(None), columns)]
                else:
                    place = self.offset(k)
                    for p, b in enumerate(free[::-1]):
                        place = place + chosen[b] * (1 << p)
                    came = self.next_got[h, place]
                return at, self.held[at + (slice(None), columns)] + came.astype(F32)

            if not free:
                at, value = total({b: self.mine[b] for b in fixed})
                self.held[at + (slice(None), columns)] = value
                continue
            split = order[k]
            others = [b for b in free if b != split]

            def body(n, carry, total=total, split=split, others=others, fixed=fixed, columns=columns, h=h):
                chosen = {b: self.mine[b] for b in fixed}
                for p, b in enumerate(others[::-1]):
                    chosen[b] = (n // (1 << p)) % 2
                chosen[split] = self.mine[split]
                at, value = total(chosen)
                self.held[at + (slice(None), columns)] = value
                chosen[split] = 1 - self.mine[split]
                _, value = total(chosen)
                self.next_sent[h, self.offset(k + 1) + n] = value.astype(BF)
                return carry

            lax.fori_loop(0, 1 << len(others), body, 0)

    def advance(self, k):
        if k == 0:
            for t in range(4):
                self.first(t).wait()
        for h in range(2):
            if k > 0:
                self.later(k, h).wait()
            self.absorb(k, [h])
            if k < self.bits - 1:
                self.later(k + 1, h).start()

    def result(self):
        return self.held[self.spot({b: self.mine[b] for b in self.lead})]


def back_body(
    sent_grad_ref,
    w_bias_ref,
    target_ref,
    mix_hbm,
    slope_hbm,
    low_hbm,
    pooled_hbm,
    out_hbm,
    grad_pooled_hbm,
    w_hbm,
    q_hbm,
    features_out,
    q_out,
    w_out,
    bias_out,
    joined,
    grad_out,
    grad_pooled,
    slope,
    w_top,
    q_full,
    mix,
    features,
    q_bias_acc,
    bias_sent,
    bias_got,
    comm_blocks,
    comm_landed,
    sub_blocks,
    sub_landed,
    *rest,
    comms,
    subs,
    bits,
    mix_block,
    row_block,
):
    sets = [rest[7 * k : 7 * k + 7] for k in range(4)]
    load_sem, mix_sem, out_sem, bias_send, bias_recv, comm_send, comm_recv, sub_send, sub_recv = rest[28:]
    rows, width = grad_out.shape
    halo = sent_grad_ref.shape[0]
    half = width // 2
    comm, sub = lax.axis_index("comm"), lax.axis_index("sub")
    me = comm * subs + sub
    mine = [(me // (1 << b)) % 2 for b in range(bits)]
    tn = (((0,), (0,)), ((), ()))
    nt = (((1,), (1,)), ((), ()))

    def partner(b):
        other = me + (1 << b) * (1 - 2 * mine[b])
        return (other // subs, other % subs)

    high = list(range(3, bits))
    orders = ([1, 2] + high, [2, 1] + high)
    w_sets = [ScatterSum(sets[k], orders, mine, partner) for k in range(2)]
    q_sets = [ScatterSum(sets[2 + k], orders, mine, partner) for k in range(2)]

    left, right = pl.ds(0, half), pl.ds(half, half)
    loads = [
        (out_hbm.at[:, left], grad_out.at[:, left]),
        (low_hbm.at[:, left], joined.at[:, pl.ds(0, half)]),
        (low_hbm.at[:, right], joined.at[:, pl.ds(half, half)]),
        (pooled_hbm.at[:, left], joined.at[:, pl.ds(2 * half, half)]),
        (pooled_hbm.at[:, right], joined.at[:, pl.ds(3 * half, half)]),
        (out_hbm.at[:, right], grad_out.at[:, right]),
        (grad_pooled_hbm, grad_pooled),
        (slope_hbm, slope),
        (w_hbm.at[pl.ds(0, width), :], w_top),
        (q_hbm, q_full),
    ]
    loads = [pltpu.make_async_copy(a, b, load_sem.at[n]) for n, (a, b) in enumerate(loads)]
    comm_ring = ring_copies(comms, comm, comm_blocks, comm_landed, comm_send, comm_recv, lambda j: (j, sub))
    sub_ring = ring_copies(subs, sub, sub_blocks, sub_landed, sub_send, sub_recv, lambda j: (comm, j))
    bias_copies = [
        pltpu.make_async_remote_copy(
            src_ref=bias_sent.at[b],
            dst_ref=bias_got.at[b],
            send_sem=bias_send.at[b],
            recv_sem=bias_recv.at[b],
            device_id=partner(b),
            device_id_type=pl.DeviceIdType.MESH,
        )
        for b in range(bits)
    ]

    spreads = rows // mix_block
    rounds = rows // row_block

    def mix_copy(n):
        at = pl.ds(pl.multiple_of(n * mix_block, mix_block), mix_block)
        return pltpu.make_async_copy(mix_hbm.at[:, at], mix.at[n % 2], mix_sem.at[n % 2])

    def out_copy(n):
        at = pl.ds(pl.multiple_of(n * row_block, row_block), row_block)
        return pltpu.make_async_copy(features.at[n % 2], features_out.at[at, :], out_sem.at[n % 2])

    def deal(value, which, top, rows_each):
        keep_even = mine[0] == 0
        shares = value.shape[0] // rows_each
        for p in range(shares // 2):
            even = value[2 * p * rows_each : (2 * p + 1) * rows_each]
            odd = value[(2 * p + 1) * rows_each : (2 * p + 2) * rows_each]
            at = top + tuple((p >> b) & 1 for b in range(bits - 2, -1, -1))[len(top) :]
            which.held[at] = jnp.where(keep_even, even, odd)
            which.sent[at] = jnp.where(keep_even, odd, even).astype(BF)

    def w_top_bits(j):
        return ((j // 2) % 2, j % 2)

    events = {
        ("w1", 1): [(0, 0)],
        ("spread", 1): [(0, 1), (1, 0)],
        ("spread", 3): [(0, 2)],
        ("spread", 5): [(1, 1), (0, 3)],
        ("q", 1): [(0, 4)],
        ("q", 2): [(2, 0), (1, 2)],
        ("features", 0): [(3, 0)],
        ("features", 2): [(1, 3), (2, 1)],
        ("features", 4): [(3, 1), (2, 2)],
        ("features", 5): [(1, 4)],
    }
    all_sets = w_sets + q_sets

    def happen(phase, n):
        for (when, step), which in events.items():
            if when == phase:

                @pl.when(n == step)
                def _(which=which):
                    for m, k in which:
                        all_sets[m].advance(k)

    def load_when(step, n, begin=(), need=()):
        @pl.when(n == step)
        def _():
            for m in need:
                loads[m].wait()
            for m in begin:
                loads[m].start()

    for n in range(3):
        loads[n].start()
    comm_blocks[...] = sent_grad_ref[...].astype(BF).reshape(comm_blocks.shape)
    q_bias_acc[...] = jnp.zeros_like(q_bias_acc)
    greet(comm, sub, comms, subs)
    for c in comm_ring:
        c.start()
    comm_landed[comm] = comm_blocks[comm]

    for n in range(2):

        @pl.loop(0, 4)
        def _(j, n=n):
            if n == 0:
                load_when(0, j, [3], [0, 1])
                load_when(1, j, [4], [2])
                load_when(2, j, [5], [3])
                load_when(3, j, [6], [4])
            else:
                load_when(0, j, [7], [5])
                load_when(1, j, [8])
                load_when(2, j, [9])

                @pl.when(j == 3)
                def _():
                    mix_copy(0).start()

            at = pl.ds(pl.multiple_of(j * half, half), half)
            columns = slice(n * half, (n + 1) * half)
            value = lax.dot_general(joined[:, at], grad_out[:, columns], tn, preferred_element_type=F32)
            deal(value, w_sets[n], w_top_bits(j), w_out.shape[0])
            w_sets[n].first(j).start()
            happen("w" + str(n), j)

        if n == 0:
            for c in comm_ring:
                c.wait()
            moved = regroup(comm_landed[...].reshape(halo, width), comms, subs, halo // (subs * comms))
            sub_blocks[...] = moved.reshape(sub_blocks.shape)
            for c in sub_ring:
                c.start()
            sub_landed[sub] = sub_blocks[sub]

    for c in sub_ring:
        c.wait()
    for n in (6, 7):
        loads[n].wait()

    @pl.loop(0, spreads)
    def _(n):
        @pl.when(n + 1 < spreads)
        def _():
            mix_copy(n + 1).start()

        happen("spread", n)
        mix_copy(n).wait()
        start = n * mix_block
        at = pl.ds(pl.multiple_of(start, mix_block), mix_block)
        local = lax.broadcasted_iota(jnp.int32, (mix_block, halo), 0) + start
        chosen = jnp.where(local == target_ref[...], 1.0, 0.0).astype(BF)
        back = lax.dot_general(mix[n % 2], grad_pooled[...], tn, preferred_element_type=F32)
        back += jnp.dot(chosen, sub_landed[...].reshape(halo, width), preferred_element_type=F32)
        grad = (back * slope[at, :].astype(F32)).astype(BF)
        joined[at, width:] = grad
        q_bias_acc[0:1, :] += jnp.sum(grad.astype(F32), axis=0, keepdims=True)

    def bias_step(b):
        if b:
            bias_copies[b - 1].wait()
            total = bias_sent[b - 1] + bias_got[b - 1]
            if b == bits:
                bias_out[...] = total
                return
            bias_sent[b] = total
        bias_copies[b].start()

    pieces = [w_bias_ref[0:1, c : c + 128] for c in range(0, width, 128)]
    pieces += [q_bias_acc[0:1, c : c + 128] for c in range(0, width, 128)]
    bias_sent[0] = jnp.concatenate(pieces, axis=0)

    for t in range(4):
        bias_step(t)
        n, j = t // 2, t % 2
        value = lax.dot_general(
            joined[:, j * half : (j + 1) * half],
            joined[:, width + n * half : width + (n + 1) * half],
            tn,
            preferred_element_type=F32,
        )
        deal(value, q_sets[n], (j,), q_out.shape[0])
        q_sets[n].first(2 * j).start()
        q_sets[n].first(2 * j + 1).start()
        for m, k in events.get(("q", t), []):
            all_sets[m].advance(k)
    bias_step(4)
    for n in (8, 9):
        loads[n].wait()

    @pl.loop(0, rounds)
    def _(n):
        happen("features", n)

        @pl.when(n >= 2)
        def _():
            out_copy(n - 2).wait()

        at = pl.ds(pl.multiple_of(n * row_block, row_block), row_block)
        value = lax.dot_general(grad_out[at, :], w_top[...], nt, preferred_element_type=F32)
        features[n % 2] = value + lax.dot_general(
            joined[at, width:], q_full[...], nt, preferred_element_type=F32
        )
        out_copy(n).start()

    for n, k in ((1, 2), (0, 3), (1, 3), (0, 4), (1, 4)):
        q_sets[n].advance(k)
    for n in range(2):
        w_out[:, n * half : (n + 1) * half] = w_sets[n].result()
        q_out[:, n * half : (n + 1) * half] = q_sets[n].result()
    bias_step(bits)
    for n in range(rounds - 2, rounds):
        out_copy(n).wait()


def settle_kernel(features_ref, q_ref, w_ref, biases_ref, features_out, q_out, w_out, q_bias_out, w_bias_out, *, subs):
    features_out[...] = features_ref[...]

    @pl.when(pl.program_id(0) == 0)
    def _():
        q_out[...] = q_ref[...]
        w_out[...] = w_ref[...]
        share = q_bias_out.shape[1]
        each = 128 // share
        me = lax.axis_index("comm") * subs + lax.axis_index("sub")
        for first, target in ((0, w_bias_out), (8, q_bias_out)):
            row = biases_ref[pl.ds(first + me // each, 1), :]
            piece = row[:, :share]
            for k in range(1, each):
                piece = jnp.where(me % each == k, row[:, k * share : (k + 1) * share], piece)
            target[...] = piece


def settle(grad_features, grad_q, grad_w, biases):
    rows, width = grad_features.shape
    block = rows // 2
    share = grad_q.shape[0]
    shapes = [grad_q.shape, grad_w.shape, (1, share), (1, share)]

    def whole(shape):
        return pl.BlockSpec(shape, lambda i: (0, 0))

    return pl.pallas_call(
        functools.partial(settle_kernel, subs=lax.axis_size("sub")),
        grid=(rows // block,),
        in_specs=[by_rows(block, width)] + [whole(x.shape) for x in (grad_q, grad_w, biases)],
        out_specs=[by_rows(block, width)] + [whole(shape) for shape in shapes],
        out_shape=[jax.ShapeDtypeStruct(shape, F32) for shape in [grad_features.shape] + shapes],
        compiler_params=pltpu.CompilerParams(vmem_limit_bytes=62 * 2**20),
        name="settle",
    )(grad_features, grad_q, grad_w, biases)


def back_kernel(
    own_mix, low, slope, pooled, grad_out, grad_pooled, sent_grad, grad_wbias, q_full, w_full, send_rows
):
    comms, subs = lax.axis_size("comm"), lax.axis_size("sub")
    devices = comms * subs
    bits = devices.bit_length() - 1
    rows, width = low.shape
    per = send_rows.shape[2]
    halo = devices * per
    mix_block, row_block = 384, 384
    w_rows, q_rows = w_full.shape[0] // devices, q_full.shape[0] // devices
    targets = send_targets(send_rows, comms, subs)
    lead = (2,) * (bits - 1)

    def set_scratch(rows_each, columns):
        chunks = (1 << (bits - 1)) - 1
        copies = 4 + 2 * (bits - 1)
        return [
            pltpu.VMEM(lead + (rows_each, columns), F32),
            pltpu.VMEM(lead + (rows_each, columns), BF),
            pltpu.VMEM(lead + (rows_each, columns), BF),
            pltpu.VMEM((2, chunks, rows_each, columns // 2), BF),
            pltpu.VMEM((2, chunks, rows_each, columns // 2), BF),
            pltpu.SemaphoreType.DMA((copies,)),
            pltpu.SemaphoreType.DMA((copies,)),
        ]

    here = pl.BlockSpec(memory_space=pltpu.VMEM)
    anywhere = pl.BlockSpec(memory_space=pl.ANY)
    grad_features, grad_q, grad_w, biases = pl.pallas_call(
        functools.partial(
            back_body, comms=comms, subs=subs, bits=bits, mix_block=mix_block, row_block=row_block
        ),
        in_specs=[here] * 3 + [anywhere] * 8,
        out_specs=[anywhere] + [here] * 3,
        out_shape=[
            jax.ShapeDtypeStruct((rows, width), F32),
            jax.ShapeDtypeStruct((q_rows, width), F32),
            jax.ShapeDtypeStruct((w_rows, width), F32),
            jax.ShapeDtypeStruct((16, 128), F32),
        ],
        scratch_shapes=[
            pltpu.VMEM((rows, 2 * width), BF),
            pltpu.VMEM((rows, width), BF),
            pltpu.VMEM((rows, width), BF),
            pltpu.VMEM((rows, width), BF),
            pltpu.VMEM((width, width), BF),
            pltpu.VMEM((width, width), BF),
            pltpu.VMEM((2, rows, mix_block), BF),
            pltpu.VMEM((2, row_block, width), F32),
            pltpu.VMEM((8, width), F32),
            pltpu.VMEM((bits, 16, 128), F32),
            pltpu.VMEM((bits, 16, 128), F32),
            pltpu.VMEM((comms, halo // comms, width), BF),
            pltpu.VMEM((comms, halo // comms, width), BF),
            pltpu.VMEM((subs, halo // subs, width), BF),
            pltpu.VMEM((subs, halo // subs, width), BF),
        ]
        + set_scratch(w_rows, width // 2)
        + set_scratch(w_rows, width // 2)
        + set_scratch(q_rows, width // 2)
        + set_scratch(q_rows, width // 2)
        + [
            pltpu.SemaphoreType.DMA((10,)),
            pltpu.SemaphoreType.DMA((2,)),
            pltpu.SemaphoreType.DMA((2,)),
            pltpu.SemaphoreType.DMA((bits,)),
            pltpu.SemaphoreType.DMA((bits,)),
            pltpu.SemaphoreType.DMA((comms - 1,)),
            pltpu.SemaphoreType.DMA((comms - 1,)),
            pltpu.SemaphoreType.DMA((subs - 1,)),
            pltpu.SemaphoreType.DMA((subs - 1,)),
        ],
        compiler_params=pltpu.CompilerParams(
            collective_id=1, has_side_effects=True, vmem_limit_bytes=62 * 2**20
        ),
        name="back",
    )(sent_grad, grad_wbias, targets, own_mix, slope, low, pooled, grad_out, grad_pooled, w_full, q_full)
    grad_features, grad_q, grad_w, q_bias, w_bias = settle(grad_features, grad_q, grad_w, biases)
    share = width // devices
    return grad_features, grad_q, q_bias.reshape(share), grad_w, w_bias.reshape(share)


def shards(
    features,
    q_weight,
    q_bias,
    w_weight,
    w_bias,
    nbr_index,
    nbr_count,
    importance,
    send_rows,
    cotangent,
):
    devices = lax.axis_size(AXES)
    kernel_fits = devices == 32 and q_weight.shape[0] % 16 == 0
    gather, back = (gather_and_transform, back_kernel) if kernel_fits else (gather_plain, back_plain)
    own_mix, halo_mix, low, slope, pooled, q_full, w_full, biases = gather(
        features, q_weight, q_bias, w_weight, w_bias, nbr_index, nbr_count, importance, send_rows
    )
    embedding, grad_out, grad_pooled, sent_grad, grad_wbias = combine(
        pooled, halo_mix, low, w_full, biases, cotangent
    )
    grad_features, grad_q, grad_qbias, grad_w, grad_wbias = back(
        own_mix, low, slope, pooled, grad_out, grad_pooled, sent_grad, grad_wbias, q_full, w_full, send_rows
    )
    return embedding, grad_features, grad_q, grad_qbias, grad_w, grad_wbias


def solution(mesh):
    in_specs = (
        P(("comm", "sub"), None),
        P(("comm", "sub"), None),
        P(("comm", "sub")),
        P(("comm", "sub"), None),
        P(("comm", "sub")),
        P(("comm", "sub"), None),
        P(("comm", "sub")),
        P(("comm", "sub"), None),
        P(("comm", "sub"), None, None),
        P(("comm", "sub"), None),
    )
    out_specs = (
        P(("comm", "sub"), None),
        P(("comm", "sub"), None),
        P(("comm", "sub"), None),
        P(("comm", "sub")),
        P(("comm", "sub"), None),
        P(("comm", "sub")),
    )
    return jax.shard_map(shards, mesh=mesh, in_specs=in_specs, out_specs=out_specs, check_vma=False)
```

```python
import functools
import math

import jax
import jax.numpy as jnp
from jax import lax
from jax.experimental import pallas as pl
from jax.experimental.pallas import tpu as pltpu
from jax.sharding import PartitionSpec as P

BF = jnp.bfloat16
F32 = jnp.float32
AXES = ("comm", "sub")


def build_rows(index_ref, counts, importance_ref, own_ref, halo_ref, first, *, rows, halo):
    his = (rows + halo + 255) // 256
    pairs = (his + 1) // 2
    fanout = index_ref.shape[0]
    at = pl.ds(pl.multiple_of(first, 128), 128)
    lane = lax.broadcasted_iota(jnp.int32, (16, 128), 1)
    sublane = lax.broadcasted_iota(jnp.int32, (16, 128), 0)
    parity = (sublane >= 8).astype(jnp.int32)
    half = (lane >= 64).astype(jnp.int32)
    los = lax.broadcasted_iota(jnp.int32, (64, 256), 1).astype(BF)
    left = lax.broadcasted_iota(jnp.int32, (1, 128), 1) < 64
    hi_pattern = [(2 * t + parity).astype(BF) for t in range(pairs)]
    row_mask = [(sublane & 7) == 2 * c + half for c in range(4)]
    zero = jnp.zeros((), BF)
    one = jnp.ones((), BF)

    def slots(x):
        return jnp.concatenate([x, jnp.zeros((64 - fanout, 128), F32)], axis=0)

    def by_row(x):
        x = slots(x).T
        return jnp.concatenate([x, x], axis=1)

    index = index_ref[:, at]
    slot = lax.broadcasted_iota(jnp.int32, index.shape, 0)
    weight = jnp.where(slot < counts, importance_ref[:, at], 0.0)
    alpha = by_row(weight / jnp.sum(weight, axis=0, keepdims=True))
    hi = by_row((index >> 8).astype(F32))
    lo = slots((index & 255).astype(F32)).astype(BF)
    for g in range(0, 128, 16):
        tiles = []
        for s in range(2):
            left_parts, right_parts = [], []
            for c in range(4):
                r = g + s * 8 + 2 * c

                def pick(x):
                    return jnp.where(left, x[r : r + 1, :], x[r + 1 : r + 2, :]).astype(BF)

                kept = jnp.where(row_mask[c], jnp.broadcast_to(pick(alpha), (16, 128)), zero)
                hi_row = jnp.broadcast_to(pick(hi), (16, 128))
                left_parts.append(
                    jnp.concatenate(
                        [jnp.where(hi_row == hi_pattern[t], kept, zero) for t in range(pairs)], axis=0
                    )
                )
                for q in (r, r + 1):
                    right_parts.append(jnp.where(jnp.broadcast_to(lo[:, q : q + 1], (64, 256)) == los, one, zero))
            tiles.append(
                jnp.dot(
                    jnp.concatenate(left_parts, axis=1),
                    jnp.concatenate(right_parts, axis=0),
                    preferred_element_type=F32,
                )
            )
        for h in range(his):
            tile = jnp.concatenate([t[h * 8 : (h + 1) * 8, :] for t in tiles], axis=0).astype(BF)
            to = pl.ds(pl.multiple_of(first + g, 16), 16)
            if h * 256 < rows:
                own_ref[to, h * 256 : (h + 1) * 256] = tile
            else:
                start = h * 256 - rows
                stop = min(start + 256, halo)
                halo_ref[to, start:stop] = tile[:, : stop - start]


def build_kernel(index_ref, count_ref, importance_ref, own_ref, halo_ref, *, rows, halo):
    for first in range(0, own_ref.shape[0], 128):
        counts = count_ref[:, first : first + 128]
        build_rows(index_ref, counts, importance_ref, own_ref, halo_ref, first, rows=rows, halo=halo)


def build_mixing(nbr_index, nbr_count, importance, halo):
    rows, fanout = nbr_index.shape
    block = 256
    return pl.pallas_call(
        functools.partial(build_kernel, rows=rows, halo=halo),
        grid=(rows // block,),
        in_specs=[
            pl.BlockSpec((fanout, block), lambda i: (0, i)),
            pl.BlockSpec((1, block), lambda i: (0, i)),
            pl.BlockSpec((fanout, block), lambda i: (0, i)),
        ],
        out_specs=[
            pl.BlockSpec((block, rows), lambda i: (i, 0)),
            pl.BlockSpec((block, halo), lambda i: (i, 0)),
        ],
        out_shape=[
            jax.ShapeDtypeStruct((rows, rows), BF),
            jax.ShapeDtypeStruct((rows, halo), BF),
        ],
        compiler_params=pltpu.CompilerParams(vmem_limit_bytes=40 * 2**20),
        name="build_mixing",
    )(nbr_index.T, nbr_count.reshape(1, rows), importance.T)


def gelu_pair(x):
    c = math.sqrt(2.0 / math.pi)
    square = x * x
    half = 0.5 + 0.5 * jnp.tanh(x * (c + (c * 0.044715) * square))
    value = x * half
    return value, half + value * (1.0 - half) * (2.0 * c + (6.0 * c * 0.044715) * square)


def hidden_rows(features_ref, q_buf, bias_ref, send_ref, low_ref, neigh_ref, slope_ref, sent_ref, at_rows, start):
    width = features_ref.shape[1]
    lead = (slice(None),) * (len(q_buf.shape) - 1)
    low_ref[at_rows, :] = features_ref[at_rows, :].astype(BF)
    for c in range(0, width, 256):
        at = slice(c, c + 256)
        q = q_buf[lead + (at,)].reshape(width, 256)
        pre = jnp.dot(low_ref[at_rows, :], q, preferred_element_type=F32) + bias_ref[0:1, at]
        value, slope = gelu_pair(pre)
        neigh_ref[at_rows, at] = value.astype(BF)
        slope_ref[at_rows, at] = slope.astype(BF)
    neigh = neigh_ref[at_rows, :]
    local = lax.broadcasted_iota(jnp.int32, (neigh.shape[0], send_ref.shape[1]), 0) + start
    chosen = jnp.where(local == send_ref[...], 1.0, 0.0).astype(BF)
    sent_ref[...] += lax.dot_general(chosen, neigh, (((0,), (0,)), ((), ())), preferred_element_type=F32)


def ring_copies(groups, index, blocks_ref, landed_ref, send_sem, recv_sem, device_of):
    copies = []
    for k in range(1, groups):
        other = (index + k) % groups
        copies.append(
            pltpu.make_async_remote_copy(
                src_ref=blocks_ref.at[other],
                dst_ref=landed_ref.at[index],
                send_sem=send_sem.at[k - 1],
                recv_sem=recv_sem.at[k - 1],
                device_id=device_of(other),
                device_id_type=pl.DeviceIdType.MESH,
            )
        )
    return copies


def regroup(x, outer, inner, per):
    count = x.shape[0]
    to = lax.broadcasted_iota(jnp.int32, (count, count), 0)
    place = lax.broadcasted_iota(jnp.int32, (count, count), 1)
    source = ((to // per) % outer) * (inner * per) + (to // (per * outer)) * per + to % per
    chosen = jnp.where(place == source, 1.0, 0.0).astype(BF)
    return jnp.dot(chosen, x, preferred_element_type=F32).astype(BF)


def greet(comm, sub, comms, subs):
    barrier = pltpu.get_barrier_semaphore()
    for k in range(1, comms):
        pl.semaphore_signal(
            barrier, inc=1, device_id=((comm + k) % comms, sub), device_id_type=pl.DeviceIdType.MESH
        )
    for k in range(1, subs):
        pl.semaphore_signal(
            barrier, inc=1, device_id=(comm, (sub + k) % subs), device_id_type=pl.DeviceIdType.MESH
        )
    pl.semaphore_wait(barrier, comms + subs - 2)


def send_targets(send_rows, comms, subs):
    per = send_rows.shape[2]
    return send_rows.reshape(comms, subs, per).transpose(1, 0, 2).reshape(1, comms * subs * per)


def gather_kernel(
    index_ref,
    count_ref,
    importance_ref,
    q_ref,
    w_ref,
    q_bias_ref,
    w_bias_ref,
    send_ref,
    features_hbm,
    own_out,
    halo_ref,
    low_out,
    slope_out,
    pooled_out,
    q_full,
    w_full,
    bias_out,
    features,
    own_mix,
    low,
    neigh,
    slope,
    pooled,
    pooled_low,
    q_buf,
    w_own,
    bias_buf,
    sent_acc,
    sub_blocks,
    sub_landed,
    comm_blocks,
    comm_landed,
    local_sem,
    feature_sem,
    send_sem,
    recv_sem,
    sub_send,
    sub_recv,
    comm_send,
    comm_recv,
    *,
    comms,
    subs,
    bits,
    block,
    pool_block,
):
    rows = own_mix.shape[0]
    halo = halo_ref.shape[1]
    width = neigh.shape[1]
    comm, sub = lax.axis_index("comm"), lax.axis_index("sub")
    me = comm * subs + sub
    mine = [(me // (1 << b)) % 2 for b in range(bits)]
    order = list(range(bits))[::-1]

    def partner(b):
        other = me + (1 << b) * (1 - 2 * mine[b])
        return (other // subs, other % subs)

    def spot(done, part=slice(None), columns=slice(None)):
        lead = tuple(slice(None) if b in done else mine[b] for b in order)
        return lead + (part, columns)

    high = list(range(3, bits))[::-1]
    left, right = pl.ds(0, width // 2), pl.ds(width // 2, width // 2)
    count = [0]

    def exchange(buf, b, done, part=slice(None), columns=slice(None), source=None):
        at = buf.at[spot(done, part, columns)]
        n = count[0]
        count[0] += 1
        return pltpu.make_async_remote_copy(
            src_ref=at if source is None else source,
            dst_ref=at,
            send_sem=send_sem.at[n],
            recv_sem=recv_sem.at[n],
            device_id=partner(b),
            device_id_type=pl.DeviceIdType.MESH,
        )

    def chain(buf, own, split, part=slice(None)):
        groups = []
        done = []
        for b in high:
            groups.append([exchange(buf, b, done, part, source=own if not done else None)])
            done = done + [b]
        if split:
            groups.append([exchange(buf, 1, done, part, left), exchange(buf, 2, done, part, right)])
            groups.append(
                [exchange(buf, 2, done + [1], part, left), exchange(buf, 1, done + [2], part, right)]
            )
        else:
            groups.append([exchange(buf, 1, done)])
            groups.append([exchange(buf, 2, done + [1])])
        groups.append([exchange(buf, 0, done + [1, 2], part)])
        return groups

    def chain_xy(buf, own, part):
        groups = [
            [
                exchange(buf, 1, [], part, left, own.at[part, left]),
                exchange(buf, 2, [], part, right, own.at[part, right]),
            ],
            [exchange(buf, 2, [1], part, left), exchange(buf, 1, [2], part, right)],
        ]
        done = [1, 2]
        for b in high:
            groups.append([exchange(buf, b, done, part)])
            done = done + [b]
        groups.append([exchange(buf, 0, done, part)])
        return groups

    w_rows = w_own.shape[0]
    top, bottom = pl.ds(0, w_rows // 2), pl.ds(w_rows // 2, w_rows // 2)
    chains = {
        "q": chain(q_buf, None, True),
        "bias": chain(bias_buf, None, False),
        "w0": chain(w_full, w_own.at[top], True, top),
        "w1": chain_xy(w_full, w_own, bottom),
        "sub": [ring_copies(subs, sub, sub_blocks, sub_landed, sub_send, sub_recv, lambda j: (comm, j))],
        "comm": [ring_copies(comms, comm, comm_blocks, comm_landed, comm_send, comm_recv, lambda j: (j, sub))],
    }
    w_local = pltpu.make_async_copy(w_own, w_full.at[spot([])], local_sem.at[0])
    q_local = pltpu.make_async_copy(q_buf, q_full, local_sem.at[1])
    last = len(chains["q"]) - 1

    def begin(name, n):
        for c in chains[name][n]:
            c.start()

    def finish(name, n):
        for c in chains[name][n]:
            c.wait()

    def place(n, size):
        return pl.ds(pl.multiple_of(n * size, size), size)

    def feature_copy(n):
        at = place(n, block)
        return pltpu.make_async_copy(features_hbm.at[at, :], features.at[at, :], feature_sem.at[n])

    outs = [(own_mix, own_out), (low, low_out), (slope, slope_out), (pooled_low, pooled_out)]

    def give(n, at):
        source, target = outs[n]
        pltpu.make_async_copy(source.at[at, :], target.at[at, :], local_sem.at[2 + n]).start()

    def given(n):
        pltpu.make_async_copy(*outs[n], local_sem.at[2 + n]).wait()

    events = {
        ("build", 1): [("w1", -1)],
        ("build", 4): [("q", 0), ("bias", 0), ("w1", 0)],
        ("build", 6): [("w0", -1)],
        ("build", 7): [("q", 1), ("bias", 1)],
        ("build", 9): [("w1", 1)],
        ("build", 10): [("q", 2), ("bias", 2), ("w0", 0)],
        ("build", 15): [("q", 3), ("bias", 3)],
        ("build", 16): [("w0", 1)],
        ("hidden", 1): [("w1", 2), ("w0", 2)],
        ("hidden", 6): [("w0", 3)],
        ("pool", 1): [("w1", 3)],
    }

    def happen(phase, n):
        for (when, step), names in events.items():
            if when == phase:

                @pl.when(n == step)
                def _(names=names):
                    for name, k in names:
                        if k >= 0:
                            finish(name, k)
                        begin(name, k + 1)

    q_buf[spot([])] = q_ref[...].astype(BF)
    w_own[...] = w_ref[...].astype(BF)
    share = q_bias_ref.shape[1]
    bias_own = jnp.concatenate(
        [q_bias_ref[...], w_bias_ref[...], jnp.zeros((1, 128 - 2 * share), F32)], axis=1
    )
    bias_buf[spot([])] = jnp.broadcast_to(bias_own, (8, 128))
    greet(comm, sub, comms, subs)
    begin("q", 0)
    begin("bias", 0)
    w_local.start()
    sent_acc[...] = jnp.zeros_like(sent_acc)
    w_local.wait()

    @pl.loop(0, rows // block)
    def _(n):
        feature_copy(n).start()

    @pl.loop(0, rows // 128)
    def _(n):
        happen("build", n)
        build_rows(
            index_ref,
            count_ref[pl.ds(pl.multiple_of(n * 128, 128), 128)].reshape(1, 128),
            importance_ref,
            own_mix,
            halo_ref,
            n * 128,
            rows=rows,
            halo=halo,
        )
        give(0, place(n, 128))

    finish("q", last)
    finish("bias", last)
    q_local.start()
    for k in range(2):
        pieces = []
        for e in range(1 << bits):
            piece = bias_buf[tuple((e >> b) & 1 for b in order)]
            pieces.append(piece[0:1, k * share : (k + 1) * share])
        bias_out[k : k + 1, :] = jnp.concatenate(pieces, axis=1).astype(BF).astype(F32)
    bias_out[2:, :] = jnp.zeros((6, width), F32)

    @pl.loop(0, rows // block)
    def _(n):
        happen("hidden", n)
        feature_copy(n).wait()
        at = place(n, block)
        hidden_rows(features, q_buf, bias_out, send_ref, low, neigh, slope, sent_acc, at, n * block)
        give(1, at)
        give(2, at)

    sub_blocks[...] = sent_acc[...].astype(BF).reshape(sub_blocks.shape)
    begin("sub", 0)
    sub_landed[sub] = sub_blocks[sub]

    @pl.loop(0, rows // pool_block)
    def _(n):
        happen("pool", n)

        @pl.when(n == 2)
        def _():
            finish("sub", 0)
            moved = regroup(sub_landed[...].reshape(halo, width), subs, comms, halo // (subs * comms))
            comm_blocks[...] = moved.reshape(comm_blocks.shape)
            begin("comm", 0)
            comm_landed[comm] = comm_blocks[comm]

        at = place(n, pool_block)
        pooled[at, :] = jnp.dot(own_mix[at, :], neigh[...], preferred_element_type=F32)

    finish("comm", 0)

    @pl.loop(0, rows // pool_block)
    def _(n):
        at = place(n, pool_block)
        received = comm_landed[...].reshape(halo, width)
        total = pooled[at, :] + jnp.dot(halo_ref[at, :], received, preferred_element_type=F32)
        pooled_low[at, :] = total.astype(BF)
        give(3, at)

    finish("w0", last)
    finish("w1", last)
    q_local.wait()
    for n in range(4):
        given(n)


def gather_and_transform(features, q_weight, q_bias, w_weight, w_bias, nbr_index, nbr_count, importance, send_rows):
    comms, subs = lax.axis_size("comm"), lax.axis_size("sub")
    devices = comms * subs
    bits = devices.bit_length() - 1
    rows, width = features.shape
    fanout = nbr_index.shape[1]
    per = send_rows.shape[2]
    halo = devices * per
    block, pool_block = 256, 384
    q_rows, w_rows = q_weight.shape[0], w_weight.shape[0]
    share = q_bias.shape[0]
    targets = send_targets(send_rows, comms, subs)
    lead = (2,) * bits

    here = pl.BlockSpec(memory_space=pltpu.VMEM)
    anywhere = pl.BlockSpec(memory_space=pl.ANY)
    copies = 4 * bits + 3 * 2
    out = pl.pallas_call(
        functools.partial(
            gather_kernel, comms=comms, subs=subs, bits=bits, block=block, pool_block=pool_block
        ),
        in_specs=[here] * 8 + [anywhere],
        out_specs=[anywhere, here, anywhere, anywhere, anywhere, anywhere, anywhere, here],
        out_shape=[
            jax.ShapeDtypeStruct((rows, rows), BF),
            jax.ShapeDtypeStruct((rows, halo), BF),
            jax.ShapeDtypeStruct((rows, width), BF),
            jax.ShapeDtypeStruct((rows, width), BF),
            jax.ShapeDtypeStruct((rows, width), BF),
            jax.ShapeDtypeStruct(lead + (q_rows, width), BF),
            jax.ShapeDtypeStruct(lead + (w_rows, width), BF),
            jax.ShapeDtypeStruct((8, width), F32),
        ],
        scratch_shapes=[
            pltpu.VMEM((rows, width), F32),
            pltpu.VMEM((rows, rows), BF),
            pltpu.VMEM((rows, width), BF),
            pltpu.VMEM((rows, width), BF),
            pltpu.VMEM((rows, width), BF),
            pltpu.VMEM((rows, width), F32),
            pltpu.VMEM((rows, width), BF),
            pltpu.VMEM(lead + (q_rows, width), BF),
            pltpu.VMEM((w_rows, width), BF),
            pltpu.VMEM(lead + (8, 128), F32),
            pltpu.VMEM((halo, width), F32),
            pltpu.VMEM((subs, halo // subs, width), BF),
            pltpu.VMEM((subs, halo // subs, width), BF),
            pltpu.VMEM((comms, halo // comms, width), BF),
            pltpu.VMEM((comms, halo // comms, width), BF),
            pltpu.SemaphoreType.DMA((6,)),
            pltpu.SemaphoreType.DMA((rows // block,)),
            pltpu.SemaphoreType.DMA((copies,)),
            pltpu.SemaphoreType.DMA((copies,)),
            pltpu.SemaphoreType.DMA((subs - 1,)),
            pltpu.SemaphoreType.DMA((subs - 1,)),
            pltpu.SemaphoreType.DMA((comms - 1,)),
            pltpu.SemaphoreType.DMA((comms - 1,)),
        ],
        compiler_params=pltpu.CompilerParams(
            collective_id=0, has_side_effects=True, vmem_limit_bytes=62 * 2**20
        ),
        name="gather_and_transform",
    )(
        nbr_index.T,
        nbr_count,
        importance.T,
        q_weight,
        w_weight,
        q_bias.reshape(1, share),
        w_bias.reshape(1, share),
        targets,
        features,
    )
    own_mix, halo_mix, low, slope, pooled, q_full, w_full, biases = out
    return (
        own_mix,
        halo_mix,
        low,
        slope,
        pooled,
        q_full.reshape(devices * q_rows, width),
        w_full.reshape(devices * w_rows, width),
        biases,
    )


def gather_plain(features, q_weight, q_bias, w_weight, w_bias, nbr_index, nbr_count, importance, send_rows):
    rows, width = features.shape
    devices, per_peer = send_rows.shape[1:]
    halo = devices * per_peer
    own_mix, halo_mix = build_mixing(nbr_index, nbr_count, importance, halo)
    q_full = lax.all_gather(q_weight.astype(BF), AXES, axis=0, tiled=True)
    w_full = lax.all_gather(w_weight.astype(BF), AXES, axis=0, tiled=True)
    biases = doubled(jnp.stack([q_bias, w_bias]), devices)
    qbias_full = biases[:, 0].reshape(width).astype(BF).astype(F32)
    wbias_full = biases[:, 1].reshape(width).astype(BF).astype(F32)
    low = features.astype(BF)
    neigh, slope = gelu_pair(jnp.dot(low, q_full, preferred_element_type=F32) + qbias_full)
    neigh = neigh.astype(BF)
    sent = neigh[send_rows[0]]
    incoming = lax.all_to_all(sent, AXES, split_axis=0, concat_axis=0, tiled=True).reshape(halo, width)
    pooled = pool_own(own_mix, neigh) + jnp.dot(halo_mix, incoming, preferred_element_type=F32)
    biases = jnp.pad(jnp.stack([qbias_full, wbias_full]), ((0, 6), (0, 0)))
    return own_mix, halo_mix, low, slope.astype(BF), pooled.astype(BF), q_full, w_full, biases


def resident(*shape):
    return pl.BlockSpec(shape, lambda i: (0,) * len(shape), pipeline_mode=pl.Buffered(1))


def by_rows(*shape):
    return pl.BlockSpec(shape, lambda i: (i,) + (0,) * (len(shape) - 1))


def product_kernel(mix_ref, table_ref, out_ref):
    out_ref[...] = jnp.dot(mix_ref[...], table_ref[...], preferred_element_type=F32)


def pool_own(own_mix, neigh):
    rows, width = neigh.shape
    block = 384
    return pl.pallas_call(
        product_kernel,
        grid=(rows // block,),
        in_specs=[by_rows(block, rows), resident(rows, width)],
        out_specs=by_rows(block, width),
        out_shape=jax.ShapeDtypeStruct((rows, width), F32),
        compiler_params=pltpu.CompilerParams(vmem_limit_bytes=40 * 2**20),
        cost_estimate=pl.CostEstimate(
            flops=2 * rows * rows * width, bytes_accessed=2 * rows * rows + 6 * rows * width, transcendentals=0
        ),
        name="pool_own",
    )(own_mix, neigh)


def combine_kernel(
    pooled_ref,
    halo_ref,
    low_ref,
    w_ref,
    bias_ref,
    cotangent_ref,
    embedding_ref,
    grad_ref,
    grad_pooled_ref,
    sent_ref,
    bias_grad_ref,
    act_buf,
    slope_buf,
):
    i = pl.program_id(0)
    block, width = low_ref.shape
    chunk = 256

    @pl.when(i == 0)
    def _():
        sent_ref[...] = jnp.zeros_like(sent_ref)
        bias_grad_ref[...] = jnp.zeros_like(bias_grad_ref)

    squares = jnp.zeros((block, 128), F32)
    dots = jnp.zeros((block, 128), F32)
    for c in range(0, width, chunk):
        at = slice(c, c + chunk)
        pre = jnp.dot(low_ref[...], w_ref[:width, at], preferred_element_type=F32)
        pre += jnp.dot(pooled_ref[...], w_ref[width:, at], preferred_element_type=F32)
        act, slope = gelu_pair(pre + bias_ref[1:2, at])
        act_buf[:, at] = act
        slope_buf[:, at] = slope
        square = act * act
        dot = act * cotangent_ref[:, at]
        for k in range(0, chunk, 128):
            squares += square[:, k : k + 128]
            dots += dot[:, k : k + 128]
    scale = lax.rsqrt(jnp.sum(squares, axis=1, keepdims=True) * (1.0 / width) + 1e-06)
    pull = jnp.sum(dots, axis=1, keepdims=True) * (1.0 / width) * scale * scale * scale
    for c in range(0, width, chunk):
        at = slice(c, c + chunk)
        act = act_buf[:, at]
        embedding_ref[:, at] = act * scale
        grad = slope_buf[:, at] * (cotangent_ref[:, at] * scale - act * pull)
        grad_ref[:, at] = grad.astype(BF)
        bias_grad_ref[0:1, at] += jnp.sum(grad_ref[:, at].astype(F32), axis=0, keepdims=True)
    for c in range(0, width, chunk):
        at = slice(c, c + chunk)
        back = lax.dot_general(
            grad_ref[...],
            w_ref[width + c : width + c + chunk, :],
            (((1,), (1,)), ((), ())),
            preferred_element_type=F32,
        )
        grad_pooled_ref[:, at] = back.astype(BF)
    sent_ref[...] += lax.dot_general(
        halo_ref[...], grad_pooled_ref[...], (((0,), (0,)), ((), ())), preferred_element_type=F32
    )


def combine(pooled, halo_mix, low, w_full, biases, cotangent):
    rows, width = low.shape
    halo = halo_mix.shape[1]
    block = 768
    return pl.pallas_call(
        combine_kernel,
        grid=(rows // block,),
        in_specs=[
            by_rows(block, width),
            by_rows(block, halo),
            by_rows(block, width),
            resident(2 * width, width),
            resident(8, width),
            by_rows(block, width),
        ],
        out_specs=[
            by_rows(block, width),
            by_rows(block, width),
            by_rows(block, width),
            pl.BlockSpec((halo, width), lambda i: (0, 0)),
            pl.BlockSpec((8, width), lambda i: (0, 0)),
        ],
        out_shape=[
            jax.ShapeDtypeStruct((rows, width), F32),
            jax.ShapeDtypeStruct((rows, width), BF),
            jax.ShapeDtypeStruct((rows, width), BF),
            jax.ShapeDtypeStruct((halo, width), F32),
            jax.ShapeDtypeStruct((8, width), F32),
        ],
        scratch_shapes=[pltpu.VMEM((block, width), F32), pltpu.VMEM((block, width), F32)],
        compiler_params=pltpu.CompilerParams(vmem_limit_bytes=62 * 2**20),
        cost_estimate=pl.CostEstimate(
            flops=6 * rows * width * width, bytes_accessed=22 * rows * width, transcendentals=rows * width
        ),
        name="combine",
    )(pooled, halo_mix, low, w_full, biases, cotangent)


def swap(x, bit, devices):
    return lax.ppermute(x, AXES, [(i, i ^ (1 << bit)) for i in range(devices)])


def doubled(x, devices):
    me = lax.axis_index(AXES)
    x = x[None]
    for bit in range(devices.bit_length() - 1):
        other = swap(x, bit, devices)
        first = ((me >> bit) & 1) == 0
        x = jnp.where(first, jnp.concatenate([x, other]), jnp.concatenate([other, x]))
    return x


def summed(x, devices):
    for bit in range(devices.bit_length() - 1):
        x = x + swap(x, bit, devices)
    return x


def halve(part, left, bit, devices):
    mine = (lax.axis_index(AXES) >> bit) & 1
    axis = left.index(bit)
    keep = lax.dynamic_index_in_dim(part, mine, axis, keepdims=False)
    sent = lax.dynamic_index_in_dim(part, 1 - mine, axis, keepdims=False)
    total = keep.astype(F32) + swap(sent, bit, devices).astype(F32)
    return total, [b for b in left if b != bit]


def scatter_sum(partial, devices):
    bits = list(range(devices.bit_length() - 1))[::-1]
    width = partial.shape[1]
    part = partial.reshape([2] * len(bits) + [-1, width])
    part, left = halve(part, bits, 0, devices)
    part = part.astype(BF)
    rows = part.shape[-2] // 2
    orders = ([1, 2] + list(range(3, len(bits))), [2, 1] + list(range(3, len(bits))))
    halves = [(part[..., :rows, :], left), (part[..., rows:, :], left)]
    for step in range(len(bits) - 1):
        for s in range(2):
            total, rest = halve(halves[s][0], halves[s][1], orders[s][step], devices)
            halves[s] = (total if len(rest) == 0 else total.astype(BF), rest)
    return jnp.concatenate([h[0] for h in halves], axis=0)


def back_plain(
    own_mix, low, slope, pooled, grad_out, grad_pooled, sent_grad, grad_wbias, q_full, w_full, send_rows
):
    rows, width = low.shape
    devices, per = send_rows.shape[1:]
    contract = (((0,), (0,)), ((), ()))
    returned = lax.all_to_all(
        sent_grad.reshape(devices, per, width), AXES, split_axis=0, concat_axis=0, tiled=True
    )
    joined = jnp.concatenate([low, pooled], axis=1)
    grad_w = lax.dot_general(joined, grad_out, contract, preferred_element_type=F32)
    grad_low = lax.dot_general(grad_out, w_full[:width], (((1,), (1,)), ((), ())), preferred_element_type=F32)
    grad_neigh = lax.dot_general(own_mix, grad_pooled, contract, preferred_element_type=F32)
    grad_neigh = grad_neigh.at[send_rows.reshape(-1)].add(returned.reshape(devices * per, width))
    grad_hidden = (slope.astype(F32) * grad_neigh).astype(BF)
    grad_q = lax.dot_general(low, grad_hidden, contract, preferred_element_type=F32)
    grad_qbias = jnp.sum(grad_hidden.astype(F32), axis=0)
    grad_features = grad_low + lax.dot_general(
        grad_hidden, q_full, (((1,), (1,)), ((), ())), preferred_element_type=F32
    )
    me = lax.axis_index(AXES)
    share = width // devices
    sums = summed(jnp.stack([grad_qbias, grad_wbias[0]]), devices)
    sums = lax.dynamic_slice_in_dim(sums, me * share, share, 1)
    return (
        grad_features,
        scatter_sum(grad_q.astype(BF), devices),
        sums[0],
        scatter_sum(grad_w.astype(BF), devices),
        sums[1],
    )


class ScatterSum:
    def __init__(self, refs, orders, mine, partner):
        self.held, self.sent, self.got, self.next_sent, self.next_got, self.send_sem, self.recv_sem = refs
        self.orders, self.mine, self.partner = orders, mine, partner
        self.bits = len(mine)
        self.lead = list(range(1, self.bits))[::-1]
        self.half = self.held.shape[-1] // 2

    def copy(self, n, source, target, b):
        return pltpu.make_async_remote_copy(
            src_ref=source,
            dst_ref=target,
            send_sem=self.send_sem.at[n],
            recv_sem=self.recv_sem.at[n],
            device_id=self.partner(b),
            device_id_type=pl.DeviceIdType.MESH,
        )

    def first(self, top):
        return self.copy(top, self.sent.at[self.top_index(top)], self.got.at[self.top_index(top)], 0)

    def top_index(self, top):
        return ((top // 2) % 2, top % 2)

    def later(self, k, h):
        n = 4 + 2 * (k - 1) + h
        at = (h, slice(self.offset(k), self.offset(k) + (1 << (self.bits - 1 - k))))
        return self.copy(n, self.next_sent.at[at], self.next_got.at[at], self.orders[h][k - 1])

    def offset(self, k):
        return (1 << (self.bits - 1)) - (1 << (self.bits - k))

    def spot(self, chosen):
        return tuple(chosen[b] for b in self.lead)

    def absorb(self, k, halves):
        for h in halves:
            order = self.orders[h]
            fixed = order[:k]
            free = [b for b in self.lead if b not in fixed]
            columns = slice(h * self.half, (h + 1) * self.half)

            def total(chosen, h=h, free=free, columns=columns):
                at = self.spot(chosen)
                if k == 0:
                    came = self.got[at + (slice(None), columns)]
                else:
                    place = self.offset(k)
                    for p, b in enumerate(free[::-1]):
                        place = place + chosen[b] * (1 << p)
                    came = self.next_got[h, place]
                return at, self.held[at + (slice(None), columns)] + came.astype(F32)

            if not free:
                at, value = total({b: self.mine[b] for b in fixed})
                self.held[at + (slice(None), columns)] = value
                continue
            split = order[k]
            others = [b for b in free if b != split]

            def body(n, carry, total=total, split=split, others=others, fixed=fixed, columns=columns, h=h):
                chosen = {b: self.mine[b] for b in fixed}
                for p, b in enumerate(others[::-1]):
                    chosen[b] = (n // (1 << p)) % 2
                chosen[split] = self.mine[split]
                at, value = total(chosen)
                self.held[at + (slice(None), columns)] = value
                chosen[split] = 1 - self.mine[split]
                _, value = total(chosen)
                self.next_sent[h, self.offset(k + 1) + n] = value.astype(BF)
                return carry

            lax.fori_loop(0, 1 << len(others), body, 0)

    def advance(self, k):
        if k == 0:
            for t in range(4):
                self.first(t).wait()
        for h in range(2):
            if k > 0:
                self.later(k, h).wait()
            self.absorb(k, [h])
            if k < self.bits - 1:
                self.later(k + 1, h).start()

    def result(self):
        return self.held[self.spot({b: self.mine[b] for b in self.lead})]


def back_body(
    sent_grad_ref,
    w_bias_ref,
    target_ref,
    mix_hbm,
    slope_hbm,
    low_hbm,
    pooled_hbm,
    out_hbm,
    grad_pooled_hbm,
    w_hbm,
    q_hbm,
    features_out,
    q_out,
    w_out,
    bias_out,
    joined,
    grad_out,
    grad_pooled,
    slope,
    mix,
    features,
    q_bias_acc,
    bias_sent,
    bias_got,
    comm_blocks,
    comm_landed,
    sub_blocks,
    sub_landed,
    *rest,
    comms,
    subs,
    bits,
    mix_block,
    row_block,
):
    sets = [rest[7 * k : 7 * k + 7] for k in range(4)]
    load_sem, mix_sem, out_sem, bias_send, bias_recv, comm_send, comm_recv, sub_send, sub_recv = rest[28:]
    rows, width = grad_out.shape
    halo = sent_grad_ref.shape[0]
    half = width // 2
    comm, sub = lax.axis_index("comm"), lax.axis_index("sub")
    me = comm * subs + sub
    mine = [(me // (1 << b)) % 2 for b in range(bits)]
    tn = (((0,), (0,)), ((), ()))
    nt = (((1,), (1,)), ((), ()))

    def partner(b):
        other = me + (1 << b) * (1 - 2 * mine[b])
        return (other // subs, other % subs)

    high = list(range(3, bits))
    orders = ([1, 2] + high, [2, 1] + high)
    w_sets = [ScatterSum(sets[k], orders, mine, partner) for k in range(2)]
    q_sets = [ScatterSum(sets[2 + k], orders, mine, partner) for k in range(2)]

    w_top = grad_pooled.at[pl.ds(0, width), :]
    q_full = grad_pooled.at[pl.ds(width, width), :]
    left, right = pl.ds(0, half), pl.ds(half, half)
    loads = [
        (out_hbm.at[:, left], grad_out.at[:, left]),
        (low_hbm.at[:, left], joined.at[:, pl.ds(0, half)]),
        (low_hbm.at[:, right], joined.at[:, pl.ds(half, half)]),
        (pooled_hbm.at[:, left], joined.at[:, pl.ds(2 * half, half)]),
        (pooled_hbm.at[:, right], joined.at[:, pl.ds(3 * half, half)]),
        (out_hbm.at[:, right], grad_out.at[:, right]),
        (grad_pooled_hbm, grad_pooled),
        (slope_hbm, slope),
        (w_hbm.at[pl.ds(0, width), :], w_top),
        (q_hbm, q_full),
    ]
    loads = [pltpu.make_async_copy(a, b, load_sem.at[n]) for n, (a, b) in enumerate(loads)]
    comm_ring = ring_copies(comms, comm, comm_blocks, comm_landed, comm_send, comm_recv, lambda j: (j, sub))
    sub_ring = ring_copies(subs, sub, sub_blocks, sub_landed, sub_send, sub_recv, lambda j: (comm, j))
    bias_copies = [
        pltpu.make_async_remote_copy(
            src_ref=bias_sent.at[b],
            dst_ref=bias_got.at[b],
            send_sem=bias_send.at[b],
            recv_sem=bias_recv.at[b],
            device_id=partner(b),
            device_id_type=pl.DeviceIdType.MESH,
        )
        for b in range(bits)
    ]

    spreads = rows // mix_block
    rounds = rows // row_block

    def mix_copy(n):
        at = pl.ds(pl.multiple_of(n * mix_block, mix_block), mix_block)
        return pltpu.make_async_copy(mix_hbm.at[:, at], mix.at[n % 2], mix_sem.at[n % 2])

    def out_copy(n):
        at = pl.ds(pl.multiple_of(n * row_block, row_block), row_block)
        return pltpu.make_async_copy(features.at[n % 2], features_out.at[at, :], out_sem.at[n % 2])

    def deal(value, which, top, rows_each):
        keep_even = mine[0] == 0
        shares = value.shape[0] // rows_each
        for p in range(shares // 2):
            even = value[2 * p * rows_each : (2 * p + 1) * rows_each]
            odd = value[(2 * p + 1) * rows_each : (2 * p + 2) * rows_each]
            at = top + tuple((p >> b) & 1 for b in range(bits - 2, -1, -1))[len(top) :]
            which.held[at] = jnp.where(keep_even, even, odd)
            which.sent[at] = jnp.where(keep_even, odd, even).astype(BF)

    def w_top_bits(j):
        return ((j // 2) % 2, j % 2)

    events = {
        ("w1", 1): [(0, 0)],
        ("spread", 1): [(0, 1), (1, 0)],
        ("spread", 3): [(0, 2)],
        ("spread", 5): [(1, 1), (0, 3)],
        ("q", 1): [(0, 4)],
        ("q", 2): [(2, 0), (1, 2)],
        ("features", 0): [(3, 0)],
        ("features", 2): [(1, 3), (2, 1)],
        ("features", 4): [(3, 1), (2, 2)],
        ("features", 5): [(1, 4)],
    }
    all_sets = w_sets + q_sets

    def happen(phase, n):
        for (when, step), which in events.items():
            if when == phase:

                @pl.when(n == step)
                def _(which=which):
                    for m, k in which:
                        all_sets[m].advance(k)

    def due(phase, n):
        for m, k in events.get((phase, n), []):
            all_sets[m].advance(k)

    for n in range(3):
        loads[n].start()
    comm_blocks[...] = sent_grad_ref[...].astype(BF).reshape(comm_blocks.shape)
    q_bias_acc[...] = jnp.zeros_like(q_bias_acc)
    greet(comm, sub, comms, subs)
    for c in comm_ring:
        c.start()
    comm_landed[comm] = comm_blocks[comm]

    needs = {0: [0, 1], 1: [2], 2: [3], 3: [4], 4: [5], 8: [6, 7]}
    starts = {0: [3], 1: [4], 2: [5], 3: [6], 4: [7]}

    def w_deal(t, value):
        n, j = t // 4, t % 4
        deal(value, w_sets[n], (j // 2, j % 2), w_out.shape[0])
        w_sets[n].first(j).start()
        due("w" + str(n), j)

    value = None
    for t in range(8):
        n, j = t // 4, t % 4
        for m in needs.get(t, []):
            loads[m].wait()
        for m in starts.get(t, []):
            loads[m].start()
        if t == 7:
            mix_copy(0).start()
        before = value
        value = lax.dot_general(
            joined[:, j * half : (j + 1) * half],
            grad_out[:, n * half : (n + 1) * half],
            tn,
            preferred_element_type=F32,
        )
        if before is not None:
            w_deal(t - 1, before)
        if t == 4:
            for c in comm_ring:
                c.wait()
            moved = regroup(comm_landed[...].reshape(halo, width), comms, subs, halo // (subs * comms))
            sub_blocks[...] = moved.reshape(sub_blocks.shape)
            for c in sub_ring:
                c.start()
            sub_landed[sub] = sub_blocks[sub]

    for c in sub_ring:
        c.wait()
    for m in needs[8]:
        loads[m].wait()

    def hidden_grad(n, back):
        start = n * mix_block
        at = slice(start, start + mix_block)
        local = lax.broadcasted_iota(jnp.int32, (mix_block, halo), 0) + start
        chosen = jnp.where(local == target_ref[...], 1.0, 0.0).astype(BF)
        back += jnp.dot(chosen, sub_landed[...].reshape(halo, width), preferred_element_type=F32)
        grad = (back * slope[at, :].astype(F32)).astype(BF)
        joined[at, width:] = grad
        q_bias_acc[0:1, :] += jnp.sum(grad.astype(F32), axis=0, keepdims=True)

    for n in range(spreads):
        if n + 1 < spreads:
            mix_copy(n + 1).start()
        mix_copy(n).wait()
        back = lax.dot_general(mix[n % 2], grad_pooled[...], tn, preferred_element_type=F32)
        if n == 0:
            w_deal(7, value)
        hidden_grad(n, back)
        due("spread", n)
    for m in (8, 9):
        loads[m].start()

    def bias_step(b):
        if b:
            bias_copies[b - 1].wait()
            total = bias_sent[b - 1] + bias_got[b - 1]
            if b == bits:
                bias_out[...] = total
                return
            bias_sent[b] = total
        bias_copies[b].start()

    pieces = [w_bias_ref[0:1, c : c + 128] for c in range(0, width, 128)]
    pieces += [q_bias_acc[0:1, c : c + 128] for c in range(0, width, 128)]
    bias_sent[0] = jnp.concatenate(pieces, axis=0)

    for t in range(4):
        bias_step(t)
        n, j = t // 2, t % 2
        value = lax.dot_general(
            joined[:, j * half : (j + 1) * half],
            joined[:, width + n * half : width + (n + 1) * half],
            tn,
            preferred_element_type=F32,
        )
        deal(value, q_sets[n], (j,), q_out.shape[0])
        q_sets[n].first(2 * j).start()
        q_sets[n].first(2 * j + 1).start()
        for m, k in events.get(("q", t), []):
            all_sets[m].advance(k)
    bias_step(4)
    for n in (8, 9):
        loads[n].wait()

    @pl.loop(0, rounds)
    def _(n):
        happen("features", n)

        @pl.when(n >= 2)
        def _():
            out_copy(n - 2).wait()

        at = pl.ds(pl.multiple_of(n * row_block, row_block), row_block)
        value = lax.dot_general(grad_out[at, :], w_top[...], nt, preferred_element_type=F32)
        features[n % 2] = value + lax.dot_general(
            joined[at, width:], q_full[...], nt, preferred_element_type=F32
        )
        out_copy(n).start()

    for n, k in ((1, 2), (0, 3), (1, 3), (0, 4), (1, 4)):
        q_sets[n].advance(k)
    for n in range(2):
        w_out[:, n * half : (n + 1) * half] = w_sets[n].result()
        q_out[:, n * half : (n + 1) * half] = q_sets[n].result()
    bias_step(bits)
    for n in range(rounds - 2, rounds):
        out_copy(n).wait()


def settle_kernel(features_ref, q_ref, w_ref, biases_ref, features_out, q_out, w_out, q_bias_out, w_bias_out, *, subs):
    features_out[...] = features_ref[...]

    @pl.when(pl.program_id(0) == 0)
    def _():
        q_out[...] = q_ref[...]
        w_out[...] = w_ref[...]
        share = q_bias_out.shape[1]
        each = 128 // share
        me = lax.axis_index("comm") * subs + lax.axis_index("sub")
        for first, target in ((0, w_bias_out), (8, q_bias_out)):
            row = biases_ref[pl.ds(first + me // each, 1), :]
            piece = row[:, :share]
            for k in range(1, each):
                piece = jnp.where(me % each == k, row[:, k * share : (k + 1) * share], piece)
            target[...] = piece


def settle(grad_features, grad_q, grad_w, biases):
    rows, width = grad_features.shape
    block = rows // 2
    share = grad_q.shape[0]
    shapes = [grad_q.shape, grad_w.shape, (1, share), (1, share)]

    def whole(shape):
        return pl.BlockSpec(shape, lambda i: (0, 0))

    return pl.pallas_call(
        functools.partial(settle_kernel, subs=lax.axis_size("sub")),
        grid=(rows // block,),
        in_specs=[by_rows(block, width)] + [whole(x.shape) for x in (grad_q, grad_w, biases)],
        out_specs=[by_rows(block, width)] + [whole(shape) for shape in shapes],
        out_shape=[jax.ShapeDtypeStruct(shape, F32) for shape in [grad_features.shape] + shapes],
        compiler_params=pltpu.CompilerParams(vmem_limit_bytes=62 * 2**20),
        name="settle",
    )(grad_features, grad_q, grad_w, biases)


def back_kernel(
    own_mix, low, slope, pooled, grad_out, grad_pooled, sent_grad, grad_wbias, q_full, w_full, send_rows
):
    comms, subs = lax.axis_size("comm"), lax.axis_size("sub")
    devices = comms * subs
    bits = devices.bit_length() - 1
    rows, width = low.shape
    per = send_rows.shape[2]
    halo = devices * per
    mix_block, row_block = 384, 384
    w_rows, q_rows = w_full.shape[0] // devices, q_full.shape[0] // devices
    targets = send_targets(send_rows, comms, subs)
    lead = (2,) * (bits - 1)

    def set_scratch(rows_each, columns):
        chunks = (1 << (bits - 1)) - 1
        copies = 4 + 2 * (bits - 1)
        return [
            pltpu.VMEM(lead + (rows_each, columns), F32),
            pltpu.VMEM(lead + (rows_each, columns), BF),
            pltpu.VMEM(lead + (rows_each, columns), BF),
            pltpu.VMEM((2, chunks, rows_each, columns // 2), BF),
            pltpu.VMEM((2, chunks, rows_each, columns // 2), BF),
            pltpu.SemaphoreType.DMA((copies,)),
            pltpu.SemaphoreType.DMA((copies,)),
        ]

    here = pl.BlockSpec(memory_space=pltpu.VMEM)
    anywhere = pl.BlockSpec(memory_space=pl.ANY)
    grad_features, grad_q, grad_w, biases = pl.pallas_call(
        functools.partial(
            back_body, comms=comms, subs=subs, bits=bits, mix_block=mix_block, row_block=row_block
        ),
        in_specs=[here] * 3 + [anywhere] * 8,
        out_specs=[anywhere] + [here] * 3,
        out_shape=[
            jax.ShapeDtypeStruct((rows, width), F32),
            jax.ShapeDtypeStruct((q_rows, width), F32),
            jax.ShapeDtypeStruct((w_rows, width), F32),
            jax.ShapeDtypeStruct((16, 128), F32),
        ],
        scratch_shapes=[
            pltpu.VMEM((rows, 2 * width), BF),
            pltpu.VMEM((rows, width), BF),
            pltpu.VMEM((rows, width), BF),
            pltpu.VMEM((rows, width), BF),
            pltpu.VMEM((2, rows, mix_block), BF),
            pltpu.VMEM((2, row_block, width), F32),
            pltpu.VMEM((8, width), F32),
            pltpu.VMEM((bits, 16, 128), F32),
            pltpu.VMEM((bits, 16, 128), F32),
            pltpu.VMEM((comms, halo // comms, width), BF),
            pltpu.VMEM((comms, halo // comms, width), BF),
            pltpu.VMEM((subs, halo // subs, width), BF),
            pltpu.VMEM((subs, halo // subs, width), BF),
        ]
        + set_scratch(w_rows, width // 2)
        + set_scratch(w_rows, width // 2)
        + set_scratch(q_rows, width // 2)
        + set_scratch(q_rows, width // 2)
        + [
            pltpu.SemaphoreType.DMA((10,)),
            pltpu.SemaphoreType.DMA((2,)),
            pltpu.SemaphoreType.DMA((2,)),
            pltpu.SemaphoreType.DMA((bits,)),
            pltpu.SemaphoreType.DMA((bits,)),
            pltpu.SemaphoreType.DMA((comms - 1,)),
            pltpu.SemaphoreType.DMA((comms - 1,)),
            pltpu.SemaphoreType.DMA((subs - 1,)),
            pltpu.SemaphoreType.DMA((subs - 1,)),
        ],
        compiler_params=pltpu.CompilerParams(
            collective_id=1, has_side_effects=True, vmem_limit_bytes=65000000
        ),
        name="back",
    )(sent_grad, grad_wbias, targets, own_mix, slope, low, pooled, grad_out, grad_pooled, w_full, q_full)
    grad_features, grad_q, grad_w, q_bias, w_bias = settle(grad_features, grad_q, grad_w, biases)
    share = width // devices
    return grad_features, grad_q, q_bias.reshape(share), grad_w, w_bias.reshape(share)


def shards(
    features,
    q_weight,
    q_bias,
    w_weight,
    w_bias,
    nbr_index,
    nbr_count,
    importance,
    send_rows,
    cotangent,
):
    devices = lax.axis_size(AXES)
    kernel_fits = devices == 32 and q_weight.shape[0] % 16 == 0
    gather, back = (gather_and_transform, back_kernel) if kernel_fits else (gather_plain, back_plain)
    own_mix, halo_mix, low, slope, pooled, q_full, w_full, biases = gather(
        features, q_weight, q_bias, w_weight, w_bias, nbr_index, nbr_count, importance, send_rows
    )
    embedding, grad_out, grad_pooled, sent_grad, grad_wbias = combine(
        pooled, halo_mix, low, w_full, biases, cotangent
    )
    grad_features, grad_q, grad_qbias, grad_w, grad_wbias = back(
        own_mix, low, slope, pooled, grad_out, grad_pooled, sent_grad, grad_wbias, q_full, w_full, send_rows
    )
    return embedding, grad_features, grad_q, grad_qbias, grad_w, grad_wbias


def solution(mesh):
    in_specs = (
        P(("comm", "sub"), None),
        P(("comm", "sub"), None),
        P(("comm", "sub")),
        P(("comm", "sub"), None),
        P(("comm", "sub")),
        P(("comm", "sub"), None),
        P(("comm", "sub")),
        P(("comm", "sub"), None),
        P(("comm", "sub"), None, None),
        P(("comm", "sub"), None),
    )
    out_specs = (
        P(("comm", "sub"), None),
        P(("comm", "sub"), None),
        P(("comm", "sub"), None),
        P(("comm", "sub")),
        P(("comm", "sub"), None),
        P(("comm", "sub")),
    )
    return jax.shard_map(shards, mesh=mesh, in_specs=in_specs, out_specs=out_specs, check_vma=False)
```
